512 devices in a mesh: replica: 32 (over y, x), tensor: 16 (over z, core).
Axes of the slice: x: 4, y: 8, z: 8, core: 2. Of those that a mesh axis runs over, the one named last changes fastest.
Arguments:
- inputs: bfloat16 [8192, 8192], P('replica', 'tensor'), may hold values from -6 to 6
- row_adapter_slot: int32 [8192], P('replica'), may hold values from 0 to 62
- transfer_plan: int32 [32, 31], replicated, may hold values from 0 to 1023, as said below
- key_value_weight: bfloat16 [8192, 2048], P('tensor'), may hold values from -0.0625 to 0.0625
- adapter_down: bfloat16 [1024, 64, 8192], P('replica', None, 'tensor'), may hold values from -0.0625 to 0.0625
- adapter_up: bfloat16 [1024, 64, 2048], P('replica', None, 'tensor'), may hold values from -0.75 to 0.75
Outputs:
- kv_out: bfloat16 [8192, 2048], P('replica', 'tensor')
The draws below stay inside these ranges and needn't reach their ends.
Inputs may be any that keep to these rules, and one draw needn't show every extreme that they name: `transfer_plan`: row g holds 31 distinct adapters, none of whose home group (id // 32) is g, ordered by home group; at most 2 of them share a home, and in every draw each group has some home that supplies 2.
All inputs are finite; a program needn't handle non-finite values.
Results may differ from the reference program's by a relative error of at most 0.0025.
Values may be sent and summed in bfloat16 or wider, within the bound.
No kernel may reach another device: no remote copies, remote signals or barrier semaphores. Data moves between devices by JAX's collectives and lax.ppermute only.
A program may use at most 64 MiB of HBM per device.

```python
import math
import jax
import jax.numpy as jnp
import numpy as np
from jax import lax

MODEL_WIDTH = 8192
KEY_VALUE_WIDTH = 2048
ADAPTER_RANK = 64
ROWS = 256
ADP_DEV = 32
IMPORT_LIMIT = 2
SLOTS = 31
LOCAL = 63
ADAPTER_COUNT = 1024
TOTAL_ROWS = 8192
N_REPLICA = 32


def draw_transfer_plan(key, part):
    key = jax.random.fold_in(key, 7)
    subkeys = jax.random.split(key, 5)
    group_count = N_REPLICA
    heat_rank = jax.random.permutation(subkeys[0], group_count).astype(jnp.int32)
    jitter_term = jax.random.randint(subkeys[1], (group_count, group_count), 0, max(group_count // 2, 1), dtype=jnp.int32)
    home_ids = jnp.arange(group_count, dtype=jnp.int32)
    scores = (heat_rank[None, :] + jitter_term) * group_count + home_ids[None, :]
    scores = jnp.where(home_ids[None, :] == home_ids[:, None], -1, scores)
    rank_order = jnp.sum((scores[:, None, :] < scores[:, :, None]).astype(jnp.int32), axis=2)
    few_homes = (group_count - 1) // 4
    counts = jnp.where(rank_order <= few_homes, 0, jnp.where(rank_order >= group_count - few_homes, IMPORT_LIMIT, 1)).astype(jnp.int32)
    upto_sum = jnp.cumsum(counts, axis=1)
    before = upto_sum - counts
    slot_index = jnp.arange(SLOTS, dtype=jnp.int32)
    home_group = jnp.sum((upto_sum[:, None, :] <= slot_index[None, :, None]).astype(jnp.int32), axis=2)
    start_slot = jnp.take_along_axis(before, home_group, axis=1)
    second_rank = slot_index[None, :] - start_slot
    home_perms = jax.vmap(lambda subkey: jax.random.permutation(subkey, ADP_DEV))(jax.random.split(subkeys[2], group_count)).astype(jnp.int32)
    first_pick = jax.random.randint(subkeys[3], (group_count, group_count), 0, ADP_DEV, dtype=jnp.int32)
    other_pick = (first_pick + 1 + jax.random.randint(subkeys[4], (group_count, group_count), 0, ADP_DEV - 1, dtype=jnp.int32)) % ADP_DEV
    picked = jnp.where(second_rank == 0, jnp.take_along_axis(first_pick, home_group, axis=1), jnp.take_along_axis(other_pick, home_group, axis=1))
    local_index = home_perms[home_group, picked]
    return (home_group * ADP_DEV + local_index).astype(jnp.int32)


def place_ends(array, stream_key, smallest, top_value):
    place = [jax.random.randint(jax.random.fold_in(stream_key, axis), (), 0, length) for axis, length in enumerate(array.shape)]
    widest = array.shape.index(max(array.shape))
    neighbour = place[:widest] + [(place[widest] + 1) % array.shape[widest]] + place[widest + 1:]
    return array.at[tuple(place)].set(smallest).at[tuple(neighbour)].set(top_value)


def steps_of(stream_key, dims, pieces, low, largest):
    gain, own = 1.0, jax.random.fold_in(stream_key, 6)
    for dim, parts in pieces:
        steps = jnp.exp(jax.random.uniform(jax.random.fold_in(own, dim), (parts,), jnp.float32, low / len(pieces), largest / len(pieces)))
        gain = gain * jnp.repeat(steps, dims[dim] // parts).reshape([-1 if axis == dim else 1 for axis in range(len(dims))])
    return gain


def rank_table(count, slope):
    loads = [(1 << 20) // math.isqrt(standing ** slope) + 1 for standing in range(1, count + 1)]
    deviation = 1 + sum(loads) // (1 << 30)
    return np.cumsum(np.array([max(1, weight // deviation) for weight in loads]))


def ranked_ids(rng, extent, number_of, skew):
    table = rank_table(number_of, skew)
    ticket = jax.random.randint(jax.random.fold_in(rng, 1), extent, 0, int(table[number_of - 1]))
    rank = jnp.searchsorted(jnp.asarray(table, jnp.int32), ticket, side="right")
    return jax.random.permutation(jax.random.fold_in(rng, 2), number_of)[rank].astype(jnp.int32)


def scatter_about(own_key, dims, spread, most, cuts=(), kind=jnp.bfloat16):
    entries = jax.random.normal(own_key, dims, jnp.float32) * spread
    if len(cuts) > 0:
        entries = steps_of(own_key, dims, cuts, -0.22, 0.18) * entries
    return jnp.clip(entries, min=-most, max=most).astype(kind)


def setup_inputs(seed: int = 0) -> dict:
    streams_of = jax.random.split(jax.random.key(seed), 7)
    return {
        "inputs": scatter_about(streams_of[0], (TOTAL_ROWS, MODEL_WIDTH), 1.0, 6.0, ((0, 32), (1, 16))),
        "row_adapter_slot": place_ends(ranked_ids(streams_of[1], (TOTAL_ROWS,), LOCAL, 2), jax.random.fold_in(streams_of[1], 3), 0, LOCAL - 1).astype(jnp.int32),
        "transfer_plan": draw_transfer_plan(jax.random.fold_in(streams_of[6], 71), 0),
        "key_value_weight": scatter_about(streams_of[3], (MODEL_WIDTH, KEY_VALUE_WIDTH), MODEL_WIDTH ** -0.5, 0.0625, ((0, 16),)),
        "adapter_down": scatter_about(streams_of[4], (ADAPTER_COUNT, ADAPTER_RANK, MODEL_WIDTH), MODEL_WIDTH ** -0.5, 0.0625, ((0, 32), (2, 16))),
        "adapter_up": scatter_about(streams_of[5], (ADAPTER_COUNT, ADAPTER_RANK, KEY_VALUE_WIDTH), ADAPTER_RANK ** -0.5, 0.75, ((0, 32), (2, 16))),
    }


adapter_scale = 1.0


def reference(inputs, row_adapter_slot, transfer_plan, key_value_weight, adapter_down, adapter_up):
    base_output = jnp.dot(inputs, key_value_weight, preferred_element_type=jnp.float32)
    group_of = jnp.arange(TOTAL_ROWS, dtype=jnp.int32) // ROWS
    import_index = jnp.clip(row_adapter_slot - ADP_DEV, 0, SLOTS - 1).astype(jnp.int32)
    imported = transfer_plan[group_of, import_index]
    adapter = jnp.where(row_adapter_slot < ADP_DEV, group_of * ADP_DEV + row_adapter_slot, imported).astype(jnp.int32)

    def per_group(block):
        block_rows, block_numbers = block
        down_matrices = adapter_down[block_numbers].astype(jnp.float32)
        shrink = jnp.einsum("rd,rkd->rk", block_rows.astype(jnp.float32), down_matrices, precision=lax.Precision.HIGHEST)
        up_matrices = adapter_up[block_numbers].astype(jnp.float32)
        return jnp.einsum("rk,rkc->rc", shrink, up_matrices, precision=lax.Precision.HIGHEST)

    widen_rows = lax.map(per_group, (inputs.reshape(N_REPLICA, ROWS, MODEL_WIDTH), adapter.reshape(N_REPLICA, ROWS)))
    widen_rows = widen_rows.reshape(TOTAL_ROWS, KEY_VALUE_WIDTH)
    return (base_output + adapter_scale * widen_rows).astype(jnp.bfloat16)
```

```python
import functools

import jax
import jax.numpy as jnp
from jax import lax
from jax.experimental import pallas as pl
from jax.experimental.pallas import tpu as pltpu
from jax.sharding import Mesh, PartitionSpec as P

Y, X, Z, C = 8, 4, 8, 2
T = Z * C
GROUPS = Y * X
LIMIT = 2
VMEM_LIMIT = 48 * 1024 * 1024


def copies(count, source_of, target_of, sems):
    def start(i, carry):
        pltpu.make_async_copy(source_of(i), target_of(i), sems.at[i]).start()
        return carry

    def wait(i, carry):
        pltpu.make_async_copy(source_of(i), target_of(i), sems.at[i]).wait()
        return carry

    lax.fori_loop(0, count, start, 0)
    lax.fori_loop(0, count, wait, 0)


def pick_down_kernel(picked, down, out, sems):
    def source(i):
        x, rest = i // (Y * LIMIT), i % (Y * LIMIT)
        y, j = rest // LIMIT, rest % LIMIT
        return down.at[picked[(y * X + x) * LIMIT + j]]

    copies(GROUPS * LIMIT, source, lambda i: out.at[i], sems)


def pick_up_kernel(picked, up, out, sems):
    copies(GROUPS * LIMIT, lambda i: up.at[picked[i]], lambda i: out.at[i], sems)


def pick(kernel, picked, table):
    count = GROUPS * LIMIT
    out = jax.ShapeDtypeStruct((count,) + table.shape[1:], table.dtype)
    return pl.pallas_call(
        kernel,
        out_shape=out,
        in_specs=[
            pl.BlockSpec(memory_space=pltpu.SMEM),
            pl.BlockSpec(memory_space=pl.ANY),
        ],
        out_specs=pl.BlockSpec(memory_space=pl.ANY),
        scratch_shapes=[pltpu.SemaphoreType.DMA((count,))],
        cost_estimate=pl.CostEstimate(
            flops=0, bytes_accessed=2 * out.size * out.dtype.itemsize, transcendentals=0
        ),
    )(picked, table)


def prepare_kernel(resident, place, plan, slots, rows, rows_out, code_out):
    count = rows.shape[0]
    slot = slots[...]
    code = slot
    before = jnp.int32(-1)
    for k in range(plan.shape[1]):
        home = plan[place[0], k] // resident
        second = (home == before).astype(jnp.int32)
        code = jnp.where(slot == resident + k, resident + home * LIMIT + second, code)
        before = home
    code_out[...] = code
    rows_out[0:count, :] = rows[...]
    wide = jnp.concatenate([code.astype(jnp.float32), jnp.zeros((1, rows.shape[1] - count), jnp.float32)], axis=1)
    rows_out[count:, :] = jnp.broadcast_to(wide, (rows_out.shape[0] - count, rows.shape[1])).astype(rows_out.dtype)


def prepare(resident, group, plan, slots, rows):
    count, width = rows.shape
    smem = pl.BlockSpec(memory_space=pltpu.SMEM)
    vmem = pl.BlockSpec(memory_space=pltpu.VMEM)
    return pl.pallas_call(
        functools.partial(prepare_kernel, resident),
        out_shape=(
            jax.ShapeDtypeStruct((count + 16, width), rows.dtype),
            jax.ShapeDtypeStruct((1, count), jnp.int32),
        ),
        in_specs=[smem, smem, vmem, vmem],
        out_specs=(vmem, vmem),
    )(group, plan, slots, rows)


NT = (((1,), (1,)), ((), ()))


def local_kernel(code, rows, down, out):
    rank = out.shape[0]
    resident = down.shape[0] // rank
    total = jnp.zeros(out.shape, jnp.float32)
    step = 4
    for first in range(0, resident, step):
        product = lax.dot_general(
            down[first * rank : (first + step) * rank, :], rows[...], NT, preferred_element_type=jnp.float32
        )
        for k in range(step):
            total = total + jnp.where(code[...] == first + k, product[k * rank : (k + 1) * rank, :], 0.0)
    out[...] = total


def local_shrink(code, rows, down):
    resident, rank, width = down.shape
    vmem = pl.BlockSpec(memory_space=pltpu.VMEM)
    return pl.pallas_call(
        local_kernel,
        out_shape=jax.ShapeDtypeStruct((rank, rows.shape[0]), jnp.float32),
        in_specs=[vmem] * 3,
        out_specs=vmem,
        compiler_params=pltpu.CompilerParams(vmem_limit_bytes=VMEM_LIMIT),
        cost_estimate=pl.CostEstimate(
            flops=2 * rows.size * resident * rank, bytes_accessed=2 * down.size, transcendentals=0
        ),
    )(code, rows, down.reshape(resident * rank, width))


def imported_kernel(resident, place, rows, down, own, out):
    group = pl.program_id(0)
    rank, count = own.shape
    code = rows[0, count : count + 1, :count].astype(jnp.float32)
    base = (resident + place[0] * X * LIMIT).astype(jnp.float32)
    total = jnp.where(group == place[0], own[...], 0.0)
    for x in range(X):
        product = lax.dot_general(
            down[x, 0], rows[0, 0:count, :], NT, preferred_element_type=jnp.float32
        )
        for j in range(LIMIT):
            hit = code == base + (x * LIMIT + j)
            total = total + jnp.where(hit, product[j * rank : (j + 1) * rank, :], 0.0)
    for i in range(rank // 8):
        for k in range(count // 128):
            out[0, i * (count // 128) + k] = total[i * 8 : (i + 1) * 8, k * 128 : (k + 1) * 128]


def imported_shrink(resident, y, rows, down, own):
    rank, count = own.shape
    width = rows.shape[-1]
    height = rows.shape[1]
    blocks = rank * count // 1024
    return pl.pallas_call(
        functools.partial(imported_kernel, resident),
        grid=(Y,),
        out_shape=jax.ShapeDtypeStruct((Y, blocks, 8, 128), jnp.float32),
        in_specs=[
            pl.BlockSpec(memory_space=pltpu.SMEM),
            pl.BlockSpec((1, height, width), lambda i: (i, 0, 0)),
            pl.BlockSpec((X, 1, LIMIT * rank, width), lambda i: (0, i, 0, 0)),
            pl.BlockSpec((rank, count), lambda i: (0, 0)),
        ],
        out_specs=pl.BlockSpec((1, blocks, 8, 128), lambda i: (i, 0, 0, 0)),
        compiler_params=pltpu.CompilerParams(vmem_limit_bytes=VMEM_LIMIT),
        cost_estimate=pl.CostEstimate(
            flops=2 * down.size * count, bytes_accessed=2 * (down.size + rows.size), transcendentals=0
        ),
    )(y, rows, down, own)


def add_kernel(parts, out):
    total = jnp.sum(parts[...], axis=0)
    for t in range(out.shape[0]):
        out[t] = total


def add_and_spread(parts):
    vmem = pl.BlockSpec(memory_space=pltpu.VMEM)
    return pl.pallas_call(
        add_kernel,
        out_shape=jax.ShapeDtypeStruct((T,) + parts.shape[1:], jnp.float32),
        in_specs=[vmem],
        out_specs=vmem,
    )(parts)


def expand_kernel(shrink, code, up, up_in, base, out):
    count = out.shape[0]
    lanes = count // 128
    rank = shrink.shape[0] // lanes * 8
    resident, imported = up.shape[0], up_in.shape[0]
    rows = jnp.concatenate(
        [jnp.concatenate([shrink[i * lanes + k] for k in range(lanes)], axis=1) for i in range(rank // 8)], axis=0
    )
    rows = jnp.transpose(rows)
    column = jnp.transpose(jnp.broadcast_to(code[...], (8, count)).astype(jnp.float32))[:, :1]
    pair = jnp.concatenate([rows, rows], axis=1)
    high = pair.astype(jnp.bfloat16).astype(jnp.float32)
    low = pair - high
    half = lax.broadcasted_iota(jnp.int32, pair.shape, 1) // rank
    wanted = jnp.broadcast_to(column, pair.shape) - half.astype(jnp.float32)
    both = jnp.concatenate([high, low], axis=0)
    wanted = jnp.concatenate([wanted, wanted], axis=0)
    total = jnp.zeros((2 * count, out.shape[1]), jnp.float32)
    step = 4
    for table, start in ((up, 0), (up_in, resident)):
        pairs = table.shape[0] // 2
        for first in range(0, pairs, step):
            placed = jnp.concatenate(
                [
                    jnp.where(wanted == float(start + 2 * p), both, 0.0).astype(jnp.bfloat16)
                    for p in range(first, first + step)
                ],
                axis=1,
            )
            maps = table[2 * first : 2 * (first + step)].reshape(2 * step * rank, out.shape[1])
            total = total + jnp.dot(placed, maps, preferred_element_type=jnp.float32)
    out[...] = (base[...] + (total[:count] + total[count:])).astype(out.dtype)


def expand(shrink, code, up, up_in, base):
    vmem = pl.BlockSpec(memory_space=pltpu.VMEM)
    return pl.pallas_call(
        expand_kernel,
        out_shape=jax.ShapeDtypeStruct(base.shape, jnp.bfloat16),
        in_specs=[vmem] * 5,
        out_specs=vmem,
        compiler_params=pltpu.CompilerParams(vmem_limit_bytes=VMEM_LIMIT),
    )(shrink, code, up, up_in, base)


def shards(inputs, row_adapter_slot, transfer_plan, key_value_weight, adapter_down, adapter_up):
    count, width = inputs.shape
    resident, rank, _ = adapter_down.shape
    y, x = lax.axis_index("y"), lax.axis_index("x")
    group = y * X + x

    mine = transfer_plan // resident == group
    after = jnp.pad(mine[:, :-1], ((0, 0), (1, 0)))
    number = transfer_plan % resident
    picked = jnp.stack(
        [
            jnp.sum(jnp.where(mine & ~after, number, 0), axis=1),
            jnp.sum(jnp.where(mine & after, number, 0), axis=1),
        ],
        axis=1,
    ).reshape(-1)

    down_out = pick(pick_down_kernel, picked, adapter_down).reshape(X, Y * LIMIT, rank, width)
    down_in = lax.all_to_all(down_out, "x", 0, 0, tiled=True)

    sent_rows, code = prepare(
        resident, group.reshape(1), transfer_plan, row_adapter_slot.reshape(1, count), inputs
    )
    rows = lax.all_gather(sent_rows, "y")

    base_part = jnp.dot(inputs, key_value_weight, preferred_element_type=jnp.float32)
    base = lax.psum_scatter(base_part, ("z", "c"), scatter_dimension=1, tiled=True)

    own = local_shrink(code, inputs, adapter_down)
    parts = imported_shrink(
        resident, y.reshape(1), rows, down_in.reshape(X, Y, LIMIT * rank, width), own
    )
    parts = lax.all_to_all(parts.reshape(Y * T, 8, 128), ("y", "z", "c"), 0, 0, tiled=True)
    shrink = lax.all_to_all(add_and_spread(parts), ("z", "c"), 0, 0, tiled=True)

    up_out = pick(pick_up_kernel, picked, adapter_up)
    up_in = lax.all_to_all(up_out, ("y", "x"), 0, 0, tiled=True)
    return expand(shrink, code, adapter_up, up_in, base)


def solution(mesh):
    grid = Mesh(mesh.devices.reshape(Y, X, Z, C), ("y", "x", "z", "c"))
    replica, tensor = ("y", "x"), ("z", "c")
    placed = (
        P(replica, tensor),
        P(replica),
        P(),
        P(tensor, None),
        P(replica, None, tensor),
        P(replica, None, tensor),
    )
    return jax.shard_map(
        shards, mesh=grid, in_specs=placed, out_specs=P(replica, tensor), check_vma=False
    )
```

```python
import functools

import jax
import jax.numpy as jnp
from jax import lax
from jax.experimental import pallas as pl
from jax.experimental.pallas import tpu as pltpu
from jax.sharding import Mesh, PartitionSpec as P

Y, X, Z, C = 8, 4, 8, 2
T = Z * C
GROUPS = Y * X
LIMIT = 2
VMEM_LIMIT = 48 * 1024 * 1024


def dispatch_kernel(place, plan, plan_row, slots, rows, down, down_out, rows_out, code_out, picked_out,
                    staged, picked, read_sems, write_sems, picked_sem):
    resident = down.shape[0]
    group = place[0] * X + place[1]
    table = plan[...]
    home = table // resident
    number = table - home * resident
    mine = (home == group).astype(jnp.int32)
    after = jnp.concatenate([jnp.zeros((mine.shape[0], 1), jnp.int32), mine[:, :-1]], axis=1)
    first = jnp.sum(mine * (1 - after) * number, axis=1, keepdims=True)
    second = jnp.sum(mine * after * number, axis=1, keepdims=True)
    lane = lax.broadcasted_iota(jnp.int32, picked_out.shape, 1)
    picked_out[...] = jnp.where(lane == 0, first, jnp.where(lane == 1, second, 0))
    to_scalars = pltpu.make_async_copy(picked_out, picked, picked_sem)
    to_scalars.start()
    to_scalars.wait()

    def read(i):
        x, rest = i // (Y * LIMIT), i % (Y * LIMIT)
        wanted = picked[rest // LIMIT * X + x, rest % LIMIT]
        return pltpu.make_async_copy(down.at[wanted], staged.at[i], read_sems.at[i])

    def write(i):
        return pltpu.make_async_copy(staged.at[i], down_out.at[i], write_sems.at[i])

    def begin(i, carry):
        read(i).start()
        return carry

    def forward(i, carry):
        read(i).wait()
        write(i).start()
        return carry

    def finish(i, carry):
        write(i).wait()
        return carry

    count = GROUPS * LIMIT
    lax.fori_loop(0, count, begin, 0)

    height = rows.shape[0]
    slot = slots[...]
    code = slot
    before = jnp.int32(-1)
    for k in range(plan_row.shape[1]):
        its_home = plan_row[group, k] // resident
        again = (its_home == before).astype(jnp.int32)
        code = jnp.where(slot == resident + k, resident + its_home * LIMIT + again, code)
        before = its_home
    code_out[...] = code
    rows_out[0:height, :] = rows[...]
    wide = jnp.concatenate(
        [code.astype(jnp.float32), jnp.zeros((1, rows.shape[1] - height), jnp.float32)], axis=1
    )
    tail = (rows_out.shape[0] - height, rows.shape[1])
    rows_out[height:, :] = jnp.broadcast_to(wide, tail).astype(rows_out.dtype)

    lax.fori_loop(0, count, forward, 0)
    lax.fori_loop(0, count, finish, 0)


def dispatch(place, plan, slots, rows, down):
    height, width = rows.shape
    count = GROUPS * LIMIT
    smem = pl.BlockSpec(memory_space=pltpu.SMEM)
    vmem = pl.BlockSpec(memory_space=pltpu.VMEM)
    hbm = pl.BlockSpec(memory_space=pl.ANY)
    return pl.pallas_call(
        dispatch_kernel,
        out_shape=(
            jax.ShapeDtypeStruct((count,) + down.shape[1:], down.dtype),
            jax.ShapeDtypeStruct((height + 16, width), rows.dtype),
            jax.ShapeDtypeStruct((1, height), jnp.int32),
            jax.ShapeDtypeStruct((GROUPS, 128), jnp.int32),
        ),
        in_specs=[smem, vmem, smem, vmem, vmem, hbm],
        out_specs=(hbm, vmem, vmem, vmem),
        scratch_shapes=[
            pltpu.VMEM((count,) + down.shape[1:], down.dtype),
            pltpu.SMEM((GROUPS, 128), jnp.int32),
            pltpu.SemaphoreType.DMA((count,)),
            pltpu.SemaphoreType.DMA((count,)),
            pltpu.SemaphoreType.DMA,
        ],
        compiler_params=pltpu.CompilerParams(vmem_limit_bytes=VMEM_LIMIT),
        cost_estimate=pl.CostEstimate(flops=0, bytes_accessed=4 * count * down[0].size, transcendentals=0),
    )(place, plan, plan, slots, rows, down)


def pick_up_kernel(place, picked, up, *outs):
    for d in range(Y):
        y = (place[0] + d) % Y
        for x in range(X):
            for j in range(LIMIT):
                outs[d][x * LIMIT + j] = up[picked[y * X + x, j]]


def pick_up(place, picked, up):
    smem = pl.BlockSpec(memory_space=pltpu.SMEM)
    vmem = pl.BlockSpec(memory_space=pltpu.VMEM)
    shape = jax.ShapeDtypeStruct((X * LIMIT,) + up.shape[1:], up.dtype)
    return pl.pallas_call(
        pick_up_kernel,
        out_shape=(shape,) * Y,
        in_specs=[smem, smem, vmem],
        out_specs=(vmem,) * Y,
        cost_estimate=pl.CostEstimate(flops=0, bytes_accessed=6 * up.size, transcendentals=0),
    )(place, picked, up)


def turn_kernel(place, *refs):
    arrived, outs = refs[:Y], refs[Y:]
    for e in range(X):
        x = (place[1] + e) % X
        for d in range(Y):
            outs[e][d * LIMIT : (d + 1) * LIMIT] = arrived[d][pl.ds(x * LIMIT, LIMIT)]


def turn(place, arrived):
    vmem = pl.BlockSpec(memory_space=pltpu.VMEM)
    shape = jax.ShapeDtypeStruct((Y * LIMIT,) + arrived[0].shape[1:], arrived[0].dtype)
    return pl.pallas_call(
        turn_kernel,
        out_shape=(shape,) * X,
        in_specs=[pl.BlockSpec(memory_space=pltpu.SMEM)] + [vmem] * Y,
        out_specs=(vmem,) * X,
        cost_estimate=pl.CostEstimate(
            flops=0, bytes_accessed=4 * Y * arrived[0].size, transcendentals=0
        ),
    )(place, *arrived)


NT = (((1,), (1,)), ((), ()))


def local_kernel(code, rows, down, out):
    rank = out.shape[0]
    resident = down.shape[0] // rank
    total = jnp.zeros(out.shape, jnp.float32)
    step = 4
    for first in range(0, resident, step):
        product = lax.dot_general(
            down[first * rank : (first + step) * rank, :], rows[...], NT, preferred_element_type=jnp.float32
        )
        for k in range(step):
            total = total + jnp.where(code[...] == first + k, product[k * rank : (k + 1) * rank, :], 0.0)
    out[...] = total


def local_shrink(code, rows, down):
    resident, rank, width = down.shape
    vmem = pl.BlockSpec(memory_space=pltpu.VMEM)
    return pl.pallas_call(
        local_kernel,
        out_shape=jax.ShapeDtypeStruct((rank, rows.shape[0]), jnp.float32),
        in_specs=[vmem] * 3,
        out_specs=vmem,
        cost_estimate=pl.CostEstimate(
            flops=2 * rows.size * resident * rank, bytes_accessed=2 * down.size, transcendentals=0
        ),
    )(code, rows, down.reshape(resident * rank, width))


def imported_kernel(resident, place, rows, down, own, keep, give):
    group = pl.program_id(0)
    rank, count = own.shape
    half = count // C
    code = rows[0, count : count + 1, :count].astype(jnp.float32)
    base = (resident + place[0] * X * LIMIT).astype(jnp.float32)
    total = jnp.where(group == place[0], own[...], 0.0)
    product = lax.dot_general(
        down[...].reshape(X * LIMIT * rank, down.shape[-1]),
        rows[0, 0:count, :],
        NT,
        preferred_element_type=jnp.float32,
    )
    for k in range(X * LIMIT):
        total = total + jnp.where(code == base + k, product[k * rank : (k + 1) * rank, :], 0.0)
    mine = place[2] == 0
    left, right = total[:, :half], total[:, half:]
    keep[...] = jnp.where(mine, left, right).reshape(keep.shape)
    give[...] = jnp.where(mine, right, left).reshape(give.shape)


def imported_shrink(resident, place, rows, down, own):
    rank, count = own.shape
    width = rows.shape[-1]
    height = rows.shape[1]
    shape = jax.ShapeDtypeStruct((Y, rank // 8, 8, count // C), jnp.float32)
    block = pl.BlockSpec((1, rank // 8, 8, count // C), lambda i: (i, 0, 0, 0))
    return pl.pallas_call(
        functools.partial(imported_kernel, resident),
        grid=(Y,),
        out_shape=(shape, shape),
        in_specs=[
            pl.BlockSpec(memory_space=pltpu.SMEM),
            pl.BlockSpec((1, height, width), lambda i: (i, 0, 0)),
            pl.BlockSpec((X, 1, LIMIT * rank, width), lambda i: (0, i, 0, 0)),
            pl.BlockSpec((rank, count), lambda i: (0, 0)),
        ],
        out_specs=(block, block),
        cost_estimate=pl.CostEstimate(
            flops=2 * down.size * count, bytes_accessed=2 * (down.size + rows.size), transcendentals=0
        ),
    )(place, rows, down, own)


def add_kernel(parts, out):
    total = jnp.sum(parts[...], axis=0)
    for t in range(out.shape[0]):
        out[t] = total


def add_and_spread(parts):
    vmem = pl.BlockSpec(memory_space=pltpu.VMEM)
    return pl.pallas_call(
        add_kernel,
        out_shape=jax.ShapeDtypeStruct((T,) + parts.shape[1:], jnp.float32),
        in_specs=[vmem],
        out_specs=vmem,
    )(parts)


def expand_kernel(place, shrink, code, base, up, *refs):
    tables, out = refs[:-1], refs[-1]
    count = out.shape[0]
    lanes = count // 128
    rank = shrink.shape[0] // lanes * 8
    resident = up.shape[0]
    imported = code[...] - resident
    home = imported // LIMIT
    e = (place[1] - home % X + X) % X
    d = (place[0] - home // X + Y) % Y
    at = jnp.where(imported < 0, code[...], resident + (e * Y + d) * LIMIT + imported % LIMIT)
    rows = jnp.concatenate(
        [jnp.concatenate([shrink[i * lanes + k] for k in range(lanes)], axis=1) for i in range(rank // 8)], axis=0
    )
    rows = jnp.transpose(rows)
    column = jnp.transpose(jnp.broadcast_to(at, (8, count)).astype(jnp.float32))[:, :1]
    pair = jnp.concatenate([rows, rows], axis=1)
    high = pair.astype(jnp.bfloat16).astype(jnp.float32)
    low = pair - high
    half = lax.broadcasted_iota(jnp.int32, pair.shape, 1) // rank
    wanted = jnp.broadcast_to(column, pair.shape) - half.astype(jnp.float32)
    both = jnp.concatenate([high, low], axis=0)
    wanted = jnp.concatenate([wanted, wanted], axis=0)
    total = jnp.zeros((2 * count, out.shape[1]), jnp.float32)
    step = 4
    start = 0
    for table in (up,) + tables:
        for first in range(0, table.shape[0] // 2, step):
            placed = jnp.concatenate(
                [
                    jnp.where(wanted == float(start + 2 * p), both, 0.0).astype(jnp.bfloat16)
                    for p in range(first, first + step)
                ],
                axis=1,
            )
            maps = table[2 * first : 2 * (first + step)].reshape(2 * step * rank, out.shape[1])
            total = total + jnp.dot(placed, maps, preferred_element_type=jnp.float32)
        start += table.shape[0]
    out[...] = (base[...] + (total[:count] + total[count:])).astype(out.dtype)


def expand(place, shrink, code, base, up, tables):
    vmem = pl.BlockSpec(memory_space=pltpu.VMEM)
    return pl.pallas_call(
        expand_kernel,
        out_shape=jax.ShapeDtypeStruct(base.shape, jnp.bfloat16),
        in_specs=[pl.BlockSpec(memory_space=pltpu.SMEM)] + [vmem] * (4 + len(tables)),
        out_specs=vmem,
    )(place, shrink, code, base, up, *tables)


def shift(array, axis, size, by):
    return lax.ppermute(array, axis, [(i, (i + by) % size) for i in range(size)])


def shards(inputs, row_adapter_slot, transfer_plan, key_value_weight, adapter_down, adapter_up):
    count, width = inputs.shape
    resident, rank, _ = adapter_down.shape
    place = jnp.stack([lax.axis_index("y"), lax.axis_index("x"), lax.axis_index("c")])

    down_out, sent_rows, code, picked = dispatch(
        place, transfer_plan, row_adapter_slot.reshape(1, count), inputs, adapter_down
    )
    down_in = lax.all_to_all(down_out.reshape(X, Y * LIMIT, rank, width), "x", 0, 0, tiled=True)
    rows = lax.all_gather(sent_rows, "y")

    base_part = jnp.dot(inputs, key_value_weight, preferred_element_type=jnp.float32)
    base = lax.psum_scatter(base_part, ("z", "c"), scatter_dimension=1, tiled=True)
    own = local_shrink(code, inputs, adapter_down)

    ups = pick_up(place, picked, adapter_up)
    arrived = [ups[0]] + [shift(ups[d], "y", Y, d) for d in range(1, Y)]
    ups = turn(place, arrived)
    tables = [ups[0]] + [shift(ups[e], "x", X, e) for e in range(1, X)]

    keep, give = imported_shrink(
        resident, place, rows, down_in.reshape(X, Y, LIMIT * rank, width), own
    )
    parts = keep + shift(give, "c", C, 1)
    parts = lax.all_to_all(parts.reshape(Y * Z, 8, 128), ("y", "z"), 0, 0, tiled=True)
    shrink = lax.all_to_all(add_and_spread(parts), ("z", "c"), 0, 0, tiled=True)
    return expand(place, shrink, code, base, adapter_up, tables)


def solution(mesh):
    grid = Mesh(mesh.devices.reshape(Y, X, Z, C), ("y", "x", "z", "c"))
    replica, tensor = ("y", "x"), ("z", "c")
    placed = (
        P(replica, tensor),
        P(replica),
        P(),
        P(tensor, None),
        P(replica, None, tensor),
        P(replica, None, tensor),
    )
    return jax.shard_map(
        shards, mesh=grid, in_specs=placed, out_specs=P(replica, tensor), check_vma=False
    )
```

```python
import functools

import jax
import jax.numpy as jnp
from jax import lax
from jax.experimental import pallas as pl
from jax.experimental.pallas import tpu as pltpu
from jax.sharding import Mesh, PartitionSpec as P

Y, X, Z, C = 8, 4, 8, 2
T = Z * C
GROUPS = Y * X
LIMIT = 2
VMEM_LIMIT = 48 * 1024 * 1024


def dispatch_kernel(place, plan, plan_row, slots, rows, down, down_out, rows_out, code_out, picked_out,
                    picked, picked_sem):
    resident = down.shape[0]
    group = place[0] * X + place[1]
    x = pl.program_id(0)

    @pl.when(x == 0)
    def _():
        table = plan[...]
        home = table // resident
        number = table - home * resident
        mine = (home == group).astype(jnp.int32)
        after = jnp.concatenate([jnp.zeros((mine.shape[0], 1), jnp.int32), mine[:, :-1]], axis=1)
        first = jnp.sum(mine * (1 - after) * number, axis=1, keepdims=True)
        second = jnp.sum(mine * after * number, axis=1, keepdims=True)
        lane = lax.broadcasted_iota(jnp.int32, picked_out.shape, 1)
        picked_out[...] = jnp.where(lane == 0, first, jnp.where(lane == 1, second, 0))
        to_scalars = pltpu.make_async_copy(picked_out, picked, picked_sem)
        to_scalars.start()

        height = rows.shape[0]
        slot = slots[...]
        code = slot
        before = jnp.int32(-1)
        for k in range(plan_row.shape[1]):
            its_home = plan_row[group, k] // resident
            again = (its_home == before).astype(jnp.int32)
            code = jnp.where(slot == resident + k, resident + its_home * LIMIT + again, code)
            before = its_home
        code_out[...] = code
        rows_out[0:height, :] = rows[...]
        wide = jnp.concatenate(
            [code.astype(jnp.float32), jnp.zeros((1, rows.shape[1] - height), jnp.float32)], axis=1
        )
        tail = (rows_out.shape[0] - height, rows.shape[1])
        rows_out[height:, :] = jnp.broadcast_to(wide, tail).astype(rows_out.dtype)
        to_scalars.wait()

    for y in range(Y):
        for j in range(LIMIT):
            down_out[0, y * LIMIT + j] = down[picked[y * X + x, j]]


def dispatch(place, plan, slots, rows, down):
    height, width = rows.shape
    smem = pl.BlockSpec(memory_space=pltpu.SMEM)

    def whole(shape):
        return pl.BlockSpec(shape, lambda i: (0,) * len(shape))

    return pl.pallas_call(
        dispatch_kernel,
        grid=(X,),
        out_shape=(
            jax.ShapeDtypeStruct((X, Y * LIMIT) + down.shape[1:], down.dtype),
            jax.ShapeDtypeStruct((height + 16, width), rows.dtype),
            jax.ShapeDtypeStruct((1, height), jnp.int32),
            jax.ShapeDtypeStruct((GROUPS, 128), jnp.int32),
        ),
        in_specs=[smem, whole(plan.shape), smem, whole(slots.shape), whole(rows.shape), whole(down.shape)],
        out_specs=(
            pl.BlockSpec((1, Y * LIMIT) + down.shape[1:], lambda i: (i, 0, 0, 0)),
            whole((height + 16, width)),
            whole((1, height)),
            whole((GROUPS, 128)),
        ),
        scratch_shapes=[pltpu.SMEM((GROUPS, 128), jnp.int32), pltpu.SemaphoreType.DMA],
        cost_estimate=pl.CostEstimate(flops=0, bytes_accessed=6 * down.size, transcendentals=0),
    )(place, plan, plan, slots, rows, down)


def pick_up_kernel(place, picked, up, *outs):
    for d in range(Y):
        y = (place[0] + d) % Y
        for x in range(X):
            for j in range(LIMIT):
                outs[d][x * LIMIT + j] = up[picked[y * X + x, j]]


def pick_up(place, picked, up):
    smem = pl.BlockSpec(memory_space=pltpu.SMEM)
    vmem = pl.BlockSpec(memory_space=pltpu.VMEM)
    shape = jax.ShapeDtypeStruct((X * LIMIT,) + up.shape[1:], up.dtype)
    return pl.pallas_call(
        pick_up_kernel,
        out_shape=(shape,) * Y,
        in_specs=[smem, smem, vmem],
        out_specs=(vmem,) * Y,
        cost_estimate=pl.CostEstimate(flops=0, bytes_accessed=6 * up.size, transcendentals=0),
    )(place, picked, up)


def turn_kernel(place, *refs):
    arrived, outs = refs[:Y], refs[Y:]
    for e in range(X):
        x = (place[1] + e) % X
        for d in range(Y):
            outs[e][d * LIMIT : (d + 1) * LIMIT] = arrived[d][pl.ds(x * LIMIT, LIMIT)]


def turn(place, arrived):
    vmem = pl.BlockSpec(memory_space=pltpu.VMEM)
    shape = jax.ShapeDtypeStruct((Y * LIMIT,) + arrived[0].shape[1:], arrived[0].dtype)
    return pl.pallas_call(
        turn_kernel,
        out_shape=(shape,) * X,
        in_specs=[pl.BlockSpec(memory_space=pltpu.SMEM)] + [vmem] * Y,
        out_specs=(vmem,) * X,
        cost_estimate=pl.CostEstimate(
            flops=0, bytes_accessed=4 * Y * arrived[0].size, transcendentals=0
        ),
    )(place, *arrived)


NT = (((1,), (1,)), ((), ()))


def local_kernel(code, rows, down, out):
    rank = out.shape[0]
    resident = down.shape[0] // rank
    total = jnp.zeros(out.shape, jnp.float32)
    step = 4
    for first in range(0, resident, step):
        product = lax.dot_general(
            down[first * rank : (first + step) * rank, :], rows[...], NT, preferred_element_type=jnp.float32
        )
        for k in range(step):
            total = total + jnp.where(code[...] == first + k, product[k * rank : (k + 1) * rank, :], 0.0)
    out[...] = total


def local_shrink(code, rows, down):
    resident, rank, width = down.shape
    vmem = pl.BlockSpec(memory_space=pltpu.VMEM)
    return pl.pallas_call(
        local_kernel,
        out_shape=jax.ShapeDtypeStruct((rank, rows.shape[0]), jnp.float32),
        in_specs=[vmem] * 3,
        out_specs=vmem,
        cost_estimate=pl.CostEstimate(
            flops=2 * rows.size * resident * rank, bytes_accessed=2 * down.size, transcendentals=0
        ),
    )(code, rows, down.reshape(resident * rank, width))


def imported_kernel(resident, place, rows, *refs):
    down, (own, keep, give) = refs[:X], refs[X:]
    group = pl.program_id(0)
    rank, count = own.shape
    half = count // C
    code = rows[0, count : count + 1, :count].astype(jnp.float32)
    base = (resident + place[0] * X * LIMIT).astype(jnp.float32)
    total = jnp.where(group == place[0], own[...], 0.0)
    product = lax.dot_general(
        jnp.concatenate([part[0, 0] for part in down], axis=0),
        rows[0, 0:count, :],
        NT,
        preferred_element_type=jnp.float32,
    )
    for k in range(X * LIMIT):
        total = total + jnp.where(code == base + k, product[k * rank : (k + 1) * rank, :], 0.0)
    mine = place[2] == 0
    left, right = total[:, :half], total[:, half:]
    keep[...] = jnp.where(mine, left, right).reshape(keep.shape)
    give[...] = jnp.where(mine, right, left).reshape(give.shape)


def imported_shrink(resident, place, rows, down, own):
    rank, count = own.shape
    width = rows.shape[-1]
    height = rows.shape[1]
    shape = jax.ShapeDtypeStruct((Y, rank // 8, 8, count // C), jnp.float32)
    block = pl.BlockSpec((1, rank // 8, 8, count // C), lambda i: (i, 0, 0, 0))
    return pl.pallas_call(
        functools.partial(imported_kernel, resident),
        grid=(Y,),
        out_shape=(shape, shape),
        in_specs=[
            pl.BlockSpec(memory_space=pltpu.SMEM),
            pl.BlockSpec((1, height, width), lambda i: (i, 0, 0)),
        ]
        + [
            pl.BlockSpec((1, 1, LIMIT * rank, width), functools.partial(lambda x, i: (x, i, 0, 0), x))
            for x in range(X)
        ]
        + [
            pl.BlockSpec((rank, count), lambda i: (0, 0)),
        ],
        out_specs=(block, block),
        cost_estimate=pl.CostEstimate(
            flops=2 * down.size * count, bytes_accessed=2 * (down.size + rows.size), transcendentals=0
        ),
    )(place, rows, *([down] * X), own)


def add_kernel(parts, out):
    total = jnp.sum(parts[...], axis=0)
    for t in range(out.shape[0]):
        out[t] = total


def add_and_spread(parts):
    vmem = pl.BlockSpec(memory_space=pltpu.VMEM)
    return pl.pallas_call(
        add_kernel,
        out_shape=jax.ShapeDtypeStruct((T,) + parts.shape[1:], jnp.float32),
        in_specs=[vmem],
        out_specs=vmem,
    )(parts)


def expand_kernel(place, shrink, code, base, up, *refs):
    tables, out = refs[:-1], refs[-1]
    count = out.shape[0]
    lanes = count // 128
    rank = shrink.shape[0] // lanes * 8
    resident = up.shape[0]
    imported = code[...] - resident
    home = imported // LIMIT
    e = (place[1] - home % X + X) % X
    d = (place[0] - home // X + Y) % Y
    at = jnp.where(imported < 0, code[...], resident + (e * Y + d) * LIMIT + imported % LIMIT)
    rows = jnp.concatenate(
        [jnp.concatenate([shrink[i * lanes + k] for k in range(lanes)], axis=1) for i in range(rank // 8)], axis=0
    )
    rows = jnp.transpose(rows)
    column = jnp.transpose(jnp.broadcast_to(at, (8, count)).astype(jnp.float32))[:, :1]
    pair = jnp.concatenate([rows, rows], axis=1)
    high = pair.astype(jnp.bfloat16).astype(jnp.float32)
    low = pair - high
    half = lax.broadcasted_iota(jnp.int32, pair.shape, 1) // rank
    wanted = jnp.broadcast_to(column, pair.shape) - half.astype(jnp.float32)
    both = jnp.concatenate([high, low], axis=0)
    wanted = jnp.concatenate([wanted, wanted], axis=0)
    total = jnp.zeros((2 * count, out.shape[1]), jnp.float32)
    step = 4
    start = 0
    for table in (up,) + tables:
        for first in range(0, table.shape[0] // 2, step):
            placed = jnp.concatenate(
                [
                    jnp.where(wanted == float(start + 2 * p), both, 0.0).astype(jnp.bfloat16)
                    for p in range(first, first + step)
                ],
                axis=1,
            )
            maps = table[2 * first : 2 * (first + step)].reshape(2 * step * rank, out.shape[1])
            total = total + jnp.dot(placed, maps, preferred_element_type=jnp.float32)
        start += table.shape[0]
    out[...] = (base[...] + (total[:count] + total[count:])).astype(out.dtype)


def expand(place, shrink, code, base, up, tables):
    vmem = pl.BlockSpec(memory_space=pltpu.VMEM)
    return pl.pallas_call(
        expand_kernel,
        out_shape=jax.ShapeDtypeStruct(base.shape, jnp.bfloat16),
        in_specs=[pl.BlockSpec(memory_space=pltpu.SMEM)] + [vmem] * (4 + len(tables)),
        out_specs=vmem,
    )(place, shrink, code, base, up, *tables)


def shift(array, axis, size, by):
    return lax.ppermute(array, axis, [(i, (i + by) % size) for i in range(size)])


def shards(inputs, row_adapter_slot, transfer_plan, key_value_weight, adapter_down, adapter_up):
    count, width = inputs.shape
    resident, rank, _ = adapter_down.shape
    place = jnp.stack([lax.axis_index("y"), lax.axis_index("x"), lax.axis_index("c")])

    down_out, sent_rows, code, picked = dispatch(
        place, transfer_plan, row_adapter_slot.reshape(1, count), inputs, adapter_down
    )
    down_in = lax.all_to_all(down_out, "x", 0, 0, tiled=True)
    rows = lax.all_gather(sent_rows, "y")

    base_part = jnp.dot(inputs, key_value_weight, preferred_element_type=jnp.float32)
    base = lax.psum_scatter(base_part, ("z", "c"), scatter_dimension=1, tiled=True)
    own = local_shrink(code, inputs, adapter_down)

    ups = pick_up(place, picked, adapter_up)
    arrived = [ups[0]] + [shift(ups[d], "y", Y, d) for d in range(1, Y)]
    down_in, arrived = lax.optimization_barrier((down_in, arrived))
    ups = turn(place, arrived)
    tables = [ups[0]] + [shift(ups[e], "x", X, e) for e in range(1, X)]

    keep, give = imported_shrink(
        resident, place, rows, down_in.reshape(X, Y, LIMIT * rank, width), own
    )
    parts = keep + shift(give, "c", C, 1)
    parts = lax.all_to_all(parts.reshape(Y * Z, 8, 128), ("y", "z"), 0, 0, tiled=True)
    shrink = lax.all_to_all(add_and_spread(parts), ("z", "c"), 0, 0, tiled=True)
    return expand(place, shrink, code, base, adapter_up, tables)


def solution(mesh):
    grid = Mesh(mesh.devices.reshape(Y, X, Z, C), ("y", "x", "z", "c"))
    replica, tensor = ("y", "x"), ("z", "c")
    placed = (
        P(replica, tensor),
        P(replica),
        P(),
        P(tensor, None),
        P(replica, None, tensor),
        P(replica, None, tensor),
    )
    return jax.shard_map(
        shards, mesh=grid, in_specs=placed, out_specs=P(replica, tensor), check_vma=False
    )
```

```python
import functools

import jax
import jax.numpy as jnp
from jax import lax
from jax.experimental import pallas as pl
from jax.experimental.pallas import tpu as pltpu
from jax.sharding import Mesh, PartitionSpec as P

Y, X, Z, C = 8, 4, 8, 2
T = Z * C
GROUPS = Y * X
LIMIT = 2
CODE_ROWS = 16
NT = (((1,), (1,)), ((), ()))


def spot():
    return lax.axis_index("y"), lax.axis_index("x")


def dispatch_kernel(plan, down, *refs):
    outs, (picked_out, held, staged, picked, in_sems, out_sems, picked_sem) = refs[:X], refs[X:]
    resident = down.shape[0]
    y, x = spot()
    pieces = in_sems.shape[0]
    part = resident // pieces

    def read(i):
        rows = pl.ds(i * part, part)
        return pltpu.make_async_copy(down.at[rows], held.at[rows], in_sems.at[i])

    def write(e):
        return pltpu.make_async_copy(staged.at[e], outs[e], out_sems.at[e])

    for i in range(pieces):
        read(i).start()
    table = plan[...]
    home = table // resident
    number = table - home * resident
    mine = (home == y * X + x).astype(jnp.int32)
    after = jnp.concatenate([jnp.zeros((mine.shape[0], 1), jnp.int32), mine[:, :-1]], axis=1)
    first = jnp.sum(mine * (1 - after) * number, axis=1, keepdims=True)
    second = jnp.sum(mine * after * number, axis=1, keepdims=True)
    lane = lax.broadcasted_iota(jnp.int32, picked_out.shape, 1)
    picked_out[...] = jnp.where(lane == 0, first, jnp.where(lane == 1, second, 0))
    to_scalars = pltpu.make_async_copy(picked_out, picked, picked_sem)
    to_scalars.start()
    to_scalars.wait()
    for i in range(pieces):
        read(i).wait()
    for e in range(X):
        column = lax.rem(x + e, X)
        for row in range(Y):
            for j in range(LIMIT):
                staged[e, row * LIMIT + j] = held[picked[row * X + column, j]]
        write(e).start()
    for e in range(X):
        write(e).wait()


def dispatch(plan, down):
    vmem = pl.BlockSpec(memory_space=pltpu.VMEM)
    hbm = pl.BlockSpec(memory_space=pl.ANY)
    shape = (Y * LIMIT,) + down.shape[1:]
    return pl.pallas_call(
        dispatch_kernel,
        out_shape=(jax.ShapeDtypeStruct(shape, down.dtype),) * X
        + (jax.ShapeDtypeStruct((GROUPS, 128), jnp.int32),),
        in_specs=[vmem, hbm],
        out_specs=(hbm,) * X + (vmem,),
        scratch_shapes=[
            pltpu.VMEM(down.shape, down.dtype),
            pltpu.VMEM((X,) + shape, down.dtype),
            pltpu.SMEM((GROUPS, 128), jnp.int32),
            pltpu.SemaphoreType.DMA((4,)),
            pltpu.SemaphoreType.DMA((X,)),
            pltpu.SemaphoreType.DMA,
        ],
        cost_estimate=pl.CostEstimate(flops=0, bytes_accessed=6 * down.size, transcendentals=0),
    )(plan, down)


def pick_up_kernel(picked, plan, slots, up, out, code_out):
    resident, rank, _ = up.shape
    y, x = spot()
    slot = slots[...]
    code = slot
    before = jnp.int32(-1)
    for k in range(plan.shape[1]):
        home = plan[y * X + x, k] // resident
        again = (home == before).astype(jnp.int32)
        code = jnp.where(slot == resident + k, resident + home * LIMIT + again, code)
        before = home
    code_out[...] = code
    lanes = out.shape[2]
    tail = [code[:, k * lanes : (k + 1) * lanes].astype(jnp.float32) for k in range(code.shape[1] // lanes)]
    tail.append(jnp.zeros((CODE_ROWS - len(tail), lanes), jnp.float32))
    tail = jnp.concatenate(tail, axis=0).astype(out.dtype)
    for group in range(GROUPS):
        for j in range(LIMIT):
            out[group, j * rank : (j + 1) * rank, :] = up[picked[group, j]]
        out[group, LIMIT * rank :, :] = tail


def pick_up(picked, plan, slots, up):
    smem = pl.BlockSpec(memory_space=pltpu.SMEM)
    vmem = pl.BlockSpec(memory_space=pltpu.VMEM)
    _, rank, width = up.shape
    return pl.pallas_call(
        pick_up_kernel,
        out_shape=(
            jax.ShapeDtypeStruct((GROUPS, LIMIT * rank + CODE_ROWS, width), up.dtype),
            jax.ShapeDtypeStruct(slots.shape, jnp.int32),
        ),
        in_specs=[smem, smem, vmem, vmem],
        out_specs=(vmem, vmem),
        cost_estimate=pl.CostEstimate(flops=0, bytes_accessed=6 * up.size, transcendentals=0),
    )(picked, plan, slots, up)


def local_kernel(code, rows, down, out):
    rank = out.shape[0]
    resident = down.shape[0] // rank
    total = jnp.zeros(out.shape, jnp.float32)
    step = 4
    for first in range(0, resident, step):
        product = lax.dot_general(
            down[first * rank : (first + step) * rank, :], rows[...], NT, preferred_element_type=jnp.float32
        )
        for k in range(step):
            total = total + jnp.where(code[...] == first + k, product[k * rank : (k + 1) * rank, :], 0.0)
    out[...] = total


def local_shrink(code, rows, down):
    resident, rank, width = down.shape
    vmem = pl.BlockSpec(memory_space=pltpu.VMEM)
    return pl.pallas_call(
        local_kernel,
        out_shape=jax.ShapeDtypeStruct((rank, rows.shape[0]), jnp.float32),
        in_specs=[vmem] * 3,
        out_specs=vmem,
        cost_estimate=pl.CostEstimate(
            flops=2 * rows.size * resident * rank, bytes_accessed=2 * down.size, transcendentals=0
        ),
    )(code, rows, down.reshape(resident * rank, width))


def imported_kernel(resident, rows, codes, *refs):
    down, (own, out, rows_held, codes_held, down_held, sems) = refs[:X], refs[X:]
    rank, count = own.shape
    lanes = out.shape[-1]
    y, x = spot()

    def reads(g):
        wanted = pl.ds(g * LIMIT * rank, LIMIT * rank)
        pairs = [(rows.at[pl.ds(g * count, count)], rows_held.at[g])]
        pairs.append((codes.at[g * X + x, pl.ds(LIMIT * rank, CODE_ROWS)], codes_held.at[g]))
        pairs += [(down[e].at[wanted], down_held.at[g, pl.ds(e * LIMIT * rank, LIMIT * rank)]) for e in range(X)]
        return [pltpu.make_async_copy(a, b, sems.at[g, i]) for i, (a, b) in enumerate(pairs)]

    for g in range(Y):
        for read in reads(g):
            read.start()
    for g in range(Y):
        for read in reads(g):
            read.wait()
        tail = codes_held[g].astype(jnp.float32)
        code = jnp.concatenate([tail[k : k + 1] for k in range(count // lanes)], axis=1)
        total = jnp.where(y == g, own[...], 0.0)
        product = lax.dot_general(down_held[g], rows_held[g], NT, preferred_element_type=jnp.float32)
        for e in range(X):
            home = y * X + lax.rem(x - e + X, X)
            for j in range(LIMIT):
                at = (e * LIMIT + j) * rank
                hit = code == (resident + home * LIMIT + j).astype(jnp.float32)
                total = total + jnp.where(hit, product[at : at + rank, :], 0.0)
        for i in range(rank // 8):
            for k in range(count // lanes):
                out[g, i * (count // lanes) + k] = total[i * 8 : (i + 1) * 8, k * lanes : (k + 1) * lanes]


def imported_shrink(resident, rows, codes, down, own):
    rank, count = own.shape
    width = rows.shape[-1]
    blocks = rank * count // 1024
    vmem = pl.BlockSpec(memory_space=pltpu.VMEM)
    hbm = pl.BlockSpec(memory_space=pl.ANY)
    return pl.pallas_call(
        functools.partial(imported_kernel, resident),
        out_shape=jax.ShapeDtypeStruct((Y, blocks, 8, 128), jnp.float32),
        in_specs=[hbm] * (2 + X) + [vmem],
        out_specs=vmem,
        scratch_shapes=[
            pltpu.VMEM((Y, count, width), rows.dtype),
            pltpu.VMEM((Y, CODE_ROWS, codes.shape[-1]), codes.dtype),
            pltpu.VMEM((Y, X * LIMIT * rank, width), rows.dtype),
            pltpu.SemaphoreType.DMA((Y, X + 2)),
        ],
        cost_estimate=pl.CostEstimate(
            flops=2 * X * down[0].size * count, bytes_accessed=2 * (X * down[0].size + rows.size), transcendentals=0
        ),
    )(rows, codes, *[part.reshape(-1, width) for part in down], own)


def add_kernel(parts, out):
    total = jnp.sum(parts[...], axis=0)
    for t in range(out.shape[0]):
        out[t] = total


def add_and_spread(parts):
    vmem = pl.BlockSpec(memory_space=pltpu.VMEM)
    return pl.pallas_call(
        add_kernel,
        out_shape=jax.ShapeDtypeStruct((T,) + parts.shape[1:], jnp.float32),
        in_specs=[vmem],
        out_specs=vmem,
    )(parts)


def expand_kernel(shrink, code, base, up, up_in, out):
    count = out.shape[0]
    lanes = count // 128
    rank = shrink.shape[0] // lanes * 8
    rows = jnp.concatenate(
        [jnp.concatenate([shrink[i * lanes + k] for k in range(lanes)], axis=1) for i in range(rank // 8)], axis=0
    )
    rows = jnp.transpose(rows)
    column = jnp.transpose(jnp.broadcast_to(code[...], (8, count)).astype(jnp.float32))[:, :1]
    pair = jnp.concatenate([rows, rows], axis=1)
    high = pair.astype(jnp.bfloat16).astype(jnp.float32)
    low = pair - high
    half = lax.broadcasted_iota(jnp.int32, pair.shape, 1) // rank
    wanted = jnp.broadcast_to(column, pair.shape) - half.astype(jnp.float32)
    both = jnp.concatenate([high, low], axis=0)
    wanted = jnp.concatenate([wanted, wanted], axis=0)
    total = jnp.zeros((2 * count, out.shape[1]), jnp.float32)
    step = 4
    pairs = [up[2 * p : 2 * p + 2].reshape(2 * rank, -1) for p in range(up.shape[0] // 2)]
    pairs += [up_in[p, : 2 * rank, :] for p in range(up_in.shape[0])]
    for first in range(0, len(pairs), step):
        placed = jnp.concatenate(
            [
                jnp.where(wanted == float(2 * p), both, 0.0).astype(jnp.bfloat16)
                for p in range(first, first + step)
            ],
            axis=1,
        )
        maps = jnp.concatenate(pairs[first : first + step], axis=0)
        total = total + jnp.dot(placed, maps, preferred_element_type=jnp.float32)
    out[...] = (base[...] + (total[:count] + total[count:])).astype(out.dtype)


def expand(shrink, code, base, up, up_in):
    vmem = pl.BlockSpec(memory_space=pltpu.VMEM)
    return pl.pallas_call(
        expand_kernel,
        out_shape=jax.ShapeDtypeStruct(base.shape, jnp.bfloat16),
        in_specs=[vmem] * 5,
        out_specs=vmem,
    )(shrink, code, base, up, up_in)


def shift(array, axis, size, by):
    return lax.ppermute(array, axis, [(i, (i + by) % size) for i in range(size)])


def shards(inputs, row_adapter_slot, transfer_plan, key_value_weight, adapter_down, adapter_up):
    count = inputs.shape[0]
    resident = adapter_down.shape[0]
    slots = row_adapter_slot.reshape(1, count)

    rows = lax.all_gather(inputs, "y", tiled=True)
    *down, picked = dispatch(transfer_plan, adapter_down)
    down = [down[0]] + [shift(down[e], "x", X, e) for e in range(1, X)]

    up_out, code = pick_up(picked, transfer_plan, slots, adapter_up)
    up_in = lax.all_to_all(up_out, ("y", "x"), 0, 0, tiled=True)

    base_part = jnp.dot(inputs, key_value_weight, preferred_element_type=jnp.float32)
    base = lax.psum_scatter(base_part, ("z", "c"), scatter_dimension=1, tiled=True)
    own = local_shrink(code, inputs, adapter_down)

    parts = imported_shrink(resident, rows, up_in, down, own)
    parts = lax.all_to_all(parts.reshape(Y * T, 8, 128), ("y", "z", "c"), 0, 0, tiled=True)
    shrink = lax.all_to_all(add_and_spread(parts), ("z", "c"), 0, 0, tiled=True)
    return expand(shrink, code, base, adapter_up, up_in)


def solution(mesh):
    grid = Mesh(mesh.devices.reshape(Y, X, Z, C), ("y", "x", "z", "c"))
    replica, tensor = ("y", "x"), ("z", "c")
    placed = (
        P(replica, tensor),
        P(replica),
        P(),
        P(tensor, None),
        P(replica, None, tensor),
        P(replica, None, tensor),
    )
    return jax.shard_map(
        shards, mesh=grid, in_specs=placed, out_specs=P(replica, tensor), check_vma=False
    )
```

```python
import functools

import jax
import jax.numpy as jnp
from jax import lax
from jax.experimental import pallas as pl
from jax.experimental.pallas import tpu as pltpu
from jax.sharding import Mesh, PartitionSpec as P

Y, X, Z, C = 8, 4, 8, 2
T = Z * C
GROUPS = Y * X
LIMIT = 2
CODE_ROWS = 16
NT = (((1,), (1,)), ((), ()))


def spot():
    return lax.axis_index("y"), lax.axis_index("x")


def dispatch_kernel(plan, down, up, *refs):
    outs, (held, held_up, staged, picked_rows, picked, in_sems, out_sems, picked_sem) = refs[:X], refs[X:]
    resident, _, width = down.shape
    y, x = spot()
    pieces = in_sems.shape[0] - 1
    part = resident // pieces

    def read(i):
        if i == pieces:
            return pltpu.make_async_copy(up, held_up, in_sems.at[i])
        rows = pl.ds(i * part, part)
        return pltpu.make_async_copy(down.at[rows], held.at[rows], in_sems.at[i])

    def write(e):
        return pltpu.make_async_copy(staged.at[e], outs[e], out_sems.at[e])

    for i in range(pieces + 1):
        read(i).start()
    table = plan[...]
    home = table // resident
    number = table - home * resident
    mine = (home == y * X + x).astype(jnp.int32)
    after = jnp.concatenate([jnp.zeros((mine.shape[0], 1), jnp.int32), mine[:, :-1]], axis=1)
    first = jnp.sum(mine * (1 - after) * number, axis=1, keepdims=True)
    second = jnp.sum(mine * after * number, axis=1, keepdims=True)
    lane = lax.broadcasted_iota(jnp.int32, picked_rows.shape, 1)
    picked_rows[...] = jnp.where(lane == 0, first, jnp.where(lane == 1, second, 0))
    to_scalars = pltpu.make_async_copy(picked_rows, picked, picked_sem)
    to_scalars.start()
    to_scalars.wait()
    for i in range(pieces + 1):
        read(i).wait()
    for e in range(X):
        column = lax.rem(x + e, X)
        for row in range(Y):
            for j in range(LIMIT):
                wanted = picked[row * X + column, j]
                staged[e, row * LIMIT + j, :, :width] = held[wanted]
                staged[e, row * LIMIT + j, :, width:] = held_up[wanted]
        write(e).start()
    for e in range(X):
        write(e).wait()


def dispatch(plan, down, up):
    vmem = pl.BlockSpec(memory_space=pltpu.VMEM)
    hbm = pl.BlockSpec(memory_space=pl.ANY)
    shape = (Y * LIMIT, down.shape[1], down.shape[2] + up.shape[2])
    return pl.pallas_call(
        dispatch_kernel,
        out_shape=(jax.ShapeDtypeStruct(shape, down.dtype),) * X,
        in_specs=[vmem, hbm, hbm],
        out_specs=(hbm,) * X,
        scratch_shapes=[
            pltpu.VMEM(down.shape, down.dtype),
            pltpu.VMEM(up.shape, up.dtype),
            pltpu.VMEM((X,) + shape, down.dtype),
            pltpu.VMEM((GROUPS, 128), jnp.int32),
            pltpu.SMEM((GROUPS, 128), jnp.int32),
            pltpu.SemaphoreType.DMA((5,)),
            pltpu.SemaphoreType.DMA((X,)),
            pltpu.SemaphoreType.DMA,
        ],
        cost_estimate=pl.CostEstimate(flops=0, bytes_accessed=6 * down.size, transcendentals=0),
    )(plan, down, up)


def prepare_kernel(resident, plan, slots, rows, out, code_out, sent, sems):
    y, x = spot()
    height, width = rows.shape
    slot = slots[...]
    code = slot
    before = jnp.int32(-1)
    for k in range(plan.shape[1]):
        home = plan[y * X + x, k] // resident
        again = (home == before).astype(jnp.int32)
        code = jnp.where(slot == resident + k, resident + home * LIMIT + again, code)
        before = home
    code_out[...] = code
    sent[0:height, :] = rows[...]
    wide = jnp.concatenate([code.astype(jnp.float32), jnp.zeros((1, width - height), jnp.float32)], axis=1)
    sent[height:, :] = jnp.broadcast_to(wide, (CODE_ROWS, width)).astype(sent.dtype)
    copies = [pltpu.make_async_copy(sent, out.at[i], sems.at[i]) for i in range(Y)]
    for copy in copies:
        copy.start()
    for copy in copies:
        copy.wait()


def prepare(resident, plan, slots, rows):
    height, width = rows.shape
    smem = pl.BlockSpec(memory_space=pltpu.SMEM)
    vmem = pl.BlockSpec(memory_space=pltpu.VMEM)
    return pl.pallas_call(
        functools.partial(prepare_kernel, resident),
        out_shape=(
            jax.ShapeDtypeStruct((Y, height + CODE_ROWS, width), rows.dtype),
            jax.ShapeDtypeStruct(slots.shape, jnp.int32),
        ),
        in_specs=[smem, vmem, vmem],
        out_specs=(pl.BlockSpec(memory_space=pl.ANY), vmem),
        scratch_shapes=[
            pltpu.VMEM((height + CODE_ROWS, width), rows.dtype),
            pltpu.SemaphoreType.DMA((Y,)),
        ],
        cost_estimate=pl.CostEstimate(flops=0, bytes_accessed=2 * Y * rows.size, transcendentals=0),
    )(plan, slots, rows)


def base_kernel(rows, weight, keep, give):
    product = jnp.dot(rows[...], weight[...], preferred_element_type=jnp.float32)
    width = keep.shape[-1]
    left, right = product[:, :width], product[:, width:]
    first = lax.axis_index("c") == 0
    keep[0] = jnp.where(first, left, right)
    give[0] = jnp.where(first, right, left)


def base_product(rows, weight):
    count, depth = rows.shape
    width = weight.shape[1] // T
    shape = jax.ShapeDtypeStruct((Z, count, width), jnp.float32)
    block = pl.BlockSpec((1, count, width), lambda i: (i, 0, 0))
    return pl.pallas_call(
        base_kernel,
        grid=(Z,),
        out_shape=(shape, shape),
        in_specs=[
            pl.BlockSpec((count, depth), lambda i: (0, 0)),
            pl.BlockSpec((depth, C * width), lambda i: (0, i)),
        ],
        out_specs=(block, block),
        cost_estimate=pl.CostEstimate(
            flops=2 * rows.size * weight.shape[1], bytes_accessed=2 * weight.size + 8 * Z * count * width, transcendentals=0
        ),
    )(rows, weight)


def halve_kernel(bit, mine, arrived, keep, give):
    half = keep.shape[0]
    side = lax.rem(lax.axis_index("z") // bit, 2)
    for i in range(half):
        at = side * half + i
        keep[i] = mine[at] + arrived[at]
        at = (1 - side) * half + i
        give[i] = mine[at] + arrived[at]


def halve(bit, mine, arrived):
    vmem = pl.BlockSpec(memory_space=pltpu.VMEM)
    shape = jax.ShapeDtypeStruct((mine.shape[0] // 2,) + mine.shape[1:], jnp.float32)
    return pl.pallas_call(
        functools.partial(halve_kernel, bit),
        out_shape=(shape, shape),
        in_specs=[vmem, vmem],
        out_specs=(vmem, vmem),
        cost_estimate=pl.CostEstimate(flops=mine.size, bytes_accessed=12 * mine.size, transcendentals=0),
    )(mine, arrived)


def turn_kernel(*refs):
    arrived, outs, (sems,) = refs[:X], refs[X:-1], refs[-1:]
    y, _ = spot()
    width = outs[0].shape[-1]
    copies = []
    for d in range(Y):
        row = lax.rem(y + d, Y)
        for e in range(X):
            source = arrived[e].at[pl.ds(row * LIMIT, LIMIT), :, pl.ds(arrived[e].shape[-1] - width, width)]
            target = outs[d].at[pl.ds(e * LIMIT, LIMIT)]
            copies.append(pltpu.make_async_copy(source, target, sems.at[d, e]))
    for copy in copies:
        copy.start()
    for copy in copies:
        copy.wait()


def turn(width, arrived):
    hbm = pl.BlockSpec(memory_space=pl.ANY)
    vmem = pl.BlockSpec(memory_space=pltpu.VMEM)
    shape = jax.ShapeDtypeStruct((X * LIMIT, arrived[0].shape[1], width), arrived[0].dtype)
    return pl.pallas_call(
        turn_kernel,
        out_shape=(shape,) * Y,
        in_specs=[hbm] * X,
        out_specs=(vmem,) * Y,
        scratch_shapes=[pltpu.SemaphoreType.DMA((Y, X))],
        cost_estimate=pl.CostEstimate(flops=0, bytes_accessed=4 * Y * shape.size, transcendentals=0),
    )(*arrived)


def local_kernel(code, rows, down, out):
    rank = out.shape[0]
    resident = down.shape[0] // rank
    total = jnp.zeros(out.shape, jnp.float32)
    step = 4
    for first in range(0, resident, step):
        product = lax.dot_general(
            down[first * rank : (first + step) * rank, :], rows[...], NT, preferred_element_type=jnp.float32
        )
        for k in range(step):
            total = total + jnp.where(code[...] == first + k, product[k * rank : (k + 1) * rank, :], 0.0)
    out[...] = total


def local_shrink(code, rows, down):
    resident, rank, width = down.shape
    vmem = pl.BlockSpec(memory_space=pltpu.VMEM)
    return pl.pallas_call(
        local_kernel,
        out_shape=jax.ShapeDtypeStruct((rank, rows.shape[0]), jnp.float32),
        in_specs=[vmem] * 3,
        out_specs=vmem,
        cost_estimate=pl.CostEstimate(
            flops=2 * rows.size * resident * rank, bytes_accessed=2 * down.size, transcendentals=0
        ),
    )(code, rows, down.reshape(resident * rank, width))


def imported_kernel(resident, rows, *refs):
    arrived, (own, out, rows_held, down_held, sems) = refs[:X], refs[X:]
    rank, count = own.shape
    lanes = out.shape[-1]
    width = rows.shape[-1]
    y, x = spot()

    def reads(g):
        wanted = pl.ds(g * LIMIT * rank, LIMIT * rank)
        pairs = [(rows.at[g], rows_held.at[g])]
        pairs += [
            (arrived[e].at[wanted, pl.ds(0, width)], down_held.at[g, pl.ds(e * LIMIT * rank, LIMIT * rank)])
            for e in range(X)
        ]
        return [pltpu.make_async_copy(a, b, sems.at[g, i]) for i, (a, b) in enumerate(pairs)]

    for g in range(Y):
        for read in reads(g):
            read.start()
    for g in range(Y):
        for read in reads(g):
            read.wait()
        code = rows_held[g, count : count + 1, :count].astype(jnp.float32)
        total = jnp.where(y == g, own[...], 0.0)
        product = lax.dot_general(
            down_held[g], rows_held[g, 0:count, :], NT, preferred_element_type=jnp.float32
        )
        for e in range(X):
            home = y * X + lax.rem(x - e + X, X)
            for j in range(LIMIT):
                at = (e * LIMIT + j) * rank
                hit = code == (resident + home * LIMIT + j).astype(jnp.float32)
                total = total + jnp.where(hit, product[at : at + rank, :], 0.0)
        for i in range(rank // 8):
            for k in range(count // lanes):
                out[g, i * (count // lanes) + k] = total[i * 8 : (i + 1) * 8, k * lanes : (k + 1) * lanes]


def imported_shrink(resident, rows, arrived, own):
    rank, count = own.shape
    height, width = rows.shape[1:]
    wide = arrived[0].shape[-1]
    blocks = rank * count // 1024
    vmem = pl.BlockSpec(memory_space=pltpu.VMEM)
    hbm = pl.BlockSpec(memory_space=pl.ANY)
    return pl.pallas_call(
        functools.partial(imported_kernel, resident),
        out_shape=jax.ShapeDtypeStruct((Y, blocks, 8, 128), jnp.float32),
        in_specs=[hbm] * (1 + X) + [vmem],
        out_specs=vmem,
        scratch_shapes=[
            pltpu.VMEM((Y, height, width), rows.dtype),
            pltpu.VMEM((Y, X * LIMIT * rank, width), rows.dtype),
            pltpu.SemaphoreType.DMA((Y, X + 1)),
        ],
        cost_estimate=pl.CostEstimate(
            flops=2 * X * arrived[0].size * count,
            bytes_accessed=2 * (X * arrived[0].size + rows.size),
            transcendentals=0,
        ),
    )(rows, *[part.reshape(-1, wide) for part in arrived], own)


def add_kernel(parts, out):
    total = jnp.sum(parts[...], axis=0)
    for t in range(out.shape[0]):
        out[t] = total


def add_and_spread(parts):
    vmem = pl.BlockSpec(memory_space=pltpu.VMEM)
    return pl.pallas_call(
        add_kernel,
        out_shape=jax.ShapeDtypeStruct((T,) + parts.shape[1:], jnp.float32),
        in_specs=[vmem],
        out_specs=vmem,
    )(parts)


def expand_kernel(shrink, code, mine, arrived, up, *refs):
    tables, out = refs[:-1], refs[-1]
    count = out.shape[0]
    lanes = count // 128
    rank = shrink.shape[0] // lanes * 8
    resident = up.shape[0]
    y, x = spot()
    imported = code[...] - resident
    home = imported // LIMIT
    d = (y - home // X + Y) % Y
    e = (x - home % X + X) % X
    at = jnp.where(imported < 0, code[...], resident + (d * X + e) * LIMIT + imported % LIMIT)
    rows = jnp.concatenate(
        [jnp.concatenate([shrink[i * lanes + k] for k in range(lanes)], axis=1) for i in range(rank // 8)], axis=0
    )
    rows = jnp.transpose(rows)
    column = jnp.transpose(jnp.broadcast_to(at, (8, count)).astype(jnp.float32))[:, :1]
    pair = jnp.concatenate([rows, rows], axis=1)
    high = pair.astype(jnp.bfloat16).astype(jnp.float32)
    low = pair - high
    half = lax.broadcasted_iota(jnp.int32, pair.shape, 1) // rank
    wanted = jnp.broadcast_to(column, pair.shape) - half.astype(jnp.float32)
    both = jnp.concatenate([high, low], axis=0)
    wanted = jnp.concatenate([wanted, wanted], axis=0)
    total = jnp.zeros((2 * count, out.shape[1]), jnp.float32)
    step = 4
    start = 0
    for table in (up,) + tables:
        for first in range(0, table.shape[0] // 2, step):
            placed = jnp.concatenate(
                [
                    jnp.where(wanted == float(start + 2 * p), both, 0.0).astype(jnp.bfloat16)
                    for p in range(first, first + step)
                ],
                axis=1,
            )
            maps = table[2 * first : 2 * (first + step)].reshape(2 * step * rank, out.shape[1])
            total = total + jnp.dot(placed, maps, preferred_element_type=jnp.float32)
        start += table.shape[0]
    base = mine[0] + arrived[0]
    out[...] = (base + (total[:count] + total[count:])).astype(out.dtype)


def expand(shrink, code, mine, arrived, up, tables):
    vmem = pl.BlockSpec(memory_space=pltpu.VMEM)
    return pl.pallas_call(
        expand_kernel,
        out_shape=jax.ShapeDtypeStruct(mine.shape[1:], jnp.bfloat16),
        in_specs=[vmem] * (5 + len(tables)),
        out_specs=vmem,
    )(shrink, code, mine, arrived, up, *tables)


def shift(array, axis, size, by):
    return lax.ppermute(array, axis, [(i, (i + by) % size) for i in range(size)])


def swap(array, axis, size, bit):
    return lax.ppermute(array, axis, [(i, i ^ bit) for i in range(size)])


def shards(inputs, row_adapter_slot, transfer_plan, key_value_weight, adapter_down, adapter_up):
    count = inputs.shape[0]
    resident = adapter_down.shape[0]
    slots = row_adapter_slot.reshape(1, count)

    arrived = dispatch(transfer_plan, adapter_down, adapter_up)
    arrived = [arrived[0]] + [shift(arrived[e], "x", X, e) for e in range(1, X)]
    sent, code = prepare(resident, transfer_plan, slots, inputs)
    rows = lax.all_to_all(sent, "y", 0, 0, tiled=True)

    keep, give = base_product(inputs, key_value_weight)
    other = swap(give, "c", C, 1)
    for bit in (4, 2, 1):
        keep, give = halve(bit, keep, other)
        other = swap(give, "z", Z, bit)

    own = local_shrink(code, inputs, adapter_down)
    parts = imported_shrink(resident, rows, arrived, own)
    parts = lax.all_to_all(parts.reshape(Y * T, 8, 128), ("y", "z", "c"), 0, 0, tiled=True)

    ups = turn(adapter_up.shape[-1], arrived)
    tables = [ups[0]] + [shift(ups[d], "y", Y, d) for d in range(1, Y)]
    shrink = lax.all_to_all(add_and_spread(parts), ("z", "c"), 0, 0, tiled=True)
    return expand(shrink, code, keep, other, adapter_up, tables)


def solution(mesh):
    grid = Mesh(mesh.devices.reshape(Y, X, Z, C), ("y", "x", "z", "c"))
    replica, tensor = ("y", "x"), ("z", "c")
    placed = (
        P(replica, tensor),
        P(replica),
        P(),
        P(tensor, None),
        P(replica, None, tensor),
        P(replica, None, tensor),
    )
    return jax.shard_map(
        shards, mesh=grid, in_specs=placed, out_specs=P(replica, tensor), check_vma=False
    )
```

```python
import functools

import jax
import jax.numpy as jnp
from jax import lax
from jax.experimental import pallas as pl
from jax.experimental.pallas import tpu as pltpu
from jax.sharding import Mesh, PartitionSpec as P

Y, X, Z, C = 8, 4, 8, 2
T = Z * C
GROUPS = Y * X
LIMIT = 2
CODE_ROWS = 16
MIB = 1024 * 1024
NT = (((1,), (1,)), ((), ()))


def spot():
    return lax.axis_index("y"), lax.axis_index("x")


def dispatch_kernel(plan, down, *refs):
    outs, (picked_out, held, staged, picked, in_sems, out_sems, picked_sem) = refs[:X], refs[X:]
    resident = down.shape[0]
    y, x = spot()
    pieces = in_sems.shape[0]
    part = resident // pieces

    def read(i):
        rows = pl.ds(i * part, part)
        return pltpu.make_async_copy(down.at[rows], held.at[rows], in_sems.at[i])

    def write(e):
        return pltpu.make_async_copy(staged.at[e], outs[e], out_sems.at[e])

    for i in range(pieces):
        read(i).start()
    table = plan[...]
    home = table // resident
    number = table - home * resident
    mine = (home == y * X + x).astype(jnp.int32)
    after = jnp.concatenate([jnp.zeros((mine.shape[0], 1), jnp.int32), mine[:, :-1]], axis=1)
    first = jnp.sum(mine * (1 - after) * number, axis=1, keepdims=True)
    second = jnp.sum(mine * after * number, axis=1, keepdims=True)
    lane = lax.broadcasted_iota(jnp.int32, picked_out.shape, 1)
    picked_out[...] = jnp.where(lane == 0, first, jnp.where(lane == 1, second, 0))
    to_scalars = pltpu.make_async_copy(picked_out, picked, picked_sem)
    to_scalars.start()
    to_scalars.wait()
    for i in range(pieces):
        read(i).wait()
    for e in range(X):
        column = lax.rem(x + e, X)
        for row in range(Y):
            for j in range(LIMIT):
                staged[e, row * LIMIT + j] = held[picked[row * X + column, j]]
        write(e).start()
    for e in range(X):
        write(e).wait()


def dispatch(plan, down):
    vmem = pl.BlockSpec(memory_space=pltpu.VMEM)
    hbm = pl.BlockSpec(memory_space=pl.ANY)
    shape = (Y * LIMIT,) + down.shape[1:]
    return pl.pallas_call(
        dispatch_kernel,
        out_shape=(jax.ShapeDtypeStruct(shape, down.dtype),) * X
        + (jax.ShapeDtypeStruct((GROUPS, 128), jnp.int32),),
        in_specs=[vmem, hbm],
        out_specs=(hbm,) * X + (vmem,),
        scratch_shapes=[
            pltpu.VMEM(down.shape, down.dtype),
            pltpu.VMEM((X,) + shape, down.dtype),
            pltpu.SMEM((GROUPS, 128), jnp.int32),
            pltpu.SemaphoreType.DMA((4,)),
            pltpu.SemaphoreType.DMA((X,)),
            pltpu.SemaphoreType.DMA,
        ],
        cost_estimate=pl.CostEstimate(flops=0, bytes_accessed=6 * down.size, transcendentals=0),
    )(plan, down)


def prepare_kernel(resident, plan, slots, rows, out, code_out):
    y, x = spot()
    height, width = rows.shape
    slot = slots[...]
    code = slot
    before = jnp.int32(-1)
    for k in range(plan.shape[1]):
        home = plan[y * X + x, k] // resident
        again = (home == before).astype(jnp.int32)
        code = jnp.where(slot == resident + k, resident + home * LIMIT + again, code)
        before = home
    code_out[...] = code
    out[0:height, :] = rows[...]
    wide = jnp.concatenate([code.astype(jnp.float32), jnp.zeros((1, width - height), jnp.float32)], axis=1)
    out[height:, :] = jnp.broadcast_to(wide, (CODE_ROWS, width)).astype(out.dtype)


def prepare(resident, plan, slots, rows):
    height, width = rows.shape
    smem = pl.BlockSpec(memory_space=pltpu.SMEM)
    vmem = pl.BlockSpec(memory_space=pltpu.VMEM)
    return pl.pallas_call(
        functools.partial(prepare_kernel, resident),
        out_shape=(
            jax.ShapeDtypeStruct((height + CODE_ROWS, width), rows.dtype),
            jax.ShapeDtypeStruct(slots.shape, jnp.int32),
        ),
        in_specs=[smem, vmem, vmem],
        out_specs=(vmem, vmem),
        cost_estimate=pl.CostEstimate(flops=0, bytes_accessed=4 * rows.size, transcendentals=0),
    )(plan, slots, rows)


def pick_up_kernel(picked, up, out):
    for group in range(GROUPS):
        for j in range(LIMIT):
            out[group * LIMIT + j] = up[picked[group, j]]


def pick_up(picked, up):
    smem = pl.BlockSpec(memory_space=pltpu.SMEM)
    vmem = pl.BlockSpec(memory_space=pltpu.VMEM)
    return pl.pallas_call(
        pick_up_kernel,
        out_shape=jax.ShapeDtypeStruct((GROUPS * LIMIT,) + up.shape[1:], up.dtype),
        in_specs=[smem, vmem],
        out_specs=vmem,
        cost_estimate=pl.CostEstimate(flops=0, bytes_accessed=6 * up.size, transcendentals=0),
    )(picked, up)


def base_kernel(rows, weight, out):
    out[...] = jnp.dot(rows[...], weight[...], preferred_element_type=jnp.float32)


def base_product(rows, weight):
    count, depth = rows.shape
    width = weight.shape[1]
    step = 512
    return pl.pallas_call(
        base_kernel,
        grid=(width // step,),
        out_shape=jax.ShapeDtypeStruct((count, width), jnp.float32),
        in_specs=[
            pl.BlockSpec((count, depth), lambda i: (0, 0)),
            pl.BlockSpec((depth, step), lambda i: (0, i)),
        ],
        out_specs=pl.BlockSpec((count, step), lambda i: (0, i)),
        cost_estimate=pl.CostEstimate(
            flops=2 * rows.size * width, bytes_accessed=2 * weight.size + 4 * count * width, transcendentals=0
        ),
    )(rows, weight)


def turn_kernel(arrived, *refs):
    outs, (held, sem) = refs[:X], refs[X:]
    _, x = spot()
    copy = pltpu.make_async_copy(arrived, held, sem)
    copy.start()
    copy.wait()
    for e in range(X):
        column = lax.rem(x + e, X)
        for row in range(Y):
            for j in range(LIMIT):
                outs[e][row * LIMIT + j] = held[(row * X + column) * LIMIT + j]


def turn(arrived):
    vmem = pl.BlockSpec(memory_space=pltpu.VMEM)
    return pl.pallas_call(
        turn_kernel,
        out_shape=(jax.ShapeDtypeStruct((Y * LIMIT,) + arrived.shape[1:], arrived.dtype),) * X,
        in_specs=[pl.BlockSpec(memory_space=pltpu.HBM)],
        out_specs=(vmem,) * X,
        scratch_shapes=[pltpu.VMEM(arrived.shape, arrived.dtype), pltpu.SemaphoreType.DMA],
        cost_estimate=pl.CostEstimate(flops=0, bytes_accessed=4 * arrived.size, transcendentals=0),
    )(arrived)


def local_kernel(code, rows, down, out):
    rank = out.shape[0]
    resident = down.shape[0] // rank
    total = jnp.zeros(out.shape, jnp.float32)
    step = 4
    for first in range(0, resident, step):
        product = lax.dot_general(
            down[first * rank : (first + step) * rank, :], rows[...], NT, preferred_element_type=jnp.float32
        )
        for k in range(step):
            total = total + jnp.where(code[...] == first + k, product[k * rank : (k + 1) * rank, :], 0.0)
    out[...] = total


def local_shrink(code, rows, down):
    resident, rank, width = down.shape
    vmem = pl.BlockSpec(memory_space=pltpu.VMEM)
    return pl.pallas_call(
        local_kernel,
        out_shape=jax.ShapeDtypeStruct((rank, rows.shape[0]), jnp.float32),
        in_specs=[vmem] * 3,
        out_specs=vmem,
        cost_estimate=pl.CostEstimate(
            flops=2 * rows.size * resident * rank, bytes_accessed=2 * down.size, transcendentals=0
        ),
    )(code, rows, down.reshape(resident * rank, width))


def imported_kernel(resident, rows, *refs):
    down, (own, out, rows_held, down_held, sems) = refs[:X], refs[X:]
    rank, count = own.shape
    lanes = out.shape[-1]
    y, x = spot()

    def reads(g):
        wanted = pl.ds(g * LIMIT * rank, LIMIT * rank)
        pairs = [(rows.at[g], rows_held.at[g])]
        pairs += [(down[e].at[wanted], down_held.at[g, pl.ds(e * LIMIT * rank, LIMIT * rank)]) for e in range(X)]
        return [pltpu.make_async_copy(a, b, sems.at[g, i]) for i, (a, b) in enumerate(pairs)]

    for g in range(Y):
        for read in reads(g):
            read.start()
    for g in range(Y):
        for read in reads(g):
            read.wait()
        code = rows_held[g, count : count + 1, :count].astype(jnp.float32)
        total = jnp.where(y == g, own[...], 0.0)
        product = lax.dot_general(
            down_held[g], rows_held[g, 0:count, :], NT, preferred_element_type=jnp.float32
        )
        for e in range(X):
            home = y * X + lax.rem(x - e + X, X)
            for j in range(LIMIT):
                at = (e * LIMIT + j) * rank
                hit = code == (resident + home * LIMIT + j).astype(jnp.float32)
                total = total + jnp.where(hit, product[at : at + rank, :], 0.0)
        for i in range(rank // 8):
            for k in range(count // lanes):
                out[g, i * (count // lanes) + k] = total[i * 8 : (i + 1) * 8, k * lanes : (k + 1) * lanes]


def imported_shrink(resident, rows, down, own):
    rank, count = own.shape
    height, width = rows.shape[1:]
    blocks = rank * count // 1024
    vmem = pl.BlockSpec(memory_space=pltpu.VMEM)
    hbm = pl.BlockSpec(memory_space=pltpu.HBM)
    return pl.pallas_call(
        functools.partial(imported_kernel, resident),
        out_shape=jax.ShapeDtypeStruct((Y, blocks, 8, 128), jnp.float32),
        in_specs=[hbm] * (1 + X) + [vmem],
        out_specs=vmem,
        scratch_shapes=[
            pltpu.VMEM((Y, height, width), rows.dtype),
            pltpu.VMEM((Y, X * LIMIT * rank, width), rows.dtype),
            pltpu.SemaphoreType.DMA((Y, X + 1)),
        ],
        cost_estimate=pl.CostEstimate(
            flops=2 * X * down[0].size * count,
            bytes_accessed=2 * (X * down[0].size + rows.size),
            transcendentals=0,
        ),
    )(rows, *[part.reshape(-1, width) for part in down], own)


def add_kernel(parts, out):
    total = jnp.sum(parts[...], axis=0)
    for t in range(out.shape[0]):
        out[t] = total


def add_and_spread(parts):
    vmem = pl.BlockSpec(memory_space=pltpu.VMEM)
    return pl.pallas_call(
        add_kernel,
        out_shape=jax.ShapeDtypeStruct((T,) + parts.shape[1:], jnp.float32),
        in_specs=[vmem],
        out_specs=vmem,
        compiler_params=pltpu.CompilerParams(vmem_limit_bytes=2 * MIB),
    )(parts)


def expand_kernel(shrink, code, base, up, *refs):
    tables, (out, held, base_held, sems) = refs[:X], refs[X:]
    count = out.shape[0]
    lanes = count // 128
    rank = shrink.shape[0] // lanes * 8
    resident, imported_each = up.shape[0], tables[0].shape[0]
    copies = [pltpu.make_async_copy(up, held.at[pl.ds(0, resident)], sems.at[0])]
    for e in range(X):
        place = pl.ds(resident + e * imported_each, imported_each)
        copies.append(pltpu.make_async_copy(tables[e], held.at[place], sems.at[1 + e]))
    copies.append(pltpu.make_async_copy(base, base_held, sems.at[1 + X]))
    for copy in copies:
        copy.start()
    rows = jnp.concatenate(
        [jnp.concatenate([shrink[i * lanes + k] for k in range(lanes)], axis=1) for i in range(rank // 8)], axis=0
    )
    rows = jnp.transpose(rows)
    _, x = spot()
    imported = code[...] - resident
    home = imported // LIMIT
    e = (x - home % X + X) % X
    at = jnp.where(imported < 0, code[...], resident + (e * Y + home // X) * LIMIT + imported % LIMIT)
    column = jnp.transpose(jnp.broadcast_to(at, (8, count)).astype(jnp.float32))[:, :1]
    pair = jnp.concatenate([rows, rows], axis=1)
    high = pair.astype(jnp.bfloat16).astype(jnp.float32)
    low = pair - high
    half = lax.broadcasted_iota(jnp.int32, pair.shape, 1) // rank
    wanted = jnp.broadcast_to(column, pair.shape) - half.astype(jnp.float32)
    both = jnp.concatenate([high, low], axis=0)
    wanted = jnp.concatenate([wanted, wanted], axis=0)
    total = jnp.zeros((2 * count, out.shape[1]), jnp.float32)
    step = 4
    bounds = [resident + e * imported_each for e in range(X + 1)]
    for first in range(0, held.shape[0] // 2, step):
        if first == 0:
            copies[0].wait()
        if 2 * first in bounds:
            copies[1 + bounds.index(2 * first)].wait()
        placed = jnp.concatenate(
            [
                jnp.where(wanted == float(2 * p), both, 0.0).astype(jnp.bfloat16)
                for p in range(first, first + step)
            ],
            axis=1,
        )
        maps = held[2 * first : 2 * (first + step)].reshape(2 * step * rank, out.shape[1])
        total = total + jnp.dot(placed, maps, preferred_element_type=jnp.float32)
    copies[-1].wait()
    out[...] = (base_held[...] + (total[:count] + total[count:])).astype(out.dtype)


def expand(shrink, code, base, up, tables):
    vmem = pl.BlockSpec(memory_space=pltpu.VMEM)
    hbm = pl.BlockSpec(memory_space=pltpu.HBM)
    maps = up.shape[0] + X * tables[0].shape[0]
    return pl.pallas_call(
        expand_kernel,
        out_shape=jax.ShapeDtypeStruct(base.shape, jnp.bfloat16),
        in_specs=[vmem, vmem] + [hbm] * (2 + X),
        out_specs=vmem,
        scratch_shapes=[
            pltpu.VMEM((maps,) + up.shape[1:], up.dtype),
            pltpu.VMEM(base.shape, base.dtype),
            pltpu.SemaphoreType.DMA((2 + X,)),
        ],
        compiler_params=pltpu.CompilerParams(vmem_limit_bytes=12 * MIB),
    )(shrink, code, base, up, *tables)


def shift(array, axis, size, by):
    return lax.ppermute(array, axis, [(i, (i + by) % size) for i in range(size)])


def shards(inputs, row_adapter_slot, transfer_plan, key_value_weight, adapter_down, adapter_up):
    count = inputs.shape[0]
    resident = adapter_down.shape[0]
    slots = row_adapter_slot.reshape(1, count)

    sent, code = prepare(resident, transfer_plan, slots, inputs)
    rows = lax.all_gather(sent, "y")
    *down, picked = dispatch(transfer_plan, adapter_down)
    down = [down[0]] + [shift(down[e], "x", X, e) for e in range(1, X)]

    ups = turn(lax.all_to_all(pick_up(picked, adapter_up), "y", 0, 0, tiled=True))
    tables = [ups[0]] + [shift(ups[e], "x", X, e) for e in range(1, X)]

    late, picked = lax.optimization_barrier((inputs, picked))
    base_part = base_product(late, key_value_weight)
    base = lax.psum_scatter(base_part, ("z", "c"), scatter_dimension=1, tiled=True)
    own = local_shrink(code, late, adapter_down)

    parts = imported_shrink(resident, rows, down, own)
    parts = lax.all_to_all(parts.reshape(Y * T, 8, 128), ("y", "z", "c"), 0, 0, tiled=True)
    shrink = lax.all_to_all(add_and_spread(parts), ("z", "c"), 0, 0, tiled=True)
    return expand(shrink, code, base, adapter_up, tables)


def solution(mesh):
    grid = Mesh(mesh.devices.reshape(Y, X, Z, C), ("y", "x", "z", "c"))
    replica, tensor = ("y", "x"), ("z", "c")
    placed = (
        P(replica, tensor),
        P(replica),
        P(),
        P(tensor, None),
        P(replica, None, tensor),
        P(replica, None, tensor),
    )
    return jax.shard_map(
        shards, mesh=grid, in_specs=placed, out_specs=P(replica, tensor), check_vma=False
    )
```

```python
import functools

import jax
import jax.numpy as jnp
from jax import lax
from jax.experimental import pallas as pl
from jax.experimental.pallas import tpu as pltpu
from jax.sharding import Mesh, PartitionSpec as P

Y, X, Z, C = 8, 4, 8, 2
T = Z * C
GROUPS = Y * X
LIMIT = 2
CODE_ROWS = 16
MIB = 1024 * 1024
NT = (((1,), (1,)), ((), ()))


def spot():
    return lax.axis_index("y"), lax.axis_index("x")


def dispatch_kernel(plan, down, *refs):
    out, picked_out, held, staged, picked, in_sems, out_sems, picked_sem = refs
    resident = down.shape[0]
    y, x = spot()
    pieces = in_sems.shape[0]
    part = resident // pieces

    def read(i):
        rows = pl.ds(i * part, part)
        return pltpu.make_async_copy(down.at[rows], held.at[rows], in_sems.at[i])

    def write(e):
        return pltpu.make_async_copy(staged.at[e], out.at[e], out_sems.at[e])

    for i in range(pieces):
        read(i).start()
    table = plan[...]
    home = table // resident
    number = table - home * resident
    mine = (home == y * X + x).astype(jnp.int32)
    after = jnp.concatenate([jnp.zeros((mine.shape[0], 1), jnp.int32), mine[:, :-1]], axis=1)
    first = jnp.sum(mine * (1 - after) * number, axis=1, keepdims=True)
    second = jnp.sum(mine * after * number, axis=1, keepdims=True)
    lane = lax.broadcasted_iota(jnp.int32, picked_out.shape, 1)
    picked_out[...] = jnp.where(lane == 0, first, jnp.where(lane == 1, second, 0))
    to_scalars = pltpu.make_async_copy(picked_out, picked, picked_sem)
    to_scalars.start()
    to_scalars.wait()
    for i in range(pieces):
        read(i).wait()
    for e in range(X):
        for row in range(Y):
            for j in range(LIMIT):
                staged[e, row * LIMIT + j] = held[picked[row * X + e, j]]
        write(e).start()
    for e in range(X):
        write(e).wait()


def dispatch(plan, down):
    vmem = pl.BlockSpec(memory_space=pltpu.VMEM)
    hbm = pl.BlockSpec(memory_space=pl.ANY)
    shape = (X, Y * LIMIT) + down.shape[1:]
    return pl.pallas_call(
        dispatch_kernel,
        out_shape=(
            jax.ShapeDtypeStruct(shape, down.dtype),
            jax.ShapeDtypeStruct((GROUPS, 128), jnp.int32),
        ),
        in_specs=[vmem, hbm],
        out_specs=(hbm, vmem),
        scratch_shapes=[
            pltpu.VMEM(down.shape, down.dtype),
            pltpu.VMEM(shape, down.dtype),
            pltpu.SMEM((GROUPS, 128), jnp.int32),
            pltpu.SemaphoreType.DMA((4,)),
            pltpu.SemaphoreType.DMA((X,)),
            pltpu.SemaphoreType.DMA,
        ],
        cost_estimate=pl.CostEstimate(flops=0, bytes_accessed=6 * down.size, transcendentals=0),
    )(plan, down)


def prepare_kernel(resident, plan, slots, rows, out, code_out):
    y, x = spot()
    height, width = rows.shape
    slot = slots[...]
    code = slot
    before = jnp.int32(-1)
    for k in range(plan.shape[1]):
        home = plan[y * X + x, k] // resident
        again = (home == before).astype(jnp.int32)
        code = jnp.where(slot == resident + k, resident + home * LIMIT + again, code)
        before = home
    code_out[...] = code
    out[0:height, :] = rows[...]
    wide = jnp.concatenate([code.astype(jnp.float32), jnp.zeros((1, width - height), jnp.float32)], axis=1)
    out[height:, :] = jnp.broadcast_to(wide, (CODE_ROWS, width)).astype(out.dtype)


def prepare(resident, plan, slots, rows):
    height, width = rows.shape
    smem = pl.BlockSpec(memory_space=pltpu.SMEM)
    vmem = pl.BlockSpec(memory_space=pltpu.VMEM)
    return pl.pallas_call(
        functools.partial(prepare_kernel, resident),
        out_shape=(
            jax.ShapeDtypeStruct((height + CODE_ROWS, width), rows.dtype),
            jax.ShapeDtypeStruct(slots.shape, jnp.int32),
        ),
        in_specs=[smem, vmem, vmem],
        out_specs=(vmem, vmem),
        cost_estimate=pl.CostEstimate(flops=0, bytes_accessed=4 * rows.size, transcendentals=0),
    )(plan, slots, rows)


def pick_up_kernel(picked, up, *outs):
    y, _ = spot()
    for d in range(Y):
        row = lax.rem(y + d, Y)
        for x in range(X):
            for j in range(LIMIT):
                outs[d][x * LIMIT + j] = up[picked[row * X + x, j]]


def pick_up(picked, up):
    smem = pl.BlockSpec(memory_space=pltpu.SMEM)
    vmem = pl.BlockSpec(memory_space=pltpu.VMEM)
    return pl.pallas_call(
        pick_up_kernel,
        out_shape=(jax.ShapeDtypeStruct((X * LIMIT,) + up.shape[1:], up.dtype),) * Y,
        in_specs=[smem, vmem],
        out_specs=(vmem,) * Y,
        cost_estimate=pl.CostEstimate(flops=0, bytes_accessed=6 * up.size, transcendentals=0),
    )(picked, up)


def turn_kernel(*refs):
    arrived, outs = refs[:Y], refs[Y:]
    _, x = spot()
    for e in range(X):
        column = lax.rem(x + e, X)
        for d in range(Y):
            for j in range(LIMIT):
                outs[e][d * LIMIT + j] = arrived[d][column * LIMIT + j]


def turn(arrived):
    vmem = pl.BlockSpec(memory_space=pltpu.VMEM)
    shape = jax.ShapeDtypeStruct((Y * LIMIT,) + arrived[0].shape[1:], arrived[0].dtype)
    return pl.pallas_call(
        turn_kernel,
        out_shape=(shape,) * X,
        in_specs=[vmem] * Y,
        out_specs=(vmem,) * X,
        compiler_params=pltpu.CompilerParams(vmem_limit_bytes=6 * MIB),
        cost_estimate=pl.CostEstimate(flops=0, bytes_accessed=4 * Y * arrived[0].size, transcendentals=0),
    )(*arrived)


def local_kernel(code, rows, down, out):
    rank = out.shape[0]
    resident = down.shape[0] // rank
    total = jnp.zeros(out.shape, jnp.float32)
    step = 4
    for first in range(0, resident, step):
        product = lax.dot_general(
            down[first * rank : (first + step) * rank, :], rows[...], NT, preferred_element_type=jnp.float32
        )
        for k in range(step):
            total = total + jnp.where(code[...] == first + k, product[k * rank : (k + 1) * rank, :], 0.0)
    out[...] = total


def local_shrink(code, rows, down):
    resident, rank, width = down.shape
    vmem = pl.BlockSpec(memory_space=pltpu.VMEM)
    return pl.pallas_call(
        local_kernel,
        out_shape=jax.ShapeDtypeStruct((rank, rows.shape[0]), jnp.float32),
        in_specs=[vmem] * 3,
        out_specs=vmem,
        cost_estimate=pl.CostEstimate(
            flops=2 * rows.size * resident * rank, bytes_accessed=2 * down.size, transcendentals=0
        ),
    )(code, rows, down.reshape(resident * rank, width))


def imported_kernel(resident, rows, down, own, out, rows_held, down_held, sems):
    rank, count = own.shape
    lanes = out.shape[-1]
    y, _ = spot()
    odd = lax.axis_index("c")

    def reads(g):
        wanted = pl.ds(g * LIMIT * rank, LIMIT * rank)
        at = g + odd * (Y - 1 - 2 * g)
        pairs = [(rows.at[at], rows_held.at[g])]
        pairs += [(down.at[x, wanted], down_held.at[g, pl.ds(x * LIMIT * rank, LIMIT * rank)]) for x in range(X)]
        return [pltpu.make_async_copy(a, b, sems.at[g, i]) for i, (a, b) in enumerate(pairs)]

    for g in range(Y):
        for read in reads(g):
            read.start()
    base = (resident + y * X * LIMIT).astype(jnp.float32)
    for g in range(Y):
        for read in reads(g):
            read.wait()
        code = rows_held[g, count : count + 1, :count].astype(jnp.float32)
        total = jnp.where(y == g, own[...], 0.0)
        product = lax.dot_general(
            down_held[g], rows_held[g, 0:count, :], NT, preferred_element_type=jnp.float32
        )
        for k in range(X * LIMIT):
            total = total + jnp.where(code == base + k, product[k * rank : (k + 1) * rank, :], 0.0)
        for i in range(rank // 8):
            for k in range(count // lanes):
                out[g, i * (count // lanes) + k] = total[i * 8 : (i + 1) * 8, k * lanes : (k + 1) * lanes]


def imported_shrink(resident, rows, down, own):
    rank, count = own.shape
    height, width = rows.shape[1:]
    blocks = rank * count // 1024
    vmem = pl.BlockSpec(memory_space=pltpu.VMEM)
    hbm = pl.BlockSpec(memory_space=pl.ANY)
    return pl.pallas_call(
        functools.partial(imported_kernel, resident),
        out_shape=jax.ShapeDtypeStruct((Y, blocks, 8, 128), jnp.float32),
        in_specs=[hbm, hbm, vmem],
        out_specs=vmem,
        scratch_shapes=[
            pltpu.VMEM((Y, height, width), rows.dtype),
            pltpu.VMEM((Y, X * LIMIT * rank, width), rows.dtype),
            pltpu.SemaphoreType.DMA((Y, X + 1)),
        ],
        cost_estimate=pl.CostEstimate(
            flops=2 * down.size * count, bytes_accessed=2 * (down.size + rows.size), transcendentals=0
        ),
    )(rows, down.reshape(X, -1, width), own)


def add_kernel(parts, out):
    total = jnp.sum(parts[...], axis=0)
    for t in range(out.shape[0]):
        out[t] = total


def add_and_spread(parts):
    vmem = pl.BlockSpec(memory_space=pltpu.VMEM)
    return pl.pallas_call(
        add_kernel,
        out_shape=jax.ShapeDtypeStruct((T,) + parts.shape[1:], jnp.float32),
        in_specs=[vmem],
        out_specs=vmem,
        compiler_params=pltpu.CompilerParams(vmem_limit_bytes=2 * MIB),
    )(parts)


def expand_kernel(shrink, code, base, up, *refs):
    tables, (out, held, base_held, sems) = refs[:X], refs[X:]
    count = out.shape[0]
    lanes = count // 128
    rank = shrink.shape[0] // lanes * 8
    resident, imported_each = up.shape[0], tables[0].shape[0]
    copies = [pltpu.make_async_copy(up, held.at[pl.ds(0, resident)], sems.at[0])]
    for e in range(X):
        place = pl.ds(resident + e * imported_each, imported_each)
        copies.append(pltpu.make_async_copy(tables[e], held.at[place], sems.at[1 + e]))
    copies.append(pltpu.make_async_copy(base, base_held, sems.at[1 + X]))
    for copy in copies:
        copy.start()
    rows = jnp.concatenate(
        [jnp.concatenate([shrink[i * lanes + k] for k in range(lanes)], axis=1) for i in range(rank // 8)], axis=0
    )
    rows = jnp.transpose(rows)
    y, x = spot()
    imported = code[...] - resident
    home = imported // LIMIT
    e = (x - home % X + X) % X
    d = (y - home // X + Y) % Y
    at = jnp.where(imported < 0, code[...], resident + (e * Y + d) * LIMIT + imported % LIMIT)
    column = jnp.transpose(jnp.broadcast_to(at, (8, count)).astype(jnp.float32))[:, :1]
    pair = jnp.concatenate([rows, rows], axis=1)
    high = pair.astype(jnp.bfloat16).astype(jnp.float32)
    low = pair - high
    half = lax.broadcasted_iota(jnp.int32, pair.shape, 1) // rank
    wanted = jnp.broadcast_to(column, pair.shape) - half.astype(jnp.float32)
    both = jnp.concatenate([high, low], axis=0)
    wanted = jnp.concatenate([wanted, wanted], axis=0)
    total = jnp.zeros((2 * count, out.shape[1]), jnp.float32)
    step = 4
    bounds = [resident + e * imported_each for e in range(X + 1)]
    for first in range(0, held.shape[0] // 2, step):
        if first == 0:
            copies[0].wait()
        if 2 * first in bounds:
            copies[1 + bounds.index(2 * first)].wait()
        placed = jnp.concatenate(
            [
                jnp.where(wanted == float(2 * p), both, 0.0).astype(jnp.bfloat16)
                for p in range(first, first + step)
            ],
            axis=1,
        )
        maps = held[2 * first : 2 * (first + step)].reshape(2 * step * rank, out.shape[1])
        total = total + jnp.dot(placed, maps, preferred_element_type=jnp.float32)
    copies[-1].wait()
    out[...] = (base_held[...] + (total[:count] + total[count:])).astype(out.dtype)


def expand(shrink, code, base, up, tables):
    vmem = pl.BlockSpec(memory_space=pltpu.VMEM)
    hbm = pl.BlockSpec(memory_space=pltpu.HBM)
    maps = up.shape[0] + X * tables[0].shape[0]
    return pl.pallas_call(
        expand_kernel,
        out_shape=jax.ShapeDtypeStruct(base.shape, jnp.bfloat16),
        in_specs=[vmem, vmem] + [hbm] * (2 + X),
        out_specs=vmem,
        scratch_shapes=[
            pltpu.VMEM((maps,) + up.shape[1:], up.dtype),
            pltpu.VMEM(base.shape, base.dtype),
            pltpu.SemaphoreType.DMA((2 + X,)),
        ],
    )(shrink, code, base, up, *tables)


def shift(array, axis, size, by):
    return lax.ppermute(array, axis, [(i, (i + by) % size) for i in range(size)])


def shards(inputs, row_adapter_slot, transfer_plan, key_value_weight, adapter_down, adapter_up):
    count = inputs.shape[0]
    resident = adapter_down.shape[0]
    slots = row_adapter_slot.reshape(1, count)

    sent, code = prepare(resident, transfer_plan, slots, inputs)
    rings = [[i * C for i in range(Y)], [i * C + 1 for i in reversed(range(Y))]]
    rows = lax.all_gather(sent, ("y", "c"), axis_index_groups=rings)
    down, picked = dispatch(transfer_plan, adapter_down)
    down = lax.all_to_all(down, "x", 0, 0, tiled=True)

    late, picked = lax.optimization_barrier((inputs, picked))
    base_part = jnp.dot(late, key_value_weight, preferred_element_type=jnp.float32)
    base = lax.psum_scatter(base_part, ("z", "c"), scatter_dimension=1, tiled=True)
    own = local_shrink(code, late, adapter_down)

    ups = pick_up(picked, adapter_up)
    ups = [ups[0]] + [shift(ups[d], "y", Y, d) for d in range(1, Y)]
    down, ups = lax.optimization_barrier((down, ups))
    ups = turn(ups)
    tables = [ups[0]] + [shift(ups[e], "x", X, e) for e in range(1, X)]

    parts = imported_shrink(resident, rows, down, own)
    parts = lax.all_to_all(parts.reshape(Y * T, 8, 128), ("y", "z", "c"), 0, 0, tiled=True)
    shrink = lax.all_to_all(add_and_spread(parts), ("z", "c"), 0, 0, tiled=True)
    return expand(shrink, code, base, adapter_up, tables)


def solution(mesh):
    grid = Mesh(mesh.devices.reshape(Y, X, Z, C), ("y", "x", "z", "c"))
    replica, tensor = ("y", "x"), ("z", "c")
    placed = (
        P(replica, tensor),
        P(replica),
        P(),
        P(tensor, None),
        P(replica, None, tensor),
        P(replica, None, tensor),
    )
    return jax.shard_map(
        shards, mesh=grid, in_specs=placed, out_specs=P(replica, tensor), check_vma=False
    )
```

```python
import functools

import jax
import jax.numpy as jnp
from jax import lax
from jax.experimental import pallas as pl
from jax.experimental.pallas import tpu as pltpu
from jax.sharding import Mesh, PartitionSpec as P

Y, X, Z, C = 8, 4, 8, 2
T = Z * C
GROUPS = Y * X
LIMIT = 2
CODE_ROWS = 16
MIB = 1024 * 1024
AHEAD = 6
NT = (((1,), (1,)), ((), ()))


def spot():
    return lax.axis_index("y"), lax.axis_index("x")


def dispatch_kernel(plan, down, *refs):
    out, picked_out, held, staged, picked, in_sems, out_sems, picked_sem = refs
    resident = down.shape[0]
    y, x = spot()
    pieces = in_sems.shape[0]
    part = resident // pieces

    def read(i):
        rows = pl.ds(i * part, part)
        return pltpu.make_async_copy(down.at[rows], held.at[rows], in_sems.at[i])

    def write(e):
        return pltpu.make_async_copy(staged.at[e], out.at[e], out_sems.at[e])

    for i in range(pieces):
        read(i).start()
    table = plan[...]
    home = table // resident
    number = table - home * resident
    mine = (home == y * X + x).astype(jnp.int32)
    after = jnp.concatenate([jnp.zeros((mine.shape[0], 1), jnp.int32), mine[:, :-1]], axis=1)
    first = jnp.sum(mine * (1 - after) * number, axis=1, keepdims=True)
    second = jnp.sum(mine * after * number, axis=1, keepdims=True)
    lane = lax.broadcasted_iota(jnp.int32, picked_out.shape, 1)
    picked_out[...] = jnp.where(lane == 0, first, jnp.where(lane == 1, second, 0))
    to_scalars = pltpu.make_async_copy(picked_out, picked, picked_sem)
    to_scalars.start()
    to_scalars.wait()
    for i in range(pieces):
        read(i).wait()
    for e in range(X):
        for row in range(Y):
            for j in range(LIMIT):
                staged[e, row * LIMIT + j] = held[picked[row * X + e, j]]
        write(e).start()
    for e in range(X):
        write(e).wait()


def dispatch(plan, down):
    vmem = pl.BlockSpec(memory_space=pltpu.VMEM)
    hbm = pl.BlockSpec(memory_space=pl.ANY)
    shape = (X, Y * LIMIT) + down.shape[1:]
    return pl.pallas_call(
        dispatch_kernel,
        out_shape=(
            jax.ShapeDtypeStruct(shape, down.dtype),
            jax.ShapeDtypeStruct((GROUPS, 128), jnp.int32),
        ),
        in_specs=[vmem, hbm],
        out_specs=(hbm, vmem),
        scratch_shapes=[
            pltpu.VMEM(down.shape, down.dtype),
            pltpu.VMEM(shape, down.dtype),
            pltpu.SMEM((GROUPS, 128), jnp.int32),
            pltpu.SemaphoreType.DMA((4,)),
            pltpu.SemaphoreType.DMA((X,)),
            pltpu.SemaphoreType.DMA,
        ],
        cost_estimate=pl.CostEstimate(flops=0, bytes_accessed=6 * down.size, transcendentals=0),
    )(plan, down)


def prepare_kernel(resident, plan, slots, rows, out, code_out):
    y, x = spot()
    height, width = rows.shape
    slot = slots[...]
    code = slot
    before = jnp.int32(-1)
    for k in range(plan.shape[1]):
        home = plan[y * X + x, k] // resident
        again = (home == before).astype(jnp.int32)
        code = jnp.where(slot == resident + k, resident + home * LIMIT + again, code)
        before = home
    code_out[...] = code
    out[0:height, :] = rows[...]
    wide = jnp.concatenate([code.astype(jnp.float32), jnp.zeros((1, width - height), jnp.float32)], axis=1)
    out[height:, :] = jnp.broadcast_to(wide, (CODE_ROWS, width)).astype(out.dtype)


def prepare(resident, plan, slots, rows):
    height, width = rows.shape
    smem = pl.BlockSpec(memory_space=pltpu.SMEM)
    vmem = pl.BlockSpec(memory_space=pltpu.VMEM)
    return pl.pallas_call(
        functools.partial(prepare_kernel, resident),
        out_shape=(
            jax.ShapeDtypeStruct((height + CODE_ROWS, width), rows.dtype),
            jax.ShapeDtypeStruct(slots.shape, jnp.int32),
        ),
        in_specs=[smem, vmem, vmem],
        out_specs=(vmem, vmem),
        cost_estimate=pl.CostEstimate(flops=0, bytes_accessed=4 * rows.size, transcendentals=0),
    )(plan, slots, rows)


def pick_up_kernel(picked, up, *outs):
    _, x = spot()
    for e in range(X):
        column = lax.rem(x + e, X)
        for row in range(Y):
            for j in range(LIMIT):
                outs[e][row * LIMIT + j] = up[picked[row * X + column, j]]


def pick_up(picked, up):
    smem = pl.BlockSpec(memory_space=pltpu.SMEM)
    vmem = pl.BlockSpec(memory_space=pltpu.VMEM)
    return pl.pallas_call(
        pick_up_kernel,
        out_shape=(jax.ShapeDtypeStruct((Y * LIMIT,) + up.shape[1:], up.dtype),) * X,
        in_specs=[smem, vmem],
        out_specs=(vmem,) * X,
        cost_estimate=pl.CostEstimate(flops=0, bytes_accessed=6 * up.size, transcendentals=0),
    )(picked, up)


def turn_kernel(*refs):
    arrived, outs = refs[:X], refs[X:]
    y, _ = spot()
    for d in range(Y):
        row = lax.rem(y + d, Y)
        for e in range(X):
            for j in range(LIMIT):
                outs[d][e * LIMIT + j] = arrived[e][row * LIMIT + j]


def turn(arrived):
    vmem = pl.BlockSpec(memory_space=pltpu.VMEM)
    shape = jax.ShapeDtypeStruct((X * LIMIT,) + arrived[0].shape[1:], arrived[0].dtype)
    return pl.pallas_call(
        turn_kernel,
        out_shape=(shape,) * Y,
        in_specs=[vmem] * X,
        out_specs=(vmem,) * Y,
        compiler_params=pltpu.CompilerParams(vmem_limit_bytes=6 * MIB),
        cost_estimate=pl.CostEstimate(flops=0, bytes_accessed=4 * X * arrived[0].size, transcendentals=0),
    )(*arrived)


def local_kernel(code, rows, down, out):
    rank = out.shape[0]
    resident = down.shape[0] // rank
    total = jnp.zeros(out.shape, jnp.float32)
    step = 4
    for first in range(0, resident, step):
        product = lax.dot_general(
            down[first * rank : (first + step) * rank, :], rows[...], NT, preferred_element_type=jnp.float32
        )
        for k in range(step):
            total = total + jnp.where(code[...] == first + k, product[k * rank : (k + 1) * rank, :], 0.0)
    out[...] = total


def local_shrink(code, rows, down):
    resident, rank, width = down.shape
    vmem = pl.BlockSpec(memory_space=pltpu.VMEM)
    return pl.pallas_call(
        local_kernel,
        out_shape=jax.ShapeDtypeStruct((rank, rows.shape[0]), jnp.float32),
        in_specs=[vmem] * 3,
        out_specs=vmem,
        cost_estimate=pl.CostEstimate(
            flops=2 * rows.size * resident * rank, bytes_accessed=2 * down.size, transcendentals=0
        ),
    )(code, rows, down.reshape(resident * rank, width))


def imported_kernel(resident, rows, down, own, out, rows_held, down_held, sems):
    rank, count = own.shape
    lanes = out.shape[-1]
    y, _ = spot()
    odd = lax.axis_index("c")

    def reads(g):
        wanted = pl.ds(g * LIMIT * rank, LIMIT * rank)
        at = g + odd * (Y - 1 - 2 * g)
        pairs = [(rows.at[at], rows_held.at[g])]
        pairs += [(down.at[x, wanted], down_held.at[g, pl.ds(x * LIMIT * rank, LIMIT * rank)]) for x in range(X)]
        return [pltpu.make_async_copy(a, b, sems.at[g, i]) for i, (a, b) in enumerate(pairs)]

    for g in range(Y):
        for read in reads(g):
            read.start()
    base = (resident + y * X * LIMIT).astype(jnp.float32)
    for g in range(Y):
        for read in reads(g):
            read.wait()
        code = rows_held[g, count : count + 1, :count].astype(jnp.float32)
        total = jnp.where(y == g, own[...], 0.0)
        product = lax.dot_general(
            down_held[g], rows_held[g, 0:count, :], NT, preferred_element_type=jnp.float32
        )
        for k in range(X * LIMIT):
            total = total + jnp.where(code == base + k, product[k * rank : (k + 1) * rank, :], 0.0)
        for i in range(rank // 8):
            for k in range(count // lanes):
                out[g, i * (count // lanes) + k] = total[i * 8 : (i + 1) * 8, k * lanes : (k + 1) * lanes]


def imported_shrink(resident, rows, down, own):
    rank, count = own.shape
    height, width = rows.shape[1:]
    blocks = rank * count // 1024
    vmem = pl.BlockSpec(memory_space=pltpu.VMEM)
    hbm = pl.BlockSpec(memory_space=pl.ANY)
    return pl.pallas_call(
        functools.partial(imported_kernel, resident),
        out_shape=jax.ShapeDtypeStruct((Y, blocks, 8, 128), jnp.float32),
        in_specs=[hbm, hbm, vmem],
        out_specs=vmem,
        scratch_shapes=[
            pltpu.VMEM((Y, height, width), rows.dtype),
            pltpu.VMEM((Y, X * LIMIT * rank, width), rows.dtype),
            pltpu.SemaphoreType.DMA((Y, X + 1)),
        ],
        cost_estimate=pl.CostEstimate(
            flops=2 * down.size * count, bytes_accessed=2 * (down.size + rows.size), transcendentals=0
        ),
    )(rows, down.reshape(X, -1, width), own)


def add_kernel(parts, out):
    total = jnp.sum(parts[...], axis=0)
    for t in range(out.shape[0]):
        out[t] = total


def add_and_spread(parts):
    vmem = pl.BlockSpec(memory_space=pltpu.VMEM)
    return pl.pallas_call(
        add_kernel,
        out_shape=jax.ShapeDtypeStruct((T,) + parts.shape[1:], jnp.float32),
        in_specs=[vmem],
        out_specs=vmem,
        compiler_params=pltpu.CompilerParams(vmem_limit_bytes=2 * MIB),
    )(parts)


def expand_kernel(shrink, code, base, up, *refs):
    tables, (out, held, base_held, sems) = refs[:Y], refs[Y:]
    count = out.shape[0]
    lanes = count // 128
    rank = shrink.shape[0] // lanes * 8
    resident, imported_each = up.shape[0], tables[0].shape[0]
    copies = [pltpu.make_async_copy(up, held.at[pl.ds(0, resident)], sems.at[0])]
    for d in range(Y):
        place = pl.ds(resident + d * imported_each, imported_each)
        copies.append(pltpu.make_async_copy(tables[d], held.at[place], sems.at[1 + d]))
    copies.append(pltpu.make_async_copy(base, base_held, sems.at[1 + Y]))
    for copy in copies:
        copy.start()
    rows = jnp.concatenate(
        [jnp.concatenate([shrink[i * lanes + k] for k in range(lanes)], axis=1) for i in range(rank // 8)], axis=0
    )
    rows = jnp.transpose(rows)
    y, x = spot()
    imported = code[...] - resident
    home = imported // LIMIT
    e = (x - home % X + X) % X
    d = (y - home // X + Y) % Y
    at = jnp.where(imported < 0, code[...], resident + (d * X + e) * LIMIT + imported % LIMIT)
    column = jnp.transpose(jnp.broadcast_to(at, (8, count)).astype(jnp.float32))[:, :1]
    pair = jnp.concatenate([rows, rows], axis=1)
    high = pair.astype(jnp.bfloat16).astype(jnp.float32)
    low = pair - high
    half = lax.broadcasted_iota(jnp.int32, pair.shape, 1) // rank
    wanted = jnp.broadcast_to(column, pair.shape) - half.astype(jnp.float32)
    both = jnp.concatenate([high, low], axis=0)
    wanted = jnp.concatenate([wanted, wanted], axis=0)
    total = jnp.zeros((2 * count, out.shape[1]), jnp.float32)
    step = 4
    bounds = [resident + d * imported_each for d in range(Y)]
    for first in range(0, held.shape[0] // 2, step):
        if first == 0:
            copies[0].wait()
        if 2 * first in bounds:
            copies[1 + bounds.index(2 * first)].wait()
        placed = jnp.concatenate(
            [
                jnp.where(wanted == float(2 * p), both, 0.0).astype(jnp.bfloat16)
                for p in range(first, first + step)
            ],
            axis=1,
        )
        maps = held[2 * first : 2 * (first + step)].reshape(2 * step * rank, out.shape[1])
        total = total + jnp.dot(placed, maps, preferred_element_type=jnp.float32)
    copies[-1].wait()
    out[...] = (base_held[...] + (total[:count] + total[count:])).astype(out.dtype)


def expand(shrink, code, base, up, tables):
    vmem = pl.BlockSpec(memory_space=pltpu.VMEM)
    hbm = pl.BlockSpec(memory_space=pltpu.HBM)
    maps = up.shape[0] + Y * tables[0].shape[0]
    return pl.pallas_call(
        expand_kernel,
        out_shape=jax.ShapeDtypeStruct(base.shape, jnp.bfloat16),
        in_specs=[vmem, vmem] + [hbm] * (2 + Y),
        out_specs=vmem,
        scratch_shapes=[
            pltpu.VMEM((maps,) + up.shape[1:], up.dtype),
            pltpu.VMEM(base.shape, base.dtype),
            pltpu.SemaphoreType.DMA((2 + Y,)),
        ],
    )(shrink, code, base, up, *tables)


def shift(array, axis, size, by):
    return lax.ppermute(array, axis, [(i, (i + by) % size) for i in range(size)])


def shards(inputs, row_adapter_slot, transfer_plan, key_value_weight, adapter_down, adapter_up):
    count = inputs.shape[0]
    resident = adapter_down.shape[0]
    slots = row_adapter_slot.reshape(1, count)

    sent, code = prepare(resident, transfer_plan, slots, inputs)
    rings = [[i * C for i in range(Y)], [i * C + 1 for i in reversed(range(Y))]]
    rows = lax.all_gather(sent, ("y", "c"), axis_index_groups=rings)
    down, picked = dispatch(transfer_plan, adapter_down)
    down = lax.all_to_all(down, "x", 0, 0, tiled=True)

    late, picked = lax.optimization_barrier((inputs, picked))
    base_part = jnp.dot(late, key_value_weight, preferred_element_type=jnp.float32)
    base = lax.psum_scatter(base_part, ("z", "c"), scatter_dimension=1, tiled=True)
    own = local_shrink(code, late, adapter_down)

    ups = pick_up(picked, adapter_up)
    ups = turn([ups[0]] + [shift(ups[e], "x", X, e) for e in range(1, X)])
    tables = [ups[0]] + [shift(ups[d], "y", Y, d) for d in range(1, Y)]
    down, tables[1:AHEAD] = lax.optimization_barrier((down, tables[1:AHEAD]))

    parts = imported_shrink(resident, rows, down, own)
    parts = lax.all_to_all(parts.reshape(Y * T, 8, 128), ("y", "z", "c"), 0, 0, tiled=True)
    shrink = lax.all_to_all(add_and_spread(parts), ("z", "c"), 0, 0, tiled=True)
    return expand(shrink, code, base, adapter_up, tables)


def solution(mesh):
    grid = Mesh(mesh.devices.reshape(Y, X, Z, C), ("y", "x", "z", "c"))
    replica, tensor = ("y", "x"), ("z", "c")
    placed = (
        P(replica, tensor),
        P(replica),
        P(),
        P(tensor, None),
        P(replica, None, tensor),
        P(replica, None, tensor),
    )
    return jax.shard_map(
        shards, mesh=grid, in_specs=placed, out_specs=P(replica, tensor), check_vma=False
    )
```

```python
import functools

import jax
import jax.numpy as jnp
from jax import lax
from jax.experimental import pallas as pl
from jax.experimental.pallas import tpu as pltpu
from jax.sharding import Mesh, PartitionSpec as P

Y, X, Z, C = 8, 4, 8, 2
T = Z * C
GROUPS = Y * X
LIMIT = 2
CODE_ROWS = 16
MIB = 1024 * 1024
NT = (((1,), (1,)), ((), ()))


def spot():
    return lax.axis_index("y"), lax.axis_index("x")


def dispatch_kernel(plan, down, *refs):
    out, picked_out, held, staged, picked, in_sems, out_sems, picked_sem = refs
    resident = down.shape[0]
    y, x = spot()
    pieces = in_sems.shape[0]
    part = resident // pieces

    def read(i):
        rows = pl.ds(i * part, part)
        return pltpu.make_async_copy(down.at[rows], held.at[rows], in_sems.at[i])

    def write(e):
        return pltpu.make_async_copy(staged.at[e], out.at[e], out_sems.at[e])

    for i in range(pieces):
        read(i).start()
    table = plan[...]
    home = table // resident
    number = table - home * resident
    mine = (home == y * X + x).astype(jnp.int32)
    after = jnp.concatenate([jnp.zeros((mine.shape[0], 1), jnp.int32), mine[:, :-1]], axis=1)
    first = jnp.sum(mine * (1 - after) * number, axis=1, keepdims=True)
    second = jnp.sum(mine * after * number, axis=1, keepdims=True)
    lane = lax.broadcasted_iota(jnp.int32, picked_out.shape, 1)
    picked_out[...] = jnp.where(lane == 0, first, jnp.where(lane == 1, second, 0))
    to_scalars = pltpu.make_async_copy(picked_out, picked, picked_sem)
    to_scalars.start()
    to_scalars.wait()
    for i in range(pieces):
        read(i).wait()
    for e in range(X):
        for row in range(Y):
            for j in range(LIMIT):
                staged[e, row * LIMIT + j] = held[picked[row * X + e, j]]
        write(e).start()
    for e in range(X):
        write(e).wait()


def dispatch(plan, down):
    vmem = pl.BlockSpec(memory_space=pltpu.VMEM)
    hbm = pl.BlockSpec(memory_space=pl.ANY)
    shape = (X, Y * LIMIT) + down.shape[1:]
    return pl.pallas_call(
        dispatch_kernel,
        out_shape=(
            jax.ShapeDtypeStruct(shape, down.dtype),
            jax.ShapeDtypeStruct((GROUPS, 128), jnp.int32),
        ),
        in_specs=[vmem, hbm],
        out_specs=(hbm, vmem),
        scratch_shapes=[
            pltpu.VMEM(down.shape, down.dtype),
            pltpu.VMEM(shape, down.dtype),
            pltpu.SMEM((GROUPS, 128), jnp.int32),
            pltpu.SemaphoreType.DMA((4,)),
            pltpu.SemaphoreType.DMA((X,)),
            pltpu.SemaphoreType.DMA,
        ],
        cost_estimate=pl.CostEstimate(flops=0, bytes_accessed=6 * down.size, transcendentals=0),
    )(plan, down)


def prepare_kernel(resident, plan, slots, rows, out, code_out):
    y, x = spot()
    height, width = rows.shape
    slot = slots[...]
    code = slot
    before = jnp.int32(-1)
    for k in range(plan.shape[1]):
        home = plan[y * X + x, k] // resident
        again = (home == before).astype(jnp.int32)
        code = jnp.where(slot == resident + k, resident + home * LIMIT + again, code)
        before = home
    code_out[...] = code
    out[0:height, :] = rows[...]
    wide = jnp.concatenate([code.astype(jnp.float32), jnp.zeros((1, width - height), jnp.float32)], axis=1)
    out[height:, :] = jnp.broadcast_to(wide, (CODE_ROWS, width)).astype(out.dtype)


def prepare(resident, plan, slots, rows):
    height, width = rows.shape
    smem = pl.BlockSpec(memory_space=pltpu.SMEM)
    vmem = pl.BlockSpec(memory_space=pltpu.VMEM)
    return pl.pallas_call(
        functools.partial(prepare_kernel, resident),
        out_shape=(
            jax.ShapeDtypeStruct((height + CODE_ROWS, width), rows.dtype),
            jax.ShapeDtypeStruct(slots.shape, jnp.int32),
        ),
        in_specs=[smem, vmem, vmem],
        out_specs=(vmem, vmem),
        cost_estimate=pl.CostEstimate(flops=0, bytes_accessed=4 * rows.size, transcendentals=0),
    )(plan, slots, rows)


def pick_up_kernel(picked, up, *outs):
    y, _ = spot()
    for d in range(Y):
        row = lax.rem(y + d, Y)
        for x in range(X):
            for j in range(LIMIT):
                outs[d][x * LIMIT + j] = up[picked[row * X + x, j]]


def pick_up(picked, up):
    smem = pl.BlockSpec(memory_space=pltpu.SMEM)
    vmem = pl.BlockSpec(memory_space=pltpu.VMEM)
    return pl.pallas_call(
        pick_up_kernel,
        out_shape=(jax.ShapeDtypeStruct((X * LIMIT,) + up.shape[1:], up.dtype),) * Y,
        in_specs=[smem, vmem],
        out_specs=(vmem,) * Y,
        cost_estimate=pl.CostEstimate(flops=0, bytes_accessed=6 * up.size, transcendentals=0),
    )(picked, up)


def turn_kernel(*refs):
    arrived, outs = refs[:Y], refs[Y:]
    _, x = spot()
    for e in range(X):
        column = lax.rem(x + e, X)
        for d in range(Y):
            for j in range(LIMIT):
                outs[e][d * LIMIT + j] = arrived[d][column * LIMIT + j]


def turn(arrived):
    vmem = pl.BlockSpec(memory_space=pltpu.VMEM)
    shape = jax.ShapeDtypeStruct((Y * LIMIT,) + arrived[0].shape[1:], arrived[0].dtype)
    return pl.pallas_call(
        turn_kernel,
        out_shape=(shape,) * X,
        in_specs=[vmem] * Y,
        out_specs=(vmem,) * X,
        compiler_params=pltpu.CompilerParams(vmem_limit_bytes=6 * MIB),
        cost_estimate=pl.CostEstimate(flops=0, bytes_accessed=4 * Y * arrived[0].size, transcendentals=0),
    )(*arrived)


def local_kernel(code, rows, down, out):
    rank = out.shape[0]
    resident = down.shape[0] // rank
    total = jnp.zeros(out.shape, jnp.float32)
    step = 4
    for first in range(0, resident, step):
        product = lax.dot_general(
            down[first * rank : (first + step) * rank, :], rows[...], NT, preferred_element_type=jnp.float32
        )
        for k in range(step):
            total = total + jnp.where(code[...] == first + k, product[k * rank : (k + 1) * rank, :], 0.0)
    out[...] = total


def local_shrink(code, rows, down):
    resident, rank, width = down.shape
    vmem = pl.BlockSpec(memory_space=pltpu.VMEM)
    return pl.pallas_call(
        local_kernel,
        out_shape=jax.ShapeDtypeStruct((rank, rows.shape[0]), jnp.float32),
        in_specs=[vmem] * 3,
        out_specs=vmem,
        cost_estimate=pl.CostEstimate(
            flops=2 * rows.size * resident * rank, bytes_accessed=2 * down.size, transcendentals=0
        ),
    )(code, rows, down.reshape(resident * rank, width))


def imported_kernel(resident, rows, down, own, out, rows_held, down_held, sems):
    rank, count = own.shape
    lanes = out.shape[-1]
    y, _ = spot()
    odd = lax.axis_index("c")

    def reads(g):
        wanted = pl.ds(g * LIMIT * rank, LIMIT * rank)
        at = g + odd * (Y - 1 - 2 * g)
        pairs = [(rows.at[at], rows_held.at[g])]
        pairs += [(down.at[x, wanted], down_held.at[g, pl.ds(x * LIMIT * rank, LIMIT * rank)]) for x in range(X)]
        return [pltpu.make_async_copy(a, b, sems.at[g, i]) for i, (a, b) in enumerate(pairs)]

    for g in range(Y):
        for read in reads(g):
            read.start()
    base = (resident + y * X * LIMIT).astype(jnp.float32)
    for g in range(Y):
        for read in reads(g):
            read.wait()
        code = rows_held[g, count : count + 1, :count].astype(jnp.float32)
        total = jnp.where(y == g, own[...], 0.0)
        product = lax.dot_general(
            down_held[g], rows_held[g, 0:count, :], NT, preferred_element_type=jnp.float32
        )
        for k in range(X * LIMIT):
            total = total + jnp.where(code == base + k, product[k * rank : (k + 1) * rank, :], 0.0)
        for i in range(rank // 8):
            for k in range(count // lanes):
                out[g, i * (count // lanes) + k] = total[i * 8 : (i + 1) * 8, k * lanes : (k + 1) * lanes]


def imported_shrink(resident, rows, down, own):
    rank, count = own.shape
    height, width = rows.shape[1:]
    blocks = rank * count // 1024
    vmem = pl.BlockSpec(memory_space=pltpu.VMEM)
    hbm = pl.BlockSpec(memory_space=pl.ANY)
    return pl.pallas_call(
        functools.partial(imported_kernel, resident),
        out_shape=jax.ShapeDtypeStruct((Y, blocks, 8, 128), jnp.float32),
        in_specs=[hbm, hbm, vmem],
        out_specs=vmem,
        scratch_shapes=[
            pltpu.VMEM((Y, height, width), rows.dtype),
            pltpu.VMEM((Y, X * LIMIT * rank, width), rows.dtype),
            pltpu.SemaphoreType.DMA((Y, X + 1)),
        ],
        cost_estimate=pl.CostEstimate(
            flops=2 * down.size * count, bytes_accessed=2 * (down.size + rows.size), transcendentals=0
        ),
    )(rows, down.reshape(X, -1, width), own)


def add_kernel(parts, out):
    total = jnp.sum(parts[...], axis=0)
    for t in range(out.shape[0]):
        out[t] = total


def add_and_spread(parts):
    vmem = pl.BlockSpec(memory_space=pltpu.VMEM)
    return pl.pallas_call(
        add_kernel,
        out_shape=jax.ShapeDtypeStruct((T,) + parts.shape[1:], jnp.float32),
        in_specs=[vmem],
        out_specs=vmem,
        compiler_params=pltpu.CompilerParams(vmem_limit_bytes=2 * MIB),
    )(parts)


def expand_kernel(shrink, code, base, up, *refs):
    tables, (out, held, base_held, sems) = refs[:X], refs[X:]
    count = out.shape[0]
    lanes = count // 128
    rank = shrink.shape[0] // lanes * 8
    resident, imported_each = up.shape[0], tables[0].shape[0]
    copies = [pltpu.make_async_copy(up, held.at[pl.ds(0, resident)], sems.at[0])]
    for e in range(X):
        place = pl.ds(resident + e * imported_each, imported_each)
        copies.append(pltpu.make_async_copy(tables[e], held.at[place], sems.at[1 + e]))
    copies.append(pltpu.make_async_copy(base, base_held, sems.at[1 + X]))
    for copy in copies:
        copy.start()
    rows = jnp.concatenate(
        [jnp.concatenate([shrink[i * lanes + k] for k in range(lanes)], axis=1) for i in range(rank // 8)], axis=0
    )
    rows = jnp.transpose(rows)
    y, x = spot()
    imported = code[...] - resident
    home = imported // LIMIT
    e = (x - home % X + X) % X
    d = (y - home // X + Y) % Y
    at = jnp.where(imported < 0, code[...], resident + (e * Y + d) * LIMIT + imported % LIMIT)
    column = jnp.transpose(jnp.broadcast_to(at, (8, count)).astype(jnp.float32))[:, :1]
    pair = jnp.concatenate([rows, rows], axis=1)
    high = pair.astype(jnp.bfloat16).astype(jnp.float32)
    low = pair - high
    half = lax.broadcasted_iota(jnp.int32, pair.shape, 1) // rank
    wanted = jnp.broadcast_to(column, pair.shape) - half.astype(jnp.float32)
    both = jnp.concatenate([high, low], axis=0)
    wanted = jnp.concatenate([wanted, wanted], axis=0)
    total = jnp.zeros((2 * count, out.shape[1]), jnp.float32)
    step = 4
    bounds = [resident + e * imported_each for e in range(X + 1)]
    for first in range(0, held.shape[0] // 2, step):
        if first == 0:
            copies[0].wait()
        if 2 * first in bounds:
            copies[1 + bounds.index(2 * first)].wait()
        placed = jnp.concatenate(
            [
                jnp.where(wanted == float(2 * p), both, 0.0).astype(jnp.bfloat16)
                for p in range(first, first + step)
            ],
            axis=1,
        )
        maps = held[2 * first : 2 * (first + step)].reshape(2 * step * rank, out.shape[1])
        total = total + jnp.dot(placed, maps, preferred_element_type=jnp.float32)
    copies[-1].wait()
    out[...] = (base_held[...] + (total[:count] + total[count:])).astype(out.dtype)


def expand(shrink, code, base, up, tables):
    vmem = pl.BlockSpec(memory_space=pltpu.VMEM)
    hbm = pl.BlockSpec(memory_space=pltpu.HBM)
    maps = up.shape[0] + X * tables[0].shape[0]
    return pl.pallas_call(
        expand_kernel,
        out_shape=jax.ShapeDtypeStruct(base.shape, jnp.bfloat16),
        in_specs=[vmem, vmem] + [hbm] * (2 + X),
        out_specs=vmem,
        scratch_shapes=[
            pltpu.VMEM((maps,) + up.shape[1:], up.dtype),
            pltpu.VMEM(base.shape, base.dtype),
            pltpu.SemaphoreType.DMA((2 + X,)),
        ],
    )(shrink, code, base, up, *tables)


def shift(array, axis, size, by):
    return lax.ppermute(array, axis, [(i, (i + by) % size) for i in range(size)])


def shards(inputs, row_adapter_slot, transfer_plan, key_value_weight, adapter_down, adapter_up):
    count = inputs.shape[0]
    resident = adapter_down.shape[0]
    slots = row_adapter_slot.reshape(1, count)

    sent, code = prepare(resident, transfer_plan, slots, inputs)
    rings = [[i * C for i in range(Y)], [i * C + 1 for i in reversed(range(Y))]]
    rows = lax.all_gather(sent, ("y", "c"), axis_index_groups=rings)
    down, picked = dispatch(transfer_plan, adapter_down)
    down = lax.all_to_all(down, "x", 0, 0, tiled=True)

    late, picked = lax.optimization_barrier((inputs, picked))
    base_part = jnp.dot(late, key_value_weight, preferred_element_type=jnp.float32)
    base = lax.psum_scatter(base_part, ("z", "c"), scatter_dimension=1, tiled=True)
    own = local_shrink(code, late, adapter_down)

    ups = pick_up(picked, adapter_up)
    near, far = (1, 7, 2, 6), (3, 5, 4)
    moved = {d: shift(ups[d], "y", Y, d) for d in near}
    moved, later = lax.optimization_barrier((moved, {d: ups[d] for d in far}))
    moved |= {d: shift(later[d], "y", Y, d) for d in far}
    moved[0] = ups[0]
    down, moved = lax.optimization_barrier((down, moved))
    ups = [moved[d] for d in range(Y)]
    ups = turn(ups)
    tables = [ups[0]] + [shift(ups[e], "x", X, e) for e in range(1, X)]

    parts = imported_shrink(resident, rows, down, own)
    parts = lax.all_to_all(parts.reshape(Y * T, 8, 128), ("y", "z", "c"), 0, 0, tiled=True)
    shrink = lax.all_to_all(add_and_spread(parts), ("z", "c"), 0, 0, tiled=True)
    return expand(shrink, code, base, adapter_up, tables)


def solution(mesh):
    grid = Mesh(mesh.devices.reshape(Y, X, Z, C), ("y", "x", "z", "c"))
    replica, tensor = ("y", "x"), ("z", "c")
    placed = (
        P(replica, tensor),
        P(replica),
        P(),
        P(tensor, None),
        P(replica, None, tensor),
        P(replica, None, tensor),
    )
    return jax.shard_map(
        shards, mesh=grid, in_specs=placed, out_specs=P(replica, tensor), check_vma=False
    )
```

```python
import functools

import jax
import jax.numpy as jnp
from jax import lax
from jax.experimental import pallas as pl
from jax.experimental.pallas import tpu as pltpu
from jax.sharding import Mesh, PartitionSpec as P

Y, X, Z, C = 8, 4, 8, 2
T = Z * C
GROUPS = Y * X
LIMIT = 2
CODE_ROWS = 16
MIB = 1024 * 1024
NT = (((1,), (1,)), ((), ()))


def spot():
    return lax.axis_index("y"), lax.axis_index("x")


def dispatch_kernel(plan, down, *refs):
    out, picked_out, held, staged, picked, in_sems, out_sems, picked_sem = refs
    resident = down.shape[0]
    y, x = spot()
    pieces = in_sems.shape[0]
    part = resident // pieces

    def read(i):
        rows = pl.ds(i * part, part)
        return pltpu.make_async_copy(down.at[rows], held.at[rows], in_sems.at[i])

    def write(e):
        return pltpu.make_async_copy(staged.at[e], out.at[e], out_sems.at[e])

    for i in range(pieces):
        read(i).start()
    table = plan[...]
    home = table // resident
    number = table - home * resident
    mine = (home == y * X + x).astype(jnp.int32)
    after = jnp.concatenate([jnp.zeros((mine.shape[0], 1), jnp.int32), mine[:, :-1]], axis=1)
    first = jnp.sum(mine * (1 - after) * number, axis=1, keepdims=True)
    second = jnp.sum(mine * after * number, axis=1, keepdims=True)
    lane = lax.broadcasted_iota(jnp.int32, picked_out.shape, 1)
    picked_out[...] = jnp.where(lane == 0, first, jnp.where(lane == 1, second, 0))
    to_scalars = pltpu.make_async_copy(picked_out, picked, picked_sem)
    to_scalars.start()
    to_scalars.wait()
    for i in range(pieces):
        read(i).wait()
    for e in range(X):
        for row in range(Y):
            for j in range(LIMIT):
                staged[e, row * LIMIT + j] = held[picked[row * X + e, j]]
        write(e).start()
    for e in range(X):
        write(e).wait()


def dispatch(plan, down):
    vmem = pl.BlockSpec(memory_space=pltpu.VMEM)
    hbm = pl.BlockSpec(memory_space=pl.ANY)
    shape = (X, Y * LIMIT) + down.shape[1:]
    return pl.pallas_call(
        dispatch_kernel,
        out_shape=(
            jax.ShapeDtypeStruct(shape, down.dtype),
            jax.ShapeDtypeStruct((GROUPS, 128), jnp.int32),
        ),
        in_specs=[vmem, hbm],
        out_specs=(hbm, vmem),
        scratch_shapes=[
            pltpu.VMEM(down.shape, down.dtype),
            pltpu.VMEM(shape, down.dtype),
            pltpu.SMEM((GROUPS, 128), jnp.int32),
            pltpu.SemaphoreType.DMA((4,)),
            pltpu.SemaphoreType.DMA((X,)),
            pltpu.SemaphoreType.DMA,
        ],
        cost_estimate=pl.CostEstimate(flops=0, bytes_accessed=6 * down.size, transcendentals=0),
    )(plan, down)


def pick_up_kernel(picked, plan, slots, up, *refs):
    outs, code_out = refs[:Y], refs[Y]
    resident, rank, lanes = up.shape
    y, x = spot()
    slot = slots[...]
    code = slot
    before = jnp.int32(-1)
    for k in range(plan.shape[1]):
        home = plan[y * X + x, k] // resident
        again = (home == before).astype(jnp.int32)
        code = jnp.where(slot == resident + k, resident + home * LIMIT + again, code)
        before = home
    code_out[...] = code
    tail = [code[:, k * lanes : (k + 1) * lanes].astype(jnp.float32) for k in range(code.shape[1] // lanes)]
    tail.append(jnp.zeros((CODE_ROWS - len(tail), lanes), jnp.float32))
    tail = jnp.concatenate(tail, axis=0).astype(up.dtype)
    for d in range(Y):
        row = lax.rem(y + d, Y)
        for column in range(X):
            for j in range(LIMIT):
                at = (column * LIMIT + j) * rank
                outs[d][at : at + rank, :] = up[picked[row * X + column, j]]
        outs[d][X * LIMIT * rank :, :] = tail


def pick_up(picked, plan, slots, up):
    smem = pl.BlockSpec(memory_space=pltpu.SMEM)
    vmem = pl.BlockSpec(memory_space=pltpu.VMEM)
    _, rank, lanes = up.shape
    shape = jax.ShapeDtypeStruct((X * LIMIT * rank + CODE_ROWS, lanes), up.dtype)
    return pl.pallas_call(
        pick_up_kernel,
        out_shape=(shape,) * Y + (jax.ShapeDtypeStruct(slots.shape, jnp.int32),),
        in_specs=[smem, smem, vmem, vmem],
        out_specs=(vmem,) * (Y + 1),
        cost_estimate=pl.CostEstimate(flops=0, bytes_accessed=6 * up.size, transcendentals=0),
    )(picked, plan, slots, up)


def turn_kernel(*refs):
    arrived, outs, codes = refs[:Y], refs[Y:-1], refs[-1]
    _, x = spot()
    rank = outs[0].shape[1]
    for d in range(Y):
        codes[d] = arrived[d][X * LIMIT * rank :, :]
    for e in range(X):
        column = lax.rem(x + e, X)
        for d in range(Y):
            for j in range(LIMIT):
                at = pl.multiple_of((column * LIMIT + j) * rank, rank)
                outs[e][d * LIMIT + j] = arrived[d][pl.ds(at, rank), :]


def turn(rank, arrived):
    vmem = pl.BlockSpec(memory_space=pltpu.VMEM)
    shape = jax.ShapeDtypeStruct((Y * LIMIT, rank, arrived[0].shape[-1]), arrived[0].dtype)
    return pl.pallas_call(
        turn_kernel,
        out_shape=(shape,) * X
        + (jax.ShapeDtypeStruct((Y, CODE_ROWS, arrived[0].shape[-1]), arrived[0].dtype),),
        in_specs=[vmem] * Y,
        out_specs=(vmem,) * (X + 1),
        compiler_params=pltpu.CompilerParams(vmem_limit_bytes=6 * MIB),
        cost_estimate=pl.CostEstimate(flops=0, bytes_accessed=4 * Y * arrived[0].size, transcendentals=0),
    )(*arrived)


def local_kernel(code, rows, down, out):
    rank = out.shape[0]
    resident = down.shape[0] // rank
    total = jnp.zeros(out.shape, jnp.float32)
    step = 4
    for first in range(0, resident, step):
        product = lax.dot_general(
            down[first * rank : (first + step) * rank, :], rows[...], NT, preferred_element_type=jnp.float32
        )
        for k in range(step):
            total = total + jnp.where(code[...] == first + k, product[k * rank : (k + 1) * rank, :], 0.0)
    out[...] = total


def local_shrink(code, rows, down):
    resident, rank, width = down.shape
    vmem = pl.BlockSpec(memory_space=pltpu.VMEM)
    return pl.pallas_call(
        local_kernel,
        out_shape=jax.ShapeDtypeStruct((rank, rows.shape[0]), jnp.float32),
        in_specs=[vmem] * 3,
        out_specs=vmem,
        cost_estimate=pl.CostEstimate(
            flops=2 * rows.size * resident * rank, bytes_accessed=2 * down.size, transcendentals=0
        ),
    )(code, rows, down.reshape(resident * rank, width))


def imported_kernel(resident, rows, down, own, codes, out, rows_held, down_held, sems):
    rank, count = own.shape
    lanes = out.shape[-1]
    y, _ = spot()
    odd = lax.axis_index("c")

    def group(d):
        return lax.rem(y - d + Y, Y)

    def reads(d):
        g = group(d)
        at = g + odd * (Y - 1 - 2 * g)
        wanted = pl.ds(pl.multiple_of(g * LIMIT * rank, LIMIT * rank), LIMIT * rank)
        pairs = [(rows.at[at], rows_held.at[d])]
        pairs += [(down.at[x, wanted], down_held.at[d, pl.ds(x * LIMIT * rank, LIMIT * rank)]) for x in range(X)]
        return [pltpu.make_async_copy(a, b, sems.at[d, i]) for i, (a, b) in enumerate(pairs)]

    for d in range(Y):
        for read in reads(d):
            read.start()
    base = (resident + y * X * LIMIT).astype(jnp.float32)
    for d in range(Y):
        for read in reads(d):
            read.wait()
        tail = codes[d].astype(jnp.float32)
        code = jnp.concatenate([tail[k : k + 1] for k in range(count // lanes)], axis=1)
        total = own[...] if d == 0 else jnp.zeros(own.shape, jnp.float32)
        product = lax.dot_general(down_held[d], rows_held[d], NT, preferred_element_type=jnp.float32)
        for k in range(X * LIMIT):
            total = total + jnp.where(code == base + k, product[k * rank : (k + 1) * rank, :], 0.0)
        g = group(d)
        for i in range(rank // 8):
            for k in range(count // lanes):
                out[g, i * (count // lanes) + k] = total[i * 8 : (i + 1) * 8, k * lanes : (k + 1) * lanes]


def imported_shrink(resident, rows, down, own, codes):
    rank, count = own.shape
    width = rows.shape[-1]
    blocks = rank * count // 1024
    vmem = pl.BlockSpec(memory_space=pltpu.VMEM)
    hbm = pl.BlockSpec(memory_space=pl.ANY)
    return pl.pallas_call(
        functools.partial(imported_kernel, resident),
        out_shape=jax.ShapeDtypeStruct((Y, blocks, 8, 128), jnp.float32),
        in_specs=[hbm, hbm, vmem, vmem],
        out_specs=vmem,
        scratch_shapes=[
            pltpu.VMEM((Y, count, width), rows.dtype),
            pltpu.VMEM((Y, X * LIMIT * rank, width), rows.dtype),
            pltpu.SemaphoreType.DMA((Y, X + 1)),
        ],
        cost_estimate=pl.CostEstimate(
            flops=2 * down.size * count, bytes_accessed=2 * (down.size + rows.size), transcendentals=0
        ),
    )(rows, down.reshape(X, -1, width), own, codes)


def add_kernel(parts, out):
    total = jnp.sum(parts[...], axis=0)
    for t in range(out.shape[0]):
        out[t] = total


def add_and_spread(parts):
    vmem = pl.BlockSpec(memory_space=pltpu.VMEM)
    return pl.pallas_call(
        add_kernel,
        out_shape=jax.ShapeDtypeStruct((T,) + parts.shape[1:], jnp.float32),
        in_specs=[vmem],
        out_specs=vmem,
        compiler_params=pltpu.CompilerParams(vmem_limit_bytes=2 * MIB),
    )(parts)


def expand_kernel(shrink, code, base, up, *refs):
    tables, (out, held, base_held, sems) = refs[:X], refs[X:]
    count = out.shape[0]
    lanes = count // 128
    rank = shrink.shape[0] // lanes * 8
    resident, imported_each = up.shape[0], tables[0].shape[0]
    copies = [pltpu.make_async_copy(up, held.at[pl.ds(0, resident)], sems.at[0])]
    for e in range(X):
        place = pl.ds(resident + e * imported_each, imported_each)
        copies.append(pltpu.make_async_copy(tables[e], held.at[place], sems.at[1 + e]))
    copies.append(pltpu.make_async_copy(base, base_held, sems.at[1 + X]))
    for copy in copies:
        copy.start()
    rows = jnp.concatenate(
        [jnp.concatenate([shrink[i * lanes + k] for k in range(lanes)], axis=1) for i in range(rank // 8)], axis=0
    )
    rows = jnp.transpose(rows)
    y, x = spot()
    imported = code[...] - resident
    home = imported // LIMIT
    e = (x - home % X + X) % X
    d = (y - home // X + Y) % Y
    at = jnp.where(imported < 0, code[...], resident + (e * Y + d) * LIMIT + imported % LIMIT)
    column = jnp.transpose(jnp.broadcast_to(at, (8, count)).astype(jnp.float32))[:, :1]
    pair = jnp.concatenate([rows, rows], axis=1)
    high = pair.astype(jnp.bfloat16).astype(jnp.float32)
    low = pair - high
    half = lax.broadcasted_iota(jnp.int32, pair.shape, 1) // rank
    wanted = jnp.broadcast_to(column, pair.shape) - half.astype(jnp.float32)
    both = jnp.concatenate([high, low], axis=0)
    wanted = jnp.concatenate([wanted, wanted], axis=0)
    total = jnp.zeros((2 * count, out.shape[1]), jnp.float32)
    step = 4
    bounds = [resident + e * imported_each for e in range(X + 1)]
    for first in range(0, held.shape[0] // 2, step):
        if first == 0:
            copies[0].wait()
        if 2 * first in bounds:
            copies[1 + bounds.index(2 * first)].wait()
        placed = jnp.concatenate(
            [
                jnp.where(wanted == float(2 * p), both, 0.0).astype(jnp.bfloat16)
                for p in range(first, first + step)
            ],
            axis=1,
        )
        maps = held[2 * first : 2 * (first + step)].reshape(2 * step * rank, out.shape[1])
        total = total + jnp.dot(placed, maps, preferred_element_type=jnp.float32)
    copies[-1].wait()
    out[...] = (base_held[...] + (total[:count] + total[count:])).astype(out.dtype)


def expand(shrink, code, base, up, tables):
    vmem = pl.BlockSpec(memory_space=pltpu.VMEM)
    hbm = pl.BlockSpec(memory_space=pltpu.HBM)
    maps = up.shape[0] + X * tables[0].shape[0]
    return pl.pallas_call(
        expand_kernel,
        out_shape=jax.ShapeDtypeStruct(base.shape, jnp.bfloat16),
        in_specs=[vmem, vmem] + [hbm] * (2 + X),
        out_specs=vmem,
        scratch_shapes=[
            pltpu.VMEM((maps,) + up.shape[1:], up.dtype),
            pltpu.VMEM(base.shape, base.dtype),
            pltpu.SemaphoreType.DMA((2 + X,)),
        ],
    )(shrink, code, base, up, *tables)


def shift(array, axis, size, by):
    return lax.ppermute(array, axis, [(i, (i + by) % size) for i in range(size)])


def shards(inputs, row_adapter_slot, transfer_plan, key_value_weight, adapter_down, adapter_up):
    count = inputs.shape[0]
    resident, rank, _ = adapter_down.shape
    slots = row_adapter_slot.reshape(1, count)

    rings = [[i * C for i in range(Y)], [i * C + 1 for i in reversed(range(Y))]]
    rows = lax.all_gather(inputs, ("y", "c"), axis_index_groups=rings)
    down, picked = dispatch(transfer_plan, adapter_down)
    down = lax.all_to_all(down, "x", 0, 0, tiled=True)

    late, picked = lax.optimization_barrier((inputs, picked))
    base_part = jnp.dot(late, key_value_weight, preferred_element_type=jnp.float32)
    base = lax.psum_scatter(base_part, ("z", "c"), scatter_dimension=1, tiled=True)

    *ups, code = pick_up(picked, transfer_plan, slots, adapter_up)
    own = local_shrink(code, late, adapter_down)
    near, far = (1, 7, 2, 6), (3, 5, 4)
    moved = {d: shift(ups[d], "y", Y, d) for d in near}
    moved, later, own = lax.optimization_barrier((moved, {d: ups[d] for d in far}, own))
    moved |= {d: shift(later[d], "y", Y, d) for d in far}
    moved[0] = ups[0]
    down, moved = lax.optimization_barrier((down, moved))
    ups = [moved[d] for d in range(Y)]
    *ups, codes = turn(rank, ups)
    parts = imported_shrink(resident, rows, down, own, codes)
    tables = [ups[0]] + [shift(ups[e], "x", X, e) for e in range(1, X)]

    parts = lax.all_to_all(parts.reshape(Y * T, 8, 128), ("y", "z", "c"), 0, 0, tiled=True)
    shrink = lax.all_to_all(add_and_spread(parts), ("z", "c"), 0, 0, tiled=True)
    return expand(shrink, code, base, adapter_up, tables)


def solution(mesh):
    grid = Mesh(mesh.devices.reshape(Y, X, Z, C), ("y", "x", "z", "c"))
    replica, tensor = ("y", "x"), ("z", "c")
    placed = (
        P(replica, tensor),
        P(replica),
        P(),
        P(tensor, None),
        P(replica, None, tensor),
        P(replica, None, tensor),
    )
    return jax.shard_map(
        shards, mesh=grid, in_specs=placed, out_specs=P(replica, tensor), check_vma=False
    )
```

```python
import functools

import jax
import jax.numpy as jnp
from jax import lax
from jax.experimental import pallas as pl
from jax.experimental.pallas import tpu as pltpu
from jax.sharding import Mesh, PartitionSpec as P

Y, X, Z, C = 8, 4, 8, 2
T = Z * C
GROUPS = Y * X
LIMIT = 2
CODE_ROWS = 16
MIB = 1024 * 1024
NT = (((1,), (1,)), ((), ()))


def spot():
    return lax.axis_index("y"), lax.axis_index("x")


def dispatch_kernel(plan, down, *refs):
    out, picked_out, held, staged, picked, in_sems, out_sems, picked_sem = refs
    resident = down.shape[0]
    y, x = spot()
    pieces = in_sems.shape[0]
    part = resident // pieces

    def read(i):
        rows = pl.ds(i * part, part)
        return pltpu.make_async_copy(down.at[rows], held.at[rows], in_sems.at[i])

    def write(e):
        return pltpu.make_async_copy(staged.at[e], out.at[e], out_sems.at[e])

    for i in range(pieces):
        read(i).start()
    table = plan[...]
    home = table // resident
    number = table - home * resident
    mine = (home == y * X + x).astype(jnp.int32)
    after = jnp.concatenate([jnp.zeros((mine.shape[0], 1), jnp.int32), mine[:, :-1]], axis=1)
    first = jnp.sum(mine * (1 - after) * number, axis=1, keepdims=True)
    second = jnp.sum(mine * after * number, axis=1, keepdims=True)
    lane = lax.broadcasted_iota(jnp.int32, picked_out.shape, 1)
    picked_out[...] = jnp.where(lane == 0, first, jnp.where(lane == 1, second, 0))
    to_scalars = pltpu.make_async_copy(picked_out, picked, picked_sem)
    to_scalars.start()
    to_scalars.wait()
    for i in range(pieces):
        read(i).wait()
    for e in range(X):
        for row in range(Y):
            for j in range(LIMIT):
                staged[e, row * LIMIT + j] = held[picked[row * X + e, j]]
        write(e).start()
    for e in range(X):
        write(e).wait()


def dispatch(plan, down):
    vmem = pl.BlockSpec(memory_space=pltpu.VMEM)
    hbm = pl.BlockSpec(memory_space=pl.ANY)
    shape = (X, Y * LIMIT) + down.shape[1:]
    return pl.pallas_call(
        dispatch_kernel,
        out_shape=(
            jax.ShapeDtypeStruct(shape, down.dtype),
            jax.ShapeDtypeStruct((GROUPS, 128), jnp.int32),
        ),
        in_specs=[vmem, hbm],
        out_specs=(hbm, vmem),
        scratch_shapes=[
            pltpu.VMEM(down.shape, down.dtype),
            pltpu.VMEM(shape, down.dtype),
            pltpu.SMEM((GROUPS, 128), jnp.int32),
            pltpu.SemaphoreType.DMA((4,)),
            pltpu.SemaphoreType.DMA((X,)),
            pltpu.SemaphoreType.DMA,
        ],
        cost_estimate=pl.CostEstimate(flops=0, bytes_accessed=6 * down.size, transcendentals=0),
    )(plan, down)


def prepare_kernel(resident, plan, slots, rows, out, code_out):
    y, x = spot()
    height, width = rows.shape
    slot = slots[...]
    code = slot
    before = jnp.int32(-1)
    for k in range(plan.shape[1]):
        home = plan[y * X + x, k] // resident
        again = (home == before).astype(jnp.int32)
        code = jnp.where(slot == resident + k, resident + home * LIMIT + again, code)
        before = home
    code_out[...] = code
    out[0:height, :] = rows[...]
    wide = jnp.concatenate([code.astype(jnp.float32), jnp.zeros((1, width - height), jnp.float32)], axis=1)
    out[height:, :] = jnp.broadcast_to(wide, (CODE_ROWS, width)).astype(out.dtype)


def prepare(resident, plan, slots, rows):
    height, width = rows.shape
    smem = pl.BlockSpec(memory_space=pltpu.SMEM)
    vmem = pl.BlockSpec(memory_space=pltpu.VMEM)
    return pl.pallas_call(
        functools.partial(prepare_kernel, resident),
        out_shape=(
            jax.ShapeDtypeStruct((height + CODE_ROWS, width), rows.dtype),
            jax.ShapeDtypeStruct(slots.shape, jnp.int32),
        ),
        in_specs=[smem, vmem, vmem],
        out_specs=(vmem, vmem),
        cost_estimate=pl.CostEstimate(flops=0, bytes_accessed=4 * rows.size, transcendentals=0),
    )(plan, slots, rows)


def pick_up_kernel(picked, up, *outs):
    y, _ = spot()
    for d in range(Y):
        row = lax.rem(y + d, Y)
        for x in range(X):
            for j in range(LIMIT):
                outs[d][x * LIMIT + j] = up[picked[row * X + x, j]]


def pick_up(picked, up):
    smem = pl.BlockSpec(memory_space=pltpu.SMEM)
    vmem = pl.BlockSpec(memory_space=pltpu.VMEM)
    return pl.pallas_call(
        pick_up_kernel,
        out_shape=(jax.ShapeDtypeStruct((X * LIMIT,) + up.shape[1:], up.dtype),) * Y,
        in_specs=[smem, vmem],
        out_specs=(vmem,) * Y,
        cost_estimate=pl.CostEstimate(flops=0, bytes_accessed=6 * up.size, transcendentals=0),
    )(picked, up)


def turn_kernel(*refs):
    arrived, outs = refs[:Y], refs[Y:]
    _, x = spot()
    for e in range(X):
        column = lax.rem(x + e, X)
        for d in range(Y):
            for j in range(LIMIT):
                outs[e][d * LIMIT + j] = arrived[d][column * LIMIT + j]


def turn(arrived):
    vmem = pl.BlockSpec(memory_space=pltpu.VMEM)
    shape = jax.ShapeDtypeStruct((Y * LIMIT,) + arrived[0].shape[1:], arrived[0].dtype)
    return pl.pallas_call(
        turn_kernel,
        out_shape=(shape,) * X,
        in_specs=[vmem] * Y,
        out_specs=(vmem,) * X,
        compiler_params=pltpu.CompilerParams(vmem_limit_bytes=6 * MIB),
        cost_estimate=pl.CostEstimate(flops=0, bytes_accessed=4 * Y * arrived[0].size, transcendentals=0),
    )(*arrived)


def local_kernel(code, rows, down, out):
    rank = out.shape[0]
    resident = down.shape[0] // rank
    total = jnp.zeros(out.shape, jnp.float32)
    step = 4
    for first in range(0, resident, step):
        product = lax.dot_general(
            down[first * rank : (first + step) * rank, :], rows[...], NT, preferred_element_type=jnp.float32
        )
        for k in range(step):
            total = total + jnp.where(code[...] == first + k, product[k * rank : (k + 1) * rank, :], 0.0)
    out[...] = total


def local_shrink(code, rows, down):
    resident, rank, width = down.shape
    vmem = pl.BlockSpec(memory_space=pltpu.VMEM)
    return pl.pallas_call(
        local_kernel,
        out_shape=jax.ShapeDtypeStruct((rank, rows.shape[0]), jnp.float32),
        in_specs=[vmem] * 3,
        out_specs=vmem,
        cost_estimate=pl.CostEstimate(
            flops=2 * rows.size * resident * rank, bytes_accessed=2 * down.size, transcendentals=0
        ),
    )(code, rows, down.reshape(resident * rank, width))


def imported_kernel(resident, rows, down, own, out, rows_held, down_held, sems):
    rank, count = own.shape
    lanes = out.shape[-1]
    y, _ = spot()
    odd = lax.axis_index("c")

    def reads(g):
        wanted = pl.ds(g * LIMIT * rank, LIMIT * rank)
        at = g + odd * (Y - 1 - 2 * g)
        pairs = [(rows.at[at], rows_held.at[g])]
        pairs += [(down.at[x, wanted], down_held.at[g, pl.ds(x * LIMIT * rank, LIMIT * rank)]) for x in range(X)]
        return [pltpu.make_async_copy(a, b, sems.at[g, i]) for i, (a, b) in enumerate(pairs)]

    for g in range(3):
        for read in reads(g):
            read.start()
    base = (resident + y * X * LIMIT).astype(jnp.float32)
    for g in range(Y):
        for read in reads(g):
            read.wait()
        for read in reads(g + 3) if g + 3 < Y else ():
            read.start()
        code = rows_held[g, count : count + 1, :count].astype(jnp.float32)
        total = jnp.where(y == g, own[...], 0.0)
        product = lax.dot_general(
            down_held[g], rows_held[g, 0:count, :], NT, preferred_element_type=jnp.float32
        )
        for k in range(X * LIMIT):
            total = total + jnp.where(code == base + k, product[k * rank : (k + 1) * rank, :], 0.0)
        for i in range(rank // 8):
            for k in range(count // lanes):
                out[g, i * (count // lanes) + k] = total[i * 8 : (i + 1) * 8, k * lanes : (k + 1) * lanes]


def imported_shrink(resident, rows, down, own):
    rank, count = own.shape
    height, width = rows.shape[1:]
    blocks = rank * count // 1024
    vmem = pl.BlockSpec(memory_space=pltpu.VMEM)
    hbm = pl.BlockSpec(memory_space=pl.ANY)
    return pl.pallas_call(
        functools.partial(imported_kernel, resident),
        out_shape=jax.ShapeDtypeStruct((Y, blocks, 8, 128), jnp.float32),
        in_specs=[hbm, hbm, vmem],
        out_specs=vmem,
        scratch_shapes=[
            pltpu.VMEM((Y, height, width), rows.dtype),
            pltpu.VMEM((Y, X * LIMIT * rank, width), rows.dtype),
            pltpu.SemaphoreType.DMA((Y, X + 1)),
        ],
        cost_estimate=pl.CostEstimate(
            flops=2 * down.size * count, bytes_accessed=2 * (down.size + rows.size), transcendentals=0
        ),
    )(rows, down.reshape(X, -1, width), own)


def add_kernel(parts, out):
    total = jnp.sum(parts[...], axis=0)
    for t in range(out.shape[0]):
        out[t] = total


def add_up(parts, times):
    vmem = pl.BlockSpec(memory_space=pltpu.VMEM)
    return pl.pallas_call(
        add_kernel,
        out_shape=jax.ShapeDtypeStruct((times,) + parts.shape[1:], jnp.float32),
        in_specs=[vmem],
        out_specs=vmem,
        compiler_params=pltpu.CompilerParams(vmem_limit_bytes=2 * MIB),
    )(parts)


def expand_kernel(shrink, code, base, up, *refs):
    tables, (out, held, base_held, sems) = refs[:X], refs[X:]
    count = out.shape[0]
    lanes = count // 128
    rank = shrink.shape[0] // lanes * 8
    resident, imported_each = up.shape[0], tables[0].shape[0]
    copies = [pltpu.make_async_copy(up, held.at[pl.ds(0, resident)], sems.at[0])]
    for e in range(X):
        place = pl.ds(resident + e * imported_each, imported_each)
        copies.append(pltpu.make_async_copy(tables[e], held.at[place], sems.at[1 + e]))
    copies.append(pltpu.make_async_copy(base, base_held, sems.at[1 + X]))
    for copy in copies:
        copy.start()
    rows = jnp.concatenate(
        [jnp.concatenate([shrink[i * lanes + k] for k in range(lanes)], axis=1) for i in range(rank // 8)], axis=0
    )
    rows = jnp.transpose(rows)
    y, x = spot()
    imported = code[...] - resident
    home = imported // LIMIT
    e = (x - home % X + X) % X
    d = (y - home // X + Y) % Y
    at = jnp.where(imported < 0, code[...], resident + (e * Y + d) * LIMIT + imported % LIMIT)
    column = jnp.transpose(jnp.broadcast_to(at, (8, count)).astype(jnp.float32))[:, :1]
    pair = jnp.concatenate([rows, rows], axis=1)
    high = pair.astype(jnp.bfloat16).astype(jnp.float32)
    low = pair - high
    half = lax.broadcasted_iota(jnp.int32, pair.shape, 1) // rank
    wanted = jnp.broadcast_to(column, pair.shape) - half.astype(jnp.float32)
    both = jnp.concatenate([high, low], axis=0)
    wanted = jnp.concatenate([wanted, wanted], axis=0)
    total = jnp.zeros((2 * count, out.shape[1]), jnp.float32)
    step = 4
    bounds = [resident + e * imported_each for e in range(X + 1)]
    for first in range(0, held.shape[0] // 2, step):
        if first == 0:
            copies[0].wait()
        if 2 * first in bounds:
            copies[1 + bounds.index(2 * first)].wait()
        placed = jnp.concatenate(
            [
                jnp.where(wanted == float(2 * p), both, 0.0).astype(jnp.bfloat16)
                for p in range(first, first + step)
            ],
            axis=1,
        )
        maps = held[2 * first : 2 * (first + step)].reshape(2 * step * rank, out.shape[1])
        total = total + jnp.dot(placed, maps, preferred_element_type=jnp.float32)
    copies[-1].wait()
    out[...] = (base_held[...] + (total[:count] + total[count:])).astype(out.dtype)


def expand(shrink, code, base, up, tables):
    vmem = pl.BlockSpec(memory_space=pltpu.VMEM)
    hbm = pl.BlockSpec(memory_space=pltpu.HBM)
    maps = up.shape[0] + X * tables[0].shape[0]
    return pl.pallas_call(
        expand_kernel,
        out_shape=jax.ShapeDtypeStruct(base.shape, jnp.bfloat16),
        in_specs=[vmem, vmem] + [hbm] * (2 + X),
        out_specs=vmem,
        scratch_shapes=[
            pltpu.VMEM((maps,) + up.shape[1:], up.dtype),
            pltpu.VMEM(base.shape, base.dtype),
            pltpu.SemaphoreType.DMA((2 + X,)),
        ],
    )(shrink, code, base, up, *tables)


def shift(array, axis, size, by):
    return lax.ppermute(array, axis, [(i, (i + by) % size) for i in range(size)])


def shards(inputs, row_adapter_slot, transfer_plan, key_value_weight, adapter_down, adapter_up):
    count = inputs.shape[0]
    resident = adapter_down.shape[0]
    slots = row_adapter_slot.reshape(1, count)

    sent, code = prepare(resident, transfer_plan, slots, inputs)
    rings = [[i * C for i in range(Y)], [i * C + 1 for i in reversed(range(Y))]]
    rows = lax.all_gather(sent, ("y", "c"), axis_index_groups=rings)
    down, picked = dispatch(transfer_plan, adapter_down)
    down = lax.all_to_all(down, "x", 0, 0, tiled=True)

    late, picked = lax.optimization_barrier((inputs, picked))
    base_part = jnp.dot(late, key_value_weight, preferred_element_type=jnp.float32)
    base = lax.psum_scatter(base_part, ("z", "c"), scatter_dimension=1, tiled=True)
    own = local_shrink(code, late, adapter_down)

    ups = pick_up(picked, adapter_up)
    near, far = (1, 7, 2, 6), (3, 5, 4)
    moved = {d: shift(ups[d], "y", Y, d) for d in near}
    moved, later = lax.optimization_barrier((moved, {d: ups[d] for d in far}))
    moved |= {d: shift(later[d], "y", Y, d) for d in far}
    moved[0] = ups[0]
    down, moved = lax.optimization_barrier((down, moved))
    ups = [moved[d] for d in range(Y)]
    ups = turn(ups)
    tables = [ups[0]] + [shift(ups[e], "x", X, e) for e in range(1, X)]

    parts = imported_shrink(resident, rows, down, own)
    parts = add_up(lax.all_to_all(parts, "y", 0, 0, tiled=True), 1)
    parts = add_up(lax.all_to_all(parts.reshape(T, 8, 128), ("z", "c"), 0, 0, tiled=True), T)
    shrink = lax.all_to_all(parts, ("z", "c"), 0, 0, tiled=True)
    return expand(shrink, code, base, adapter_up, tables)


def solution(mesh):
    grid = Mesh(mesh.devices.reshape(Y, X, Z, C), ("y", "x", "z", "c"))
    replica, tensor = ("y", "x"), ("z", "c")
    placed = (
        P(replica, tensor),
        P(replica),
        P(),
        P(tensor, None),
        P(replica, None, tensor),
        P(replica, None, tensor),
    )
    return jax.shard_map(
        shards, mesh=grid, in_specs=placed, out_specs=P(replica, tensor), check_vma=False
    )
```

```python
import functools

import jax
import jax.numpy as jnp
from jax import lax
from jax.experimental import pallas as pl
from jax.experimental.pallas import tpu as pltpu
from jax.sharding import Mesh, PartitionSpec as P

Y, X, Z, C = 8, 4, 8, 2
T = Z * C
GROUPS = Y * X
LIMIT = 2
CODE_ROWS = 16
MIB = 1024 * 1024
NT = (((1,), (1,)), ((), ()))


def spot():
    return lax.axis_index("y"), lax.axis_index("x")


def dispatch_kernel(plan, down, *refs):
    out, picked_out, held, staged, picked, in_sems, out_sems, picked_sem = refs
    resident = down.shape[0]
    y, x = spot()
    pieces = in_sems.shape[0]
    part = resident // pieces

    def read(i):
        rows = pl.ds(i * part, part)
        return pltpu.make_async_copy(down.at[rows], held.at[rows], in_sems.at[i])

    def write(e):
        return pltpu.make_async_copy(staged.at[e], out.at[e], out_sems.at[e])

    for i in range(pieces):
        read(i).start()
    table = plan[...]
    home = table // resident
    number = table - home * resident
    mine = (home == y * X + x).astype(jnp.int32)
    after = jnp.concatenate([jnp.zeros((mine.shape[0], 1), jnp.int32), mine[:, :-1]], axis=1)
    first = jnp.sum(mine * (1 - after) * number, axis=1, keepdims=True)
    second = jnp.sum(mine * after * number, axis=1, keepdims=True)
    lane = lax.broadcasted_iota(jnp.int32, picked_out.shape, 1)
    picked_out[...] = jnp.where(lane == 0, first, jnp.where(lane == 1, second, 0))
    to_scalars = pltpu.make_async_copy(picked_out, picked, picked_sem)
    to_scalars.start()
    to_scalars.wait()
    for i in range(pieces):
        read(i).wait()
    for e in range(X):
        for row in range(Y):
            for j in range(LIMIT):
                staged[e, row * LIMIT + j] = held[picked[row * X + e, j]]
        write(e).start()
    for e in range(X):
        write(e).wait()


def dispatch(plan, down):
    vmem = pl.BlockSpec(memory_space=pltpu.VMEM)
    hbm = pl.BlockSpec(memory_space=pl.ANY)
    shape = (X, Y * LIMIT) + down.shape[1:]
    return pl.pallas_call(
        dispatch_kernel,
        out_shape=(
            jax.ShapeDtypeStruct(shape, down.dtype),
            jax.ShapeDtypeStruct((GROUPS, 128), jnp.int32),
        ),
        in_specs=[vmem, hbm],
        out_specs=(hbm, vmem),
        scratch_shapes=[
            pltpu.VMEM(down.shape, down.dtype),
            pltpu.VMEM(shape, down.dtype),
            pltpu.SMEM((GROUPS, 128), jnp.int32),
            pltpu.SemaphoreType.DMA((4,)),
            pltpu.SemaphoreType.DMA((X,)),
            pltpu.SemaphoreType.DMA,
        ],
        cost_estimate=pl.CostEstimate(flops=0, bytes_accessed=6 * down.size, transcendentals=0),
    )(plan, down)


def prepare_kernel(resident, plan, slots, rows, out, code_out):
    y, x = spot()
    height, width = rows.shape
    slot = slots[...]
    code = slot
    before = jnp.int32(-1)
    for k in range(plan.shape[1]):
        home = plan[y * X + x, k] // resident
        again = (home == before).astype(jnp.int32)
        code = jnp.where(slot == resident + k, resident + home * LIMIT + again, code)
        before = home
    code_out[...] = code
    out[0:height, :] = rows[...]
    wide = jnp.concatenate([code.astype(jnp.float32), jnp.zeros((1, width - height), jnp.float32)], axis=1)
    out[height:, :] = jnp.broadcast_to(wide, (CODE_ROWS, width)).astype(out.dtype)


def prepare(resident, plan, slots, rows):
    height, width = rows.shape
    smem = pl.BlockSpec(memory_space=pltpu.SMEM)
    vmem = pl.BlockSpec(memory_space=pltpu.VMEM)
    return pl.pallas_call(
        functools.partial(prepare_kernel, resident),
        out_shape=(
            jax.ShapeDtypeStruct((height + CODE_ROWS, width), rows.dtype),
            jax.ShapeDtypeStruct(slots.shape, jnp.int32),
        ),
        in_specs=[smem, vmem, vmem],
        out_specs=(vmem, vmem),
        cost_estimate=pl.CostEstimate(flops=0, bytes_accessed=4 * rows.size, transcendentals=0),
    )(plan, slots, rows)


def pick_up_kernel(picked, up, *outs):
    y, _ = spot()
    for d in range(Y):
        row = lax.rem(y + d, Y)
        for x in range(X):
            for j in range(LIMIT):
                outs[d][x * LIMIT + j] = up[picked[row * X + x, j]]


def pick_up(picked, up):
    smem = pl.BlockSpec(memory_space=pltpu.SMEM)
    vmem = pl.BlockSpec(memory_space=pltpu.VMEM)
    return pl.pallas_call(
        pick_up_kernel,
        out_shape=(jax.ShapeDtypeStruct((X * LIMIT,) + up.shape[1:], up.dtype),) * Y,
        in_specs=[smem, vmem],
        out_specs=(vmem,) * Y,
        cost_estimate=pl.CostEstimate(flops=0, bytes_accessed=6 * up.size, transcendentals=0),
    )(picked, up)


def turn_kernel(*refs):
    arrived, outs = refs[:Y], refs[Y:]
    _, x = spot()
    for e in range(X):
        column = lax.rem(x + e, X)
        for d in range(Y):
            for j in range(LIMIT):
                outs[e][d * LIMIT + j] = arrived[d][column * LIMIT + j]


def turn(arrived):
    vmem = pl.BlockSpec(memory_space=pltpu.VMEM)
    shape = jax.ShapeDtypeStruct((Y * LIMIT,) + arrived[0].shape[1:], arrived[0].dtype)
    return pl.pallas_call(
        turn_kernel,
        out_shape=(shape,) * X,
        in_specs=[vmem] * Y,
        out_specs=(vmem,) * X,
        compiler_params=pltpu.CompilerParams(vmem_limit_bytes=6 * MIB),
        cost_estimate=pl.CostEstimate(flops=0, bytes_accessed=4 * Y * arrived[0].size, transcendentals=0),
    )(*arrived)


def local_kernel(code, rows, down, out):
    rank = out.shape[0]
    resident = down.shape[0] // rank
    total = jnp.zeros(out.shape, jnp.float32)
    step = 4
    for first in range(0, resident, step):
        product = lax.dot_general(
            down[first * rank : (first + step) * rank, :], rows[...], NT, preferred_element_type=jnp.float32
        )
        for k in range(step):
            total = total + jnp.where(code[...] == first + k, product[k * rank : (k + 1) * rank, :], 0.0)
    out[...] = total


def local_shrink(code, rows, down):
    resident, rank, width = down.shape
    vmem = pl.BlockSpec(memory_space=pltpu.VMEM)
    return pl.pallas_call(
        local_kernel,
        out_shape=jax.ShapeDtypeStruct((rank, rows.shape[0]), jnp.float32),
        in_specs=[vmem] * 3,
        out_specs=vmem,
        cost_estimate=pl.CostEstimate(
            flops=2 * rows.size * resident * rank, bytes_accessed=2 * down.size, transcendentals=0
        ),
    )(code, rows, down.reshape(resident * rank, width))


def imported_kernel(resident, rows, down, own, out, rows_held, down_held, sems):
    rank, count = own.shape
    lanes = out.shape[-1]
    y, _ = spot()
    odd = lax.axis_index("c")

    def reads(g):
        wanted = pl.ds(g * LIMIT * rank, LIMIT * rank)
        at = g + odd * (Y - 1 - 2 * g)
        pairs = [(rows.at[at], rows_held.at[g])]
        pairs += [(down.at[x, wanted], down_held.at[g, pl.ds(x * LIMIT * rank, LIMIT * rank)]) for x in range(X)]
        return [pltpu.make_async_copy(a, b, sems.at[g, i]) for i, (a, b) in enumerate(pairs)]

    for g in range(Y):
        for read in reads(g):
            read.start()
    base = (resident + y * X * LIMIT).astype(jnp.float32)
    for g in range(Y):
        for read in reads(g):
            read.wait()
        code = rows_held[g, count : count + 1, :count].astype(jnp.float32)
        total = jnp.where(y == g, own[...], 0.0)
        product = lax.dot_general(
            down_held[g], rows_held[g, 0:count, :], NT, preferred_element_type=jnp.float32
        )
        for k in range(X * LIMIT):
            total = total + jnp.where(code == base + k, product[k * rank : (k + 1) * rank, :], 0.0)
        for i in range(rank // 8):
            for k in range(count // lanes):
                out[g, i * (count // lanes) + k] = total[i * 8 : (i + 1) * 8, k * lanes : (k + 1) * lanes]


def imported_shrink(resident, rows, down, own):
    rank, count = own.shape
    height, width = rows.shape[1:]
    blocks = rank * count // 1024
    vmem = pl.BlockSpec(memory_space=pltpu.VMEM)
    hbm = pl.BlockSpec(memory_space=pl.ANY)
    return pl.pallas_call(
        functools.partial(imported_kernel, resident),
        out_shape=jax.ShapeDtypeStruct((Y, blocks, 8, 128), jnp.float32),
        in_specs=[hbm, hbm, vmem],
        out_specs=vmem,
        scratch_shapes=[
            pltpu.VMEM((Y, height, width), rows.dtype),
            pltpu.VMEM((Y, X * LIMIT * rank, width), rows.dtype),
            pltpu.SemaphoreType.DMA((Y, X + 1)),
        ],
        cost_estimate=pl.CostEstimate(
            flops=2 * down.size * count, bytes_accessed=2 * (down.size + rows.size), transcendentals=0
        ),
    )(rows, down.reshape(X, -1, width), own)


def add_kernel(parts, out):
    total = jnp.sum(parts[...], axis=0)
    for t in range(out.shape[0]):
        out[t] = total


def add_and_spread(parts):
    vmem = pl.BlockSpec(memory_space=pltpu.VMEM)
    return pl.pallas_call(
        add_kernel,
        out_shape=jax.ShapeDtypeStruct((T,) + parts.shape[1:], jnp.float32),
        in_specs=[vmem],
        out_specs=vmem,
        compiler_params=pltpu.CompilerParams(vmem_limit_bytes=2 * MIB),
    )(parts)


def expand_kernel(shrink, code, base, up, *refs):
    tables, (out, held, base_held, sems) = refs[:X], refs[X:]
    count = out.shape[0]
    lanes = count // 128
    rank = shrink.shape[0] // lanes * 8
    resident, imported_each = up.shape[0], tables[0].shape[0]
    copies = [pltpu.make_async_copy(up, held.at[pl.ds(0, resident)], sems.at[0])]
    for e in range(X):
        place = pl.ds(resident + e * imported_each, imported_each)
        copies.append(pltpu.make_async_copy(tables[e], held.at[place], sems.at[1 + e]))
    copies.append(pltpu.make_async_copy(base, base_held, sems.at[1 + X]))
    for copy in copies:
        copy.start()
    rows = jnp.concatenate(
        [jnp.concatenate([shrink[i * lanes + k] for k in range(lanes)], axis=1) for i in range(rank // 8)], axis=0
    )
    rows = jnp.transpose(rows)
    y, x = spot()
    imported = code[...] - resident
    home = imported // LIMIT
    e = (x - home % X + X) % X
    d = (y - home // X + Y) % Y
    at = jnp.where(imported < 0, code[...], resident + (e * Y + d) * LIMIT + imported % LIMIT)
    column = jnp.transpose(jnp.broadcast_to(at, (8, count)).astype(jnp.float32))[:, :1]
    pair = jnp.concatenate([rows, rows], axis=1)
    high = pair.astype(jnp.bfloat16).astype(jnp.float32)
    low = pair - high
    half = lax.broadcasted_iota(jnp.int32, pair.shape, 1) // rank
    wanted = jnp.broadcast_to(column, pair.shape) - half.astype(jnp.float32)
    both = jnp.concatenate([high, low], axis=0)
    wanted = jnp.concatenate([wanted, wanted], axis=0)
    total = jnp.zeros((2 * count, out.shape[1]), jnp.float32)
    step = 4
    bounds = [resident + e * imported_each for e in range(X + 1)]
    for first in range(0, held.shape[0] // 2, step):
        if first == 0:
            copies[0].wait()
        if 2 * first in bounds:
            copies[1 + bounds.index(2 * first)].wait()
        placed = jnp.concatenate(
            [
                jnp.where(wanted == float(2 * p), both, 0.0).astype(jnp.bfloat16)
                for p in range(first, first + step)
            ],
            axis=1,
        )
        maps = held[2 * first : 2 * (first + step)].reshape(2 * step * rank, out.shape[1])
        total = total + jnp.dot(placed, maps, preferred_element_type=jnp.float32)
    copies[-1].wait()
    out[...] = (base_held[...] + (total[:count] + total[count:])).astype(out.dtype)


def expand(shrink, code, base, up, tables):
    vmem = pl.BlockSpec(memory_space=pltpu.VMEM)
    hbm = pl.BlockSpec(memory_space=pltpu.HBM)
    maps = up.shape[0] + X * tables[0].shape[0]
    return pl.pallas_call(
        expand_kernel,
        out_shape=jax.ShapeDtypeStruct(base.shape, jnp.bfloat16),
        in_specs=[vmem, vmem] + [hbm] * (2 + X),
        out_specs=vmem,
        scratch_shapes=[
            pltpu.VMEM((maps,) + up.shape[1:], up.dtype),
            pltpu.VMEM(base.shape, base.dtype),
            pltpu.SemaphoreType.DMA((2 + X,)),
        ],
    )(shrink, code, base, up, *tables)


def shift(array, axis, size, by):
    return lax.ppermute(array, axis, [(i, (i + by) % size) for i in range(size)])


def shards(inputs, row_adapter_slot, transfer_plan, key_value_weight, adapter_down, adapter_up):
    count = inputs.shape[0]
    resident = adapter_down.shape[0]
    slots = row_adapter_slot.reshape(1, count)

    sent, code = prepare(resident, transfer_plan, slots, inputs)
    rings = [[i * C for i in range(Y)], [i * C + 1 for i in reversed(range(Y))]]
    rows = lax.all_gather(sent, ("y", "c"), axis_index_groups=rings)
    down, picked = dispatch(transfer_plan, adapter_down)
    down = lax.all_to_all(down, "x", 0, 0, tiled=True)

    late, picked = lax.optimization_barrier((inputs, picked))
    base_part = jnp.dot(late, key_value_weight, preferred_element_type=jnp.float32)
    base = lax.psum_scatter(base_part, ("z", "c"), scatter_dimension=1, tiled=True)
    own = local_shrink(code, late, adapter_down)

    ups = pick_up(picked, adapter_up)
    near, far, last = (1, 7, 2, 6), (3, 5), Y // 2
    moved = {d: shift(ups[d], "y", Y, d) for d in near}
    moved, later = lax.optimization_barrier((moved, {d: ups[d] for d in far}))
    moved |= {d: shift(later[d], "y", Y, d) for d in far}
    down, moved, later = lax.optimization_barrier((down, moved, ups[last]))
    moved |= {0: ups[0], last: shift(later, "y", Y, last)}
    ups = [moved[d] for d in range(Y)]
    ups = turn(ups)
    tables = [ups[0]] + [shift(ups[e], "x", X, e) for e in range(1, X)]

    parts = imported_shrink(resident, rows, down, own)
    parts = lax.all_to_all(parts.reshape(Y * T, 8, 128), ("y", "z", "c"), 0, 0, tiled=True)
    shrink = lax.all_to_all(add_and_spread(parts), ("z", "c"), 0, 0, tiled=True)
    return expand(shrink, code, base, adapter_up, tables)


def solution(mesh):
    grid = Mesh(mesh.devices.reshape(Y, X, Z, C), ("y", "x", "z", "c"))
    replica, tensor = ("y", "x"), ("z", "c")
    placed = (
        P(replica, tensor),
        P(replica),
        P(),
        P(tensor, None),
        P(replica, None, tensor),
        P(replica, None, tensor),
    )
    return jax.shard_map(
        shards, mesh=grid, in_specs=placed, out_specs=P(replica, tensor), check_vma=False
    )
```

```python
import functools

import jax
import jax.numpy as jnp
from jax import lax
from jax.experimental import pallas as pl
from jax.experimental.pallas import tpu as pltpu
from jax.sharding import Mesh, PartitionSpec as P

Y, X, Z, C = 8, 4, 8, 2
T = Z * C
GROUPS = Y * X
LIMIT = 2
CODE_ROWS = 16
MIB = 1024 * 1024
NT = (((1,), (1,)), ((), ()))


def spot():
    return lax.axis_index("y"), lax.axis_index("x")


def dispatch_kernel(plan, down, *refs):
    out, picked_out, held, staged, picked, in_sems, out_sems, picked_sem = refs
    resident = down.shape[0]
    y, x = spot()
    pieces = in_sems.shape[0]
    part = resident // pieces

    def read(i):
        rows = pl.ds(i * part, part)
        return pltpu.make_async_copy(down.at[rows], held.at[rows], in_sems.at[i])

    def write(e):
        return pltpu.make_async_copy(staged.at[e], out.at[e], out_sems.at[e])

    for i in range(pieces):
        read(i).start()
    table = plan[...]
    home = table // resident
    number = table - home * resident
    mine = (home == y * X + x).astype(jnp.int32)
    after = jnp.concatenate([jnp.zeros((mine.shape[0], 1), jnp.int32), mine[:, :-1]], axis=1)
    first = jnp.sum(mine * (1 - after) * number, axis=1, keepdims=True)
    second = jnp.sum(mine * after * number, axis=1, keepdims=True)
    lane = lax.broadcasted_iota(jnp.int32, picked_out.shape, 1)
    picked_out[...] = jnp.where(lane == 0, first, jnp.where(lane == 1, second, 0))
    to_scalars = pltpu.make_async_copy(picked_out, picked, picked_sem)
    to_scalars.start()
    to_scalars.wait()
    for i in range(pieces):
        read(i).wait()
    for e in range(X):
        for row in range(Y):
            for j in range(LIMIT):
                staged[e, row * LIMIT + j] = held[picked[row * X + e, j]]
        write(e).start()
    for e in range(X):
        write(e).wait()


def dispatch(plan, down):
    vmem = pl.BlockSpec(memory_space=pltpu.VMEM)
    hbm = pl.BlockSpec(memory_space=pl.ANY)
    shape = (X, Y * LIMIT) + down.shape[1:]
    return pl.pallas_call(
        dispatch_kernel,
        out_shape=(
            jax.ShapeDtypeStruct(shape, down.dtype),
            jax.ShapeDtypeStruct((GROUPS, 128), jnp.int32),
        ),
        in_specs=[vmem, hbm],
        out_specs=(hbm, vmem),
        scratch_shapes=[
            pltpu.VMEM(down.shape, down.dtype),
            pltpu.VMEM(shape, down.dtype),
            pltpu.SMEM((GROUPS, 128), jnp.int32),
            pltpu.SemaphoreType.DMA((4,)),
            pltpu.SemaphoreType.DMA((X,)),
            pltpu.SemaphoreType.DMA,
        ],
        cost_estimate=pl.CostEstimate(flops=0, bytes_accessed=6 * down.size, transcendentals=0),
    )(plan, down)


def prepare_kernel(resident, plan, slots, rows, out, code_out):
    y, x = spot()
    height, width = rows.shape
    slot = slots[...]
    code = slot
    before = jnp.int32(-1)
    for k in range(plan.shape[1]):
        home = plan[y * X + x, k] // resident
        again = (home == before).astype(jnp.int32)
        code = jnp.where(slot == resident + k, resident + home * LIMIT + again, code)
        before = home
    code_out[...] = code
    out[0:height, :] = rows[...]
    wide = jnp.concatenate([code.astype(jnp.float32), jnp.zeros((1, width - height), jnp.float32)], axis=1)
    out[height:, :] = jnp.broadcast_to(wide, (CODE_ROWS, width)).astype(out.dtype)


def prepare(resident, plan, slots, rows):
    height, width = rows.shape
    smem = pl.BlockSpec(memory_space=pltpu.SMEM)
    vmem = pl.BlockSpec(memory_space=pltpu.VMEM)
    return pl.pallas_call(
        functools.partial(prepare_kernel, resident),
        out_shape=(
            jax.ShapeDtypeStruct((height + CODE_ROWS, width), rows.dtype),
            jax.ShapeDtypeStruct(slots.shape, jnp.int32),
        ),
        in_specs=[smem, vmem, vmem],
        out_specs=(vmem, vmem),
        cost_estimate=pl.CostEstimate(flops=0, bytes_accessed=4 * rows.size, transcendentals=0),
    )(plan, slots, rows)


def pick_up_kernel(picked, up, *outs):
    y, _ = spot()
    for d in range(Y):
        row = lax.rem(y + d, Y)
        for x in range(X):
            for j in range(LIMIT):
                outs[d][x * LIMIT + j] = up[picked[row * X + x, j]]


def pick_up(picked, up):
    smem = pl.BlockSpec(memory_space=pltpu.SMEM)
    vmem = pl.BlockSpec(memory_space=pltpu.VMEM)
    return pl.pallas_call(
        pick_up_kernel,
        out_shape=(jax.ShapeDtypeStruct((X * LIMIT,) + up.shape[1:], up.dtype),) * Y,
        in_specs=[smem, vmem],
        out_specs=(vmem,) * Y,
        cost_estimate=pl.CostEstimate(flops=0, bytes_accessed=6 * up.size, transcendentals=0),
    )(picked, up)


def turn_kernel(*refs):
    arrived, outs = refs[:Y], refs[Y:]
    _, x = spot()
    for e in range(X):
        column = lax.rem(x + e, X)
        for d in range(Y):
            for j in range(LIMIT):
                outs[e][d * LIMIT + j] = arrived[d][column * LIMIT + j]


def turn(arrived):
    vmem = pl.BlockSpec(memory_space=pltpu.VMEM)
    shape = jax.ShapeDtypeStruct((Y * LIMIT,) + arrived[0].shape[1:], arrived[0].dtype)
    return pl.pallas_call(
        turn_kernel,
        out_shape=(shape,) * X,
        in_specs=[vmem] * Y,
        out_specs=(vmem,) * X,
        compiler_params=pltpu.CompilerParams(vmem_limit_bytes=6 * MIB),
        cost_estimate=pl.CostEstimate(flops=0, bytes_accessed=4 * Y * arrived[0].size, transcendentals=0),
    )(*arrived)


def local_kernel(code, rows, down, out):
    rank = out.shape[0]
    resident = down.shape[0] // rank
    total = jnp.zeros(out.shape, jnp.float32)
    step = 4
    for first in range(0, resident, step):
        product = lax.dot_general(
            down[first * rank : (first + step) * rank, :], rows[...], NT, preferred_element_type=jnp.float32
        )
        for k in range(step):
            total = total + jnp.where(code[...] == first + k, product[k * rank : (k + 1) * rank, :], 0.0)
    out[...] = total


def local_shrink(code, rows, down):
    resident, rank, width = down.shape
    vmem = pl.BlockSpec(memory_space=pltpu.VMEM)
    return pl.pallas_call(
        local_kernel,
        out_shape=jax.ShapeDtypeStruct((rank, rows.shape[0]), jnp.float32),
        in_specs=[vmem] * 3,
        out_specs=vmem,
        cost_estimate=pl.CostEstimate(
            flops=2 * rows.size * resident * rank, bytes_accessed=2 * down.size, transcendentals=0
        ),
    )(code, rows, down.reshape(resident * rank, width))


def imported_kernel(resident, rows, down, own, out, rows_held, down_held, sems):
    rank, count = own.shape
    lanes = out.shape[-1]
    y, _ = spot()
    odd = lax.axis_index("c")

    def reads(g):
        wanted = pl.ds(g * LIMIT * rank, LIMIT * rank)
        at = g + odd * (Y - 1 - 2 * g)
        pairs = [(rows.at[at], rows_held.at[g])]
        pairs += [(down.at[x, wanted], down_held.at[g, pl.ds(x * LIMIT * rank, LIMIT * rank)]) for x in range(X)]
        return [pltpu.make_async_copy(a, b, sems.at[g, i]) for i, (a, b) in enumerate(pairs)]

    for g in range(Y):
        for read in reads(g):
            read.start()
    base = (resident + y * X * LIMIT).astype(jnp.float32)
    for g in range(Y):
        for read in reads(g):
            read.wait()
        code = rows_held[g, count : count + 1, :count].astype(jnp.float32)
        total = jnp.where(y == g, own[...], 0.0)
        product = lax.dot_general(
            down_held[g], rows_held[g, 0:count, :], NT, preferred_element_type=jnp.float32
        )
        for k in range(X * LIMIT):
            total = total + jnp.where(code == base + k, product[k * rank : (k + 1) * rank, :], 0.0)
        for i in range(rank // 8):
            for k in range(count // lanes):
                out[g, i * (count // lanes) + k] = total[i * 8 : (i + 1) * 8, k * lanes : (k + 1) * lanes]


def imported_shrink(resident, rows, down, own):
    rank, count = own.shape
    height, width = rows.shape[1:]
    blocks = rank * count // 1024
    vmem = pl.BlockSpec(memory_space=pltpu.VMEM)
    hbm = pl.BlockSpec(memory_space=pl.ANY)
    return pl.pallas_call(
        functools.partial(imported_kernel, resident),
        out_shape=jax.ShapeDtypeStruct((Y, blocks, 8, 128), jnp.float32),
        in_specs=[hbm, hbm, vmem],
        out_specs=vmem,
        scratch_shapes=[
            pltpu.VMEM((Y, height, width), rows.dtype),
            pltpu.VMEM((Y, X * LIMIT * rank, width), rows.dtype),
            pltpu.SemaphoreType.DMA((Y, X + 1)),
        ],
        cost_estimate=pl.CostEstimate(
            flops=2 * down.size * count, bytes_accessed=2 * (down.size + rows.size), transcendentals=0
        ),
    )(rows, down.reshape(X, -1, width), own)


def add_kernel(parts, out):
    total = jnp.sum(parts[...], axis=0)
    for t in range(out.shape[0]):
        out[t] = total


def add_and_spread(parts):
    vmem = pl.BlockSpec(memory_space=pltpu.VMEM)
    return pl.pallas_call(
        add_kernel,
        out_shape=jax.ShapeDtypeStruct((T,) + parts.shape[1:], jnp.float32),
        in_specs=[vmem],
        out_specs=vmem,
        compiler_params=pltpu.CompilerParams(vmem_limit_bytes=2 * MIB),
    )(parts)


def expand_kernel(shrink, code, base, up, *refs):
    tables, (out, held, base_held, sems) = refs[:X], refs[X:]
    count = out.shape[0]
    lanes = count // 128
    rank = shrink.shape[0] // lanes * 8
    resident, imported_each = up.shape[0], tables[0].shape[0]
    copies = [pltpu.make_async_copy(up, held.at[pl.ds(0, resident)], sems.at[0])]
    for e in range(X):
        place = pl.ds(resident + e * imported_each, imported_each)
        copies.append(pltpu.make_async_copy(tables[e], held.at[place], sems.at[1 + e]))
    copies.append(pltpu.make_async_copy(base, base_held, sems.at[1 + X]))
    for copy in copies:
        copy.start()
    rows = jnp.concatenate(
        [jnp.concatenate([shrink[i * lanes + k] for k in range(lanes)], axis=1) for i in range(rank // 8)], axis=0
    )
    rows = jnp.transpose(rows)
    y, x = spot()
    imported = code[...] - resident
    home = imported // LIMIT
    e = (x - home % X + X) % X
    d = (y - home // X + Y) % Y
    at = jnp.where(imported < 0, code[...], resident + (e * Y + d) * LIMIT + imported % LIMIT)
    column = jnp.transpose(jnp.broadcast_to(at, (8, count)).astype(jnp.float32))[:, :1]
    pair = jnp.concatenate([rows, rows], axis=1)
    high = pair.astype(jnp.bfloat16).astype(jnp.float32)
    low = pair - high
    half = lax.broadcasted_iota(jnp.int32, pair.shape, 1) // rank
    wanted = jnp.broadcast_to(column, pair.shape) - half.astype(jnp.float32)
    both = jnp.concatenate([high, low], axis=0)
    wanted = jnp.concatenate([wanted, wanted], axis=0)
    total = jnp.zeros((2 * count, out.shape[1]), jnp.float32)
    step = 4
    bounds = [resident + e * imported_each for e in range(X + 1)]
    for first in range(0, held.shape[0] // 2, step):
        if first == 0:
            copies[0].wait()
        if 2 * first in bounds:
            copies[1 + bounds.index(2 * first)].wait()
        placed = jnp.concatenate(
            [
                jnp.where(wanted == float(2 * p), both, 0.0).astype(jnp.bfloat16)
                for p in range(first, first + step)
            ],
            axis=1,
        )
        maps = held[2 * first : 2 * (first + step)].reshape(2 * step * rank, out.shape[1])
        total = total + jnp.dot(placed, maps, preferred_element_type=jnp.float32)
    copies[-1].wait()
    out[...] = (base_held[...] + (total[:count] + total[count:])).astype(out.dtype)


def expand(shrink, code, base, up, tables):
    vmem = pl.BlockSpec(memory_space=pltpu.VMEM)
    hbm = pl.BlockSpec(memory_space=pltpu.HBM)
    maps = up.shape[0] + X * tables[0].shape[0]
    return pl.pallas_call(
        expand_kernel,
        out_shape=jax.ShapeDtypeStruct(base.shape, jnp.bfloat16),
        in_specs=[vmem, vmem] + [hbm] * (2 + X),
        out_specs=vmem,
        scratch_shapes=[
            pltpu.VMEM((maps,) + up.shape[1:], up.dtype),
            pltpu.VMEM(base.shape, base.dtype),
            pltpu.SemaphoreType.DMA((2 + X,)),
        ],
    )(shrink, code, base, up, *tables)


def shift(array, axis, size, by):
    return lax.ppermute(array, axis, [(i, (i + by) % size) for i in range(size)])


def shards(inputs, row_adapter_slot, transfer_plan, key_value_weight, adapter_down, adapter_up):
    count = inputs.shape[0]
    resident = adapter_down.shape[0]
    slots = row_adapter_slot.reshape(1, count)

    sent, code = prepare(resident, transfer_plan, slots, inputs)
    rings = [[i * C for i in range(Y)], [i * C + 1 for i in reversed(range(Y))]]
    rows = lax.all_gather(sent, ("y", "c"), axis_index_groups=rings)
    down, picked = dispatch(transfer_plan, adapter_down)
    down = lax.all_to_all(down, "x", 0, 0, tiled=True)

    late, picked = lax.optimization_barrier((inputs, picked))
    base_part = jnp.dot(late, key_value_weight, preferred_element_type=jnp.float32)
    base = lax.psum_scatter(base_part, ("z", "c"), scatter_dimension=1, tiled=True)
    own = local_shrink(code, late, adapter_down)

    ups = pick_up(picked, adapter_up)
    near, far = (1, 7, 2, 6), (4, 3, 5)
    moved = [shift(ups[d], "y", Y, d) for d in near]
    moved, later = lax.optimization_barrier((moved, [ups[d] for d in far]))
    moved_far = [shift(ups_d, "y", Y, d) for ups_d, d in zip(later, far)]
    down, moved = lax.optimization_barrier((down, moved))
    parts = imported_shrink(resident, rows, down, own)
    parts, moved_far = lax.optimization_barrier((parts, moved_far))
    moved = dict(zip(near + far, moved + moved_far)) | {0: ups[0]}
    ups = turn([moved[d] for d in range(Y)])
    tables = [ups[0]] + [shift(ups[e], "x", X, e) for e in range(1, X)]

    parts = lax.all_to_all(parts.reshape(Y * T, 8, 128), ("y", "z", "c"), 0, 0, tiled=True)
    shrink = lax.all_to_all(add_and_spread(parts), ("z", "c"), 0, 0, tiled=True)
    return expand(shrink, code, base, adapter_up, tables)


def solution(mesh):
    grid = Mesh(mesh.devices.reshape(Y, X, Z, C), ("y", "x", "z", "c"))
    replica, tensor = ("y", "x"), ("z", "c")
    placed = (
        P(replica, tensor),
        P(replica),
        P(),
        P(tensor, None),
        P(replica, None, tensor),
        P(replica, None, tensor),
    )
    return jax.shard_map(
        shards, mesh=grid, in_specs=placed, out_specs=P(replica, tensor), check_vma=False
    )
```

```python
import functools

import jax
import jax.numpy as jnp
from jax import lax
from jax.experimental import pallas as pl
from jax.experimental.pallas import tpu as pltpu
from jax.sharding import Mesh, PartitionSpec as P

Y, X, Z, C = 8, 4, 8, 2
T = Z * C
GROUPS = Y * X
LIMIT = 2
CODE_ROWS = 16
MIB = 1024 * 1024
NT = (((1,), (1,)), ((), ()))


def spot():
    return lax.axis_index("y"), lax.axis_index("x")


def dispatch_kernel(plan, down, *refs):
    out, picked_out, held, staged, picked, in_sems, out_sems, picked_sem = refs
    resident = down.shape[0]
    y, x = spot()
    pieces = in_sems.shape[0]
    part = resident // pieces

    def read(i):
        rows = pl.ds(i * part, part)
        return pltpu.make_async_copy(down.at[rows], held.at[rows], in_sems.at[i])

    def write(e):
        return pltpu.make_async_copy(staged.at[e], out.at[e], out_sems.at[e])

    for i in range(pieces):
        read(i).start()
    table = plan[...]
    home = table // resident
    number = table - home * resident
    mine = (home == y * X + x).astype(jnp.int32)
    after = jnp.concatenate([jnp.zeros((mine.shape[0], 1), jnp.int32), mine[:, :-1]], axis=1)
    first = jnp.sum(mine * (1 - after) * number, axis=1, keepdims=True)
    second = jnp.sum(mine * after * number, axis=1, keepdims=True)
    lane = lax.broadcasted_iota(jnp.int32, picked_out.shape, 1)
    picked_out[...] = jnp.where(lane == 0, first, jnp.where(lane == 1, second, 0))
    to_scalars = pltpu.make_async_copy(picked_out, picked, picked_sem)
    to_scalars.start()
    to_scalars.wait()
    for i in range(pieces):
        read(i).wait()
    for e in range(X):
        for row in range(Y):
            for j in range(LIMIT):
                staged[e, row * LIMIT + j] = held[picked[row * X + e, j]]
        write(e).start()
    for e in range(X):
        write(e).wait()


def dispatch(plan, down):
    vmem = pl.BlockSpec(memory_space=pltpu.VMEM)
    hbm = pl.BlockSpec(memory_space=pl.ANY)
    shape = (X, Y * LIMIT) + down.shape[1:]
    return pl.pallas_call(
        dispatch_kernel,
        out_shape=(
            jax.ShapeDtypeStruct(shape, down.dtype),
            jax.ShapeDtypeStruct((GROUPS, 128), jnp.int32),
        ),
        in_specs=[vmem, hbm],
        out_specs=(hbm, vmem),
        scratch_shapes=[
            pltpu.VMEM(down.shape, down.dtype),
            pltpu.VMEM(shape, down.dtype),
            pltpu.SMEM((GROUPS, 128), jnp.int32),
            pltpu.SemaphoreType.DMA((4,)),
            pltpu.SemaphoreType.DMA((X,)),
            pltpu.SemaphoreType.DMA,
        ],
        cost_estimate=pl.CostEstimate(flops=0, bytes_accessed=6 * down.size, transcendentals=0),
    )(plan, down)


def prepare_kernel(resident, plan, slots, rows, out, code_out):
    y, x = spot()
    height, width = rows.shape
    slot = slots[...]
    code = slot
    before = jnp.int32(-1)
    for k in range(plan.shape[1]):
        home = plan[y * X + x, k] // resident
        again = (home == before).astype(jnp.int32)
        code = jnp.where(slot == resident + k, resident + home * LIMIT + again, code)
        before = home
    code_out[...] = code
    out[0:height, :] = rows[...]
    wide = jnp.concatenate([code.astype(jnp.float32), jnp.zeros((1, width - height), jnp.float32)], axis=1)
    out[height:, :] = jnp.broadcast_to(wide, (CODE_ROWS, width)).astype(out.dtype)


def prepare(resident, plan, slots, rows):
    height, width = rows.shape
    smem = pl.BlockSpec(memory_space=pltpu.SMEM)
    vmem = pl.BlockSpec(memory_space=pltpu.VMEM)
    return pl.pallas_call(
        functools.partial(prepare_kernel, resident),
        out_shape=(
            jax.ShapeDtypeStruct((height + CODE_ROWS, width), rows.dtype),
            jax.ShapeDtypeStruct(slots.shape, jnp.int32),
        ),
        in_specs=[smem, vmem, vmem],
        out_specs=(vmem, vmem),
        cost_estimate=pl.CostEstimate(flops=0, bytes_accessed=4 * rows.size, transcendentals=0),
    )(plan, slots, rows)


def pick_up_kernel(picked, up, *outs):
    y, _ = spot()
    for d in range(Y):
        row = lax.rem(y + d, Y)
        for x in range(X):
            for j in range(LIMIT):
                outs[d][x * LIMIT + j] = up[picked[row * X + x, j]]


def pick_up(picked, up):
    smem = pl.BlockSpec(memory_space=pltpu.SMEM)
    vmem = pl.BlockSpec(memory_space=pltpu.VMEM)
    return pl.pallas_call(
        pick_up_kernel,
        out_shape=(jax.ShapeDtypeStruct((X * LIMIT,) + up.shape[1:], up.dtype),) * Y,
        in_specs=[smem, vmem],
        out_specs=(vmem,) * Y,
        cost_estimate=pl.CostEstimate(flops=0, bytes_accessed=6 * up.size, transcendentals=0),
    )(picked, up)


def turn_kernel(*refs):
    arrived, outs = refs[:Y], refs[Y:]
    _, x = spot()
    for e in range(X):
        column = lax.rem(x + e, X)
        for d in range(Y):
            for j in range(LIMIT):
                outs[e][d * LIMIT + j] = arrived[d][column * LIMIT + j]


def turn(arrived):
    vmem = pl.BlockSpec(memory_space=pltpu.VMEM)
    shape = jax.ShapeDtypeStruct((Y * LIMIT,) + arrived[0].shape[1:], arrived[0].dtype)
    return pl.pallas_call(
        turn_kernel,
        out_shape=(shape,) * X,
        in_specs=[vmem] * Y,
        out_specs=(vmem,) * X,
        compiler_params=pltpu.CompilerParams(vmem_limit_bytes=6 * MIB),
        cost_estimate=pl.CostEstimate(flops=0, bytes_accessed=4 * Y * arrived[0].size, transcendentals=0),
    )(*arrived)


def local_kernel(code, rows, down, out):
    rank = out.shape[0]
    resident = down.shape[0] // rank
    total = jnp.zeros(out.shape, jnp.float32)
    step = 4
    for first in range(0, resident, step):
        product = lax.dot_general(
            down[first * rank : (first + step) * rank, :], rows[...], NT, preferred_element_type=jnp.float32
        )
        for k in range(step):
            total = total + jnp.where(code[...] == first + k, product[k * rank : (k + 1) * rank, :], 0.0)
    out[...] = total


def local_shrink(code, rows, down):
    resident, rank, width = down.shape
    vmem = pl.BlockSpec(memory_space=pltpu.VMEM)
    return pl.pallas_call(
        local_kernel,
        out_shape=jax.ShapeDtypeStruct((rank, rows.shape[0]), jnp.float32),
        in_specs=[vmem] * 3,
        out_specs=vmem,
        cost_estimate=pl.CostEstimate(
            flops=2 * rows.size * resident * rank, bytes_accessed=2 * down.size, transcendentals=0
        ),
    )(code, rows, down.reshape(resident * rank, width))


def imported_kernel(resident, rows, down, own, out, rows_held, down_held, sems):
    rank, count = own.shape
    lanes = out.shape[-1]
    y, _ = spot()
    odd = lax.axis_index("c")

    def reads(g):
        wanted = pl.ds(g * LIMIT * rank, LIMIT * rank)
        at = g + odd * (Y - 1 - 2 * g)
        pairs = [(rows.at[at], rows_held.at[g])]
        pairs += [(down.at[x, wanted], down_held.at[g, pl.ds(x * LIMIT * rank, LIMIT * rank)]) for x in range(X)]
        return [pltpu.make_async_copy(a, b, sems.at[g, i]) for i, (a, b) in enumerate(pairs)]

    for g in range(Y):
        for read in reads(g):
            read.start()
    base = (resident + y * X * LIMIT).astype(jnp.float32)
    for g in range(Y):
        for read in reads(g):
            read.wait()
        code = rows_held[g, count : count + 1, :count].astype(jnp.float32)
        total = jnp.where(y == g, own[...], 0.0)
        product = lax.dot_general(
            down_held[g], rows_held[g, 0:count, :], NT, preferred_element_type=jnp.float32
        )
        for k in range(X * LIMIT):
            total = total + jnp.where(code == base + k, product[k * rank : (k + 1) * rank, :], 0.0)
        for i in range(rank // 8):
            for k in range(count // lanes):
                out[g, i * (count // lanes) + k] = total[i * 8 : (i + 1) * 8, k * lanes : (k + 1) * lanes]


def imported_shrink(resident, rows, down, own):
    rank, count = own.shape
    height, width = rows.shape[1:]
    blocks = rank * count // 1024
    vmem = pl.BlockSpec(memory_space=pltpu.VMEM)
    hbm = pl.BlockSpec(memory_space=pl.ANY)
    return pl.pallas_call(
        functools.partial(imported_kernel, resident),
        out_shape=jax.ShapeDtypeStruct((Y, blocks, 8, 128), jnp.float32),
        in_specs=[hbm, hbm, vmem],
        out_specs=vmem,
        scratch_shapes=[
            pltpu.VMEM((Y, height, width), rows.dtype),
            pltpu.VMEM((Y, X * LIMIT * rank, width), rows.dtype),
            pltpu.SemaphoreType.DMA((Y, X + 1)),
        ],
        cost_estimate=pl.CostEstimate(
            flops=2 * down.size * count, bytes_accessed=2 * (down.size + rows.size), transcendentals=0
        ),
    )(rows, down.reshape(X, -1, width), own)


def add_kernel(parts, out):
    total = jnp.sum(parts[...], axis=0)
    for t in range(out.shape[0]):
        out[t] = total


def add_and_spread(parts):
    vmem = pl.BlockSpec(memory_space=pltpu.VMEM)
    return pl.pallas_call(
        add_kernel,
        out_shape=jax.ShapeDtypeStruct((T,) + parts.shape[1:], jnp.float32),
        in_specs=[vmem],
        out_specs=vmem,
        compiler_params=pltpu.CompilerParams(vmem_limit_bytes=2 * MIB),
    )(parts)


def expand_kernel(shrink, code, base, up, *refs):
    tables, (out, held, base_held, sems) = refs[:X], refs[X:]
    count = out.shape[0]
    lanes = count // 128
    rank = shrink.shape[0] // lanes * 8
    resident, imported_each = up.shape[0], tables[0].shape[0]
    copies = [pltpu.make_async_copy(up, held.at[pl.ds(0, resident)], sems.at[0])]
    for e in range(X):
        place = pl.ds(resident + e * imported_each, imported_each)
        copies.append(pltpu.make_async_copy(tables[e], held.at[place], sems.at[1 + e]))
    copies.append(pltpu.make_async_copy(base, base_held, sems.at[1 + X]))
    for copy in copies:
        copy.start()
    rows = jnp.concatenate(
        [jnp.concatenate([shrink[i * lanes + k] for k in range(lanes)], axis=1) for i in range(rank // 8)], axis=0
    )
    rows = jnp.transpose(rows)
    y, x = spot()
    imported = code[...] - resident
    home = imported // LIMIT
    e = (x - home % X + X) % X
    d = (y - home // X + Y) % Y
    at = jnp.where(imported < 0, code[...], resident + (e * Y + d) * LIMIT + imported % LIMIT)
    column = jnp.transpose(jnp.broadcast_to(at, (8, count)).astype(jnp.float32))[:, :1]
    pair = jnp.concatenate([rows, rows], axis=1)
    high = pair.astype(jnp.bfloat16)
    low = (pair - high.astype(jnp.float32)).astype(jnp.bfloat16)
    half = lax.broadcasted_iota(jnp.int32, pair.shape, 1) // rank
    wanted = (jnp.broadcast_to(column, pair.shape) - half.astype(jnp.float32)).astype(jnp.bfloat16)
    nothing = jnp.zeros(pair.shape, jnp.bfloat16)
    total = jnp.zeros((2 * count, out.shape[1]), jnp.float32)
    step = 4
    bounds = [resident + e * imported_each for e in range(X + 1)]
    for first in range(0, held.shape[0] // 2, step):
        if first == 0:
            copies[0].wait()
        if 2 * first in bounds:
            copies[1 + bounds.index(2 * first)].wait()
        hits = [wanted == jnp.bfloat16(2 * p) for p in range(first, first + step)]
        placed = jnp.concatenate(
            [
                jnp.concatenate([jnp.where(hit, part, nothing) for hit in hits], axis=1)
                for part in (high, low)
            ],
            axis=0,
        )
        maps = held[2 * first : 2 * (first + step)].reshape(2 * step * rank, out.shape[1])
        total = total + jnp.dot(placed, maps, preferred_element_type=jnp.float32)
    copies[-1].wait()
    out[...] = (base_held[...] + (total[:count] + total[count:])).astype(out.dtype)


def expand(shrink, code, base, up, tables):
    vmem = pl.BlockSpec(memory_space=pltpu.VMEM)
    hbm = pl.BlockSpec(memory_space=pltpu.HBM)
    maps = up.shape[0] + X * tables[0].shape[0]
    return pl.pallas_call(
        expand_kernel,
        out_shape=jax.ShapeDtypeStruct(base.shape, jnp.bfloat16),
        in_specs=[vmem, vmem] + [hbm] * (2 + X),
        out_specs=vmem,
        scratch_shapes=[
            pltpu.VMEM((maps,) + up.shape[1:], up.dtype),
            pltpu.VMEM(base.shape, base.dtype),
            pltpu.SemaphoreType.DMA((2 + X,)),
        ],
    )(shrink, code, base, up, *tables)


def shift(array, axis, size, by):
    return lax.ppermute(array, axis, [(i, (i + by) % size) for i in range(size)])


def shards(inputs, row_adapter_slot, transfer_plan, key_value_weight, adapter_down, adapter_up):
    count = inputs.shape[0]
    resident = adapter_down.shape[0]
    slots = row_adapter_slot.reshape(1, count)

    sent, code = prepare(resident, transfer_plan, slots, inputs)
    rings = [[i * C for i in range(Y)], [i * C + 1 for i in reversed(range(Y))]]
    rows = lax.all_gather(sent, ("y", "c"), axis_index_groups=rings)
    down, picked = dispatch(transfer_plan, adapter_down)
    down = lax.all_to_all(down, "x", 0, 0, tiled=True)

    late, picked = lax.optimization_barrier((inputs, picked))
    base_part = jnp.dot(late, key_value_weight, preferred_element_type=jnp.float32)
    base = lax.psum_scatter(base_part, ("z", "c"), scatter_dimension=1, tiled=True)
    own = local_shrink(code, late, adapter_down)

    ups = pick_up(picked, adapter_up)
    near, far = (1, 7, 2, 6), (4, 3, 5)
    moved = [shift(ups[d], "y", Y, d) for d in near]
    moved, later, own = lax.optimization_barrier((moved, [ups[d] for d in far], own))
    moved_far = [shift(ups_d, "y", Y, d) for ups_d, d in zip(later, far)]
    down, moved = lax.optimization_barrier((down, moved))
    parts = imported_shrink(resident, rows, down, own)
    parts, moved_far = lax.optimization_barrier((parts, moved_far))
    moved = dict(zip(near + far, moved + moved_far)) | {0: ups[0]}
    ups = turn([moved[d] for d in range(Y)])
    tables = [ups[0]] + [shift(ups[e], "x", X, e) for e in range(1, X)]

    parts = lax.all_to_all(parts.reshape(Y * T, 8, 128), ("y", "z", "c"), 0, 0, tiled=True)
    shrink = lax.all_to_all(add_and_spread(parts), ("z", "c"), 0, 0, tiled=True)
    return expand(shrink, code, base, adapter_up, tables)


def solution(mesh):
    grid = Mesh(mesh.devices.reshape(Y, X, Z, C), ("y", "x", "z", "c"))
    replica, tensor = ("y", "x"), ("z", "c")
    placed = (
        P(replica, tensor),
        P(replica),
        P(),
        P(tensor, None),
        P(replica, None, tensor),
        P(replica, None, tensor),
    )
    return jax.shard_map(
        shards, mesh=grid, in_specs=placed, out_specs=P(replica, tensor), check_vma=False
    )
```

```python
import functools

import jax
import jax.numpy as jnp
from jax import lax
from jax.experimental import pallas as pl
from jax.experimental.pallas import tpu as pltpu
from jax.sharding import Mesh, PartitionSpec as P

Y, X, Z, C = 8, 4, 8, 2
T = Z * C
GROUPS = Y * X
LIMIT = 2
CODE_ROWS = 16
MIB = 1024 * 1024
NT = (((1,), (1,)), ((), ()))


def spot():
    return lax.axis_index("y"), lax.axis_index("x")


def dispatch_kernel(plan, down, *refs):
    out, picked_out, held, staged, picked, in_sems, out_sems, picked_sem = refs
    resident = down.shape[0]
    y, x = spot()
    pieces = in_sems.shape[0]
    part = resident // pieces

    def read(i):
        rows = pl.ds(i * part, part)
        return pltpu.make_async_copy(down.at[rows], held.at[rows], in_sems.at[i])

    def write(e):
        return pltpu.make_async_copy(staged.at[e], out.at[e], out_sems.at[e])

    for i in range(pieces):
        read(i).start()
    table = plan[...]
    home = table // resident
    number = table - home * resident
    mine = (home == y * X + x).astype(jnp.int32)
    after = jnp.concatenate([jnp.zeros((mine.shape[0], 1), jnp.int32), mine[:, :-1]], axis=1)
    first = jnp.sum(mine * (1 - after) * number, axis=1, keepdims=True)
    second = jnp.sum(mine * after * number, axis=1, keepdims=True)
    lane = lax.broadcasted_iota(jnp.int32, picked_out.shape, 1)
    picked_out[...] = jnp.where(lane == 0, first, jnp.where(lane == 1, second, 0))
    to_scalars = pltpu.make_async_copy(picked_out, picked, picked_sem)
    to_scalars.start()
    to_scalars.wait()
    for i in range(pieces):
        read(i).wait()
    for e in range(X):
        for row in range(Y):
            for j in range(LIMIT):
                staged[e, row * LIMIT + j] = held[picked[row * X + e, j]]
        write(e).start()
    for e in range(X):
        write(e).wait()


def dispatch(plan, down):
    vmem = pl.BlockSpec(memory_space=pltpu.VMEM)
    hbm = pl.BlockSpec(memory_space=pl.ANY)
    shape = (X, Y * LIMIT) + down.shape[1:]
    return pl.pallas_call(
        dispatch_kernel,
        out_shape=(
            jax.ShapeDtypeStruct(shape, down.dtype),
            jax.ShapeDtypeStruct((GROUPS, 128), jnp.int32),
        ),
        in_specs=[vmem, hbm],
        out_specs=(hbm, vmem),
        scratch_shapes=[
            pltpu.VMEM(down.shape, down.dtype),
            pltpu.VMEM(shape, down.dtype),
            pltpu.SMEM((GROUPS, 128), jnp.int32),
            pltpu.SemaphoreType.DMA((4,)),
            pltpu.SemaphoreType.DMA((X,)),
            pltpu.SemaphoreType.DMA,
        ],
        cost_estimate=pl.CostEstimate(flops=0, bytes_accessed=6 * down.size, transcendentals=0),
    )(plan, down)


def prepare_kernel(resident, plan, slots, rows, out, code_out):
    y, x = spot()
    height, width = rows.shape
    slot = slots[...]
    code = slot
    before = jnp.int32(-1)
    for k in range(plan.shape[1]):
        home = plan[y * X + x, k] // resident
        again = (home == before).astype(jnp.int32)
        code = jnp.where(slot == resident + k, resident + home * LIMIT + again, code)
        before = home
    code_out[...] = code
    out[0:height, :] = rows[...]
    wide = jnp.concatenate([code.astype(jnp.float32), jnp.zeros((1, width - height), jnp.float32)], axis=1)
    out[height:, :] = jnp.broadcast_to(wide, (CODE_ROWS, width)).astype(out.dtype)


def prepare(resident, plan, slots, rows):
    height, width = rows.shape
    smem = pl.BlockSpec(memory_space=pltpu.SMEM)
    vmem = pl.BlockSpec(memory_space=pltpu.VMEM)
    return pl.pallas_call(
        functools.partial(prepare_kernel, resident),
        out_shape=(
            jax.ShapeDtypeStruct((height + CODE_ROWS, width), rows.dtype),
            jax.ShapeDtypeStruct(slots.shape, jnp.int32),
        ),
        in_specs=[smem, vmem, vmem],
        out_specs=(vmem, vmem),
        cost_estimate=pl.CostEstimate(flops=0, bytes_accessed=4 * rows.size, transcendentals=0),
    )(plan, slots, rows)


def pick_up_kernel(picked, up, *outs):
    y, _ = spot()
    for d in range(Y):
        row = lax.rem(y + d, Y)
        for x in range(X):
            for j in range(LIMIT):
                outs[d][x * LIMIT + j] = up[picked[row * X + x, j]]


def pick_up(picked, up):
    smem = pl.BlockSpec(memory_space=pltpu.SMEM)
    vmem = pl.BlockSpec(memory_space=pltpu.VMEM)
    return pl.pallas_call(
        pick_up_kernel,
        out_shape=(jax.ShapeDtypeStruct((X * LIMIT,) + up.shape[1:], up.dtype),) * Y,
        in_specs=[smem, vmem],
        out_specs=(vmem,) * Y,
        cost_estimate=pl.CostEstimate(flops=0, bytes_accessed=6 * up.size, transcendentals=0),
    )(picked, up)


def turn_kernel(*refs):
    arrived, outs = refs[:Y], refs[Y:]
    _, x = spot()
    for e in range(X):
        column = lax.rem(x + e, X)
        for d in range(Y):
            for j in range(LIMIT):
                outs[e][d * LIMIT + j] = arrived[d][column * LIMIT + j]


def turn(arrived):
    vmem = pl.BlockSpec(memory_space=pltpu.VMEM)
    shape = jax.ShapeDtypeStruct((Y * LIMIT,) + arrived[0].shape[1:], arrived[0].dtype)
    return pl.pallas_call(
        turn_kernel,
        out_shape=(shape,) * X,
        in_specs=[vmem] * Y,
        out_specs=(vmem,) * X,
        compiler_params=pltpu.CompilerParams(vmem_limit_bytes=6 * MIB),
        cost_estimate=pl.CostEstimate(flops=0, bytes_accessed=4 * Y * arrived[0].size, transcendentals=0),
    )(*arrived)


def local_kernel(code, rows, down, out):
    rank = out.shape[0]
    resident = down.shape[0] // rank
    total = jnp.zeros(out.shape, jnp.float32)
    step = 4
    for first in range(0, resident, step):
        product = lax.dot_general(
            down[first * rank : (first + step) * rank, :], rows[...], NT, preferred_element_type=jnp.float32
        )
        for k in range(step):
            total = total + jnp.where(code[...] == first + k, product[k * rank : (k + 1) * rank, :], 0.0)
    out[...] = total


def local_shrink(code, rows, down):
    resident, rank, width = down.shape
    vmem = pl.BlockSpec(memory_space=pltpu.VMEM)
    return pl.pallas_call(
        local_kernel,
        out_shape=jax.ShapeDtypeStruct((rank, rows.shape[0]), jnp.float32),
        in_specs=[vmem] * 3,
        out_specs=vmem,
        cost_estimate=pl.CostEstimate(
            flops=2 * rows.size * resident * rank, bytes_accessed=2 * down.size, transcendentals=0
        ),
    )(code, rows, down.reshape(resident * rank, width))


def imported_kernel(resident, rows, down, own, out, rows_held, down_held, sems):
    rank, count = own.shape
    lanes = out.shape[-1]
    y, _ = spot()
    odd = lax.axis_index("c")

    def reads(g):
        wanted = pl.ds(g * LIMIT * rank, LIMIT * rank)
        at = g + odd * (Y - 1 - 2 * g)
        pairs = [(rows.at[at], rows_held.at[g])]
        pairs += [(down.at[x, wanted], down_held.at[g, pl.ds(x * LIMIT * rank, LIMIT * rank)]) for x in range(X)]
        return [pltpu.make_async_copy(a, b, sems.at[g, i]) for i, (a, b) in enumerate(pairs)]

    for g in range(Y):
        for read in reads(g):
            read.start()
    base = (resident + y * X * LIMIT).astype(jnp.float32)
    for g in range(Y):
        for read in reads(g):
            read.wait()
        code = rows_held[g, count : count + 1, :count].astype(jnp.float32)
        total = jnp.where(y == g, own[...], 0.0)
        product = lax.dot_general(
            down_held[g], rows_held[g, 0:count, :], NT, preferred_element_type=jnp.float32
        )
        for k in range(X * LIMIT):
            total = total + jnp.where(code == base + k, product[k * rank : (k + 1) * rank, :], 0.0)
        for i in range(rank // 8):
            for k in range(count // lanes):
                out[g, i * (count // lanes) + k] = total[i * 8 : (i + 1) * 8, k * lanes : (k + 1) * lanes]


def imported_shrink(resident, rows, down, own):
    rank, count = own.shape
    height, width = rows.shape[1:]
    blocks = rank * count // 1024
    vmem = pl.BlockSpec(memory_space=pltpu.VMEM)
    hbm = pl.BlockSpec(memory_space=pl.ANY)
    return pl.pallas_call(
        functools.partial(imported_kernel, resident),
        out_shape=jax.ShapeDtypeStruct((Y, blocks, 8, 128), jnp.float32),
        in_specs=[hbm, hbm, vmem],
        out_specs=vmem,
        scratch_shapes=[
            pltpu.VMEM((Y, height, width), rows.dtype),
            pltpu.VMEM((Y, X * LIMIT * rank, width), rows.dtype),
            pltpu.SemaphoreType.DMA((Y, X + 1)),
        ],
        cost_estimate=pl.CostEstimate(
            flops=2 * down.size * count, bytes_accessed=2 * (down.size + rows.size), transcendentals=0
        ),
    )(rows, down.reshape(X, -1, width), own)


def add_kernel(parts, out):
    total = jnp.sum(parts[...], axis=0)
    for t in range(out.shape[0]):
        out[t] = total


def add_and_spread(parts):
    vmem = pl.BlockSpec(memory_space=pltpu.VMEM)
    return pl.pallas_call(
        add_kernel,
        out_shape=jax.ShapeDtypeStruct((T,) + parts.shape[1:], jnp.float32),
        in_specs=[vmem],
        out_specs=vmem,
        compiler_params=pltpu.CompilerParams(vmem_limit_bytes=2 * MIB),
    )(parts)


def expand_kernel(shrink, code, base, up, *refs):
    tables, (out, held, base_held, sems) = refs[:X], refs[X:]
    count = out.shape[0]
    lanes = count // 128
    rank = shrink.shape[0] // lanes * 8
    resident, imported_each = up.shape[0], tables[0].shape[0]
    copies = [pltpu.make_async_copy(up, held.at[pl.ds(0, resident)], sems.at[0])]
    for e in range(X):
        place = pl.ds(resident + e * imported_each, imported_each)
        copies.append(pltpu.make_async_copy(tables[e], held.at[place], sems.at[1 + e]))
    copies.append(pltpu.make_async_copy(base, base_held, sems.at[1 + X]))
    for copy in copies:
        copy.start()
    rows = jnp.concatenate(
        [jnp.concatenate([shrink[i * lanes + k] for k in range(lanes)], axis=1) for i in range(rank // 8)], axis=0
    )
    rows = jnp.transpose(rows)
    y, x = spot()
    imported = code[...] - resident
    home = imported // LIMIT
    e = (x - home % X + X) % X
    d = (y - home // X + Y) % Y
    at = jnp.where(imported < 0, code[...], resident + (e * Y + d) * LIMIT + imported % LIMIT)
    column = jnp.transpose(jnp.broadcast_to(at, (8, count)).astype(jnp.float32))[:, :1]
    pair = jnp.concatenate([rows, rows], axis=1)
    high = pair.astype(jnp.bfloat16)
    low = (pair - high.astype(jnp.float32)).astype(jnp.bfloat16)
    half = lax.broadcasted_iota(jnp.int32, pair.shape, 1) // rank
    wanted = (jnp.broadcast_to(column, pair.shape) - half.astype(jnp.float32)).astype(jnp.bfloat16)
    nothing = jnp.zeros(pair.shape, jnp.bfloat16)
    total = jnp.zeros((2 * count, out.shape[1]), jnp.float32)
    step = 8
    bounds = [resident + e * imported_each for e in range(X + 1)]
    for first in range(0, held.shape[0] // 2, step):
        if first == 0:
            copies[0].wait()
        if 2 * first in bounds:
            copies[1 + bounds.index(2 * first)].wait()
        hits = [wanted == jnp.bfloat16(2 * p) for p in range(first, first + step)]
        placed = jnp.concatenate(
            [
                jnp.concatenate([jnp.where(hit, part, nothing) for hit in hits], axis=1)
                for part in (high, low)
            ],
            axis=0,
        )
        maps = held[2 * first : 2 * (first + step)].reshape(2 * step * rank, out.shape[1])
        total = total + jnp.dot(placed, maps, preferred_element_type=jnp.float32)
    copies[-1].wait()
    out[...] = (base_held[...] + (total[:count] + total[count:])).astype(out.dtype)


def expand(shrink, code, base, up, tables):
    vmem = pl.BlockSpec(memory_space=pltpu.VMEM)
    hbm = pl.BlockSpec(memory_space=pltpu.HBM)
    maps = up.shape[0] + X * tables[0].shape[0]
    return pl.pallas_call(
        expand_kernel,
        out_shape=jax.ShapeDtypeStruct(base.shape, jnp.bfloat16),
        in_specs=[vmem, vmem] + [hbm] * (2 + X),
        out_specs=vmem,
        scratch_shapes=[
            pltpu.VMEM((maps,) + up.shape[1:], up.dtype),
            pltpu.VMEM(base.shape, base.dtype),
            pltpu.SemaphoreType.DMA((2 + X,)),
        ],
    )(shrink, code, base, up, *tables)


def shift(array, axis, size, by):
    return lax.ppermute(array, axis, [(i, (i + by) % size) for i in range(size)])


def shards(inputs, row_adapter_slot, transfer_plan, key_value_weight, adapter_down, adapter_up):
    count = inputs.shape[0]
    resident = adapter_down.shape[0]
    slots = row_adapter_slot.reshape(1, count)

    sent, code = prepare(resident, transfer_plan, slots, inputs)
    rings = [[i * C for i in range(Y)], [i * C + 1 for i in reversed(range(Y))]]
    rows = lax.all_gather(sent, ("y", "c"), axis_index_groups=rings)
    down, picked = dispatch(transfer_plan, adapter_down)
    down = lax.all_to_all(down, "x", 0, 0, tiled=True)

    late, picked = lax.optimization_barrier((inputs, picked))
    base_part = jnp.dot(late, key_value_weight, preferred_element_type=jnp.float32)
    base = lax.psum_scatter(base_part, ("z", "c"), scatter_dimension=1, tiled=True)
    own = local_shrink(code, late, adapter_down)

    ups = pick_up(picked, adapter_up)
    near, far, last = (1, 7, 2, 6), 4, (3, 5)
    moved = [shift(ups[d], "y", Y, d) for d in near]
    moved, later, own = lax.optimization_barrier((moved, ups[far], own))
    moved.append(shift(later, "y", Y, far))
    moved, later = lax.optimization_barrier((moved, [ups[d] for d in last]))
    moved_far = [shift(ups_d, "y", Y, d) for ups_d, d in zip(later, last)]
    parts = imported_shrink(resident, rows, down, own)
    parts, moved_far = lax.optimization_barrier((parts, moved_far))
    moved = dict(zip(near + (far,) + last, moved + moved_far)) | {0: ups[0]}
    ups = turn([moved[d] for d in range(Y)])
    tables = [ups[0]] + [shift(ups[e], "x", X, e) for e in range(1, X)]

    parts = lax.all_to_all(parts.reshape(Y * T, 8, 128), ("y", "z", "c"), 0, 0, tiled=True)
    shrink = lax.all_to_all(add_and_spread(parts), ("z", "c"), 0, 0, tiled=True)
    return expand(shrink, code, base, adapter_up, tables)


def solution(mesh):
    grid = Mesh(mesh.devices.reshape(Y, X, Z, C), ("y", "x", "z", "c"))
    replica, tensor = ("y", "x"), ("z", "c")
    placed = (
        P(replica, tensor),
        P(replica),
        P(),
        P(tensor, None),
        P(replica, None, tensor),
        P(replica, None, tensor),
    )
    return jax.shard_map(
        shards, mesh=grid, in_specs=placed, out_specs=P(replica, tensor), check_vma=False
    )
```
